32 devices in a mesh: patch: 8 (over z, y), visit: 4 (over x, core).
Axes of the slice: x: 2, y: 2, z: 4, core: 2. Of those that a mesh axis runs over, the one named last changes fastest.
Arguments:
- pieces: bfloat16 [3072, 32, 128], P(('patch', 'visit')), may hold values from -16 to 16
- dest: int32 [3072, 1], P(('patch', 'visit')), may hold values from 0 to 7; in each aligned block of 96 rows (0 to 95, 96 to 191, ...) at most 24 rows name the same one
- offsets: int32 [3072], P(('patch', 'visit')), may hold values from 0 to 224
- kernel_index: int32 [3072], P(('patch', 'visit')), may hold values from 0 to 39
- weights: bfloat16 [3072], P(('patch', 'visit')), may hold values from 0.25 to 4
- basis_col: bfloat16 [14, 41], replicated, may hold values from -1 to 1
- basis_row: bfloat16 [14, 41], replicated, may hold values from -1 to 1
- coef_table: float32 [40, 14], replicated, may hold values from -2.4 to 2.4
- det_taps: bfloat16 [2, 21], replicated, may hold values from -1.25 to 1.25
Outputs:
- coadd: float32 [2048, 128], P(('patch', 'visit'))
- detection: float32 [2048, 128], P(('patch', 'visit'))
The draws below stay inside these ranges and needn't reach their ends.
Inputs may be any that keep to these rules, and one draw needn't show every extreme that they name: `dest`: at most 24 of the pieces of one device intersect one patch.
All inputs are finite; a program needn't handle non-finite values.
Results may differ from the reference program's by a relative error of at most 0.0062.
Values may be sent and summed in bfloat16 or wider, within the bound.
No kernel may reach another device: no remote copies, remote signals or barrier semaphores. Data moves between devices by JAX's collectives and lax.ppermute only.
A program may use at most 64 MiB of HBM per device.

```python
import math
import jax
import jax.numpy as jnp
import numpy as np
from jax import lax

PIECES_DEV = 96
PR = 32
PW = 128
PH = 256
TAPS = 41
NB = 14
NK = 40
TD = 21
CAP = 24
PIECES = 3072
N_PATCH = 8


def touch_ends(result, stream_key, low, high):
    longest = result.shape.index(max(result.shape))
    spots = []
    for shift in (0, 1):
        where = [jax.random.randint(jax.random.fold_in(stream_key, axis), (), 0, length) for axis, length in enumerate(result.shape)]
        where[longest] = (where[longest] + shift) % result.shape[longest]
        spots.append(tuple(where))
    return result.at[spots[0]].set(low).at[spots[1]].set(high)


def levels(own_key, shape, shards, smallest, largest):
    def one(axis_at, parts):
        draws = jax.random.uniform(jax.random.fold_in(jax.random.fold_in(own_key, 6), axis_at), (parts,), jnp.float32, smallest / len(shards), largest / len(shards))
        return jnp.repeat(jnp.exp(draws), shape[axis_at] // parts).reshape((-1,) + (1,) * (len(shape) - axis_at - 1))

    loudness = one(*shards[0])
    for cut in shards[1:]:
        loudness = loudness * one(*cut)
    return loudness


def deal_out(key, own, number, rows, amount, top, bound, slope):
    sequence = jax.random.permutation(key, amount)
    crowded, ordinary = portions_of(amount, rows * top, bound, slope, True), portions_of(amount, rows * top, bound, slope, False)
    places = jnp.arange(amount)

    def named(lengths, offset_by):
        used = int((lengths > 0).sum())
        fixed = max(1, used // 4)
        moved = fixed + (places - fixed + offset_by * (used - fixed)) % max(1, amount - fixed)
        return jnp.zeros((amount,), jnp.int32).at[sequence[jnp.where(places < fixed, places, moved)]].set(jnp.asarray(lengths, jnp.int32))

    lengths = jnp.where(number % 4 == 0, named(crowded, number // 4), named(ordinary, number - number // 4 - 1))
    mixed = jax.random.permutation(jax.random.fold_in(own, 3), amount)
    donor, sink = mixed[0:amount // 2 * 2:2], mixed[1:amount // 2 * 2:2]
    room = jnp.minimum(lengths[donor] - 1, bound - lengths[sink]) // 2
    room = jnp.where((donor == sequence[0]) | (sink == sequence[0]) | (lengths[sink] == 0), 0, jnp.maximum(room, 0))
    moved = jax.random.randint(jax.random.fold_in(own, 4), (amount // 2,), 0, 1 << 20) % (room + 1)
    lengths = lengths.at[donor].add(-moved).at[sink].add(moved)
    members = jnp.searchsorted(jnp.cumsum(lengths), jnp.arange(rows * top), side="right").astype(jnp.int32)
    grid = members.reshape(top, rows).T
    grid = grid[jax.random.permutation(jax.random.fold_in(own, 1), rows)]
    offset_by = jax.random.randint(jax.random.fold_in(own, 2), (rows, 1), 0, top)
    return jnp.take_along_axis(grid, (jnp.arange(top)[None, :] + offset_by) % top, axis=1)


def portions_of(amount, total, most, slope, full):
    loads = [(1 << 20) // math.isqrt(rank ** slope) + 1 for rank in range(1, amount + 1)]
    largest = most if full else min(most, max(-(-total // amount), total * loads[0] // sum(loads)))
    least = 1 if total - largest >= amount - 1 else 0
    counts, rest = [largest] + [least] * (amount - 1), total - largest - least * (amount - 1)
    while rest > 0:
        free = [i for i in range(1, amount) if counts[i] < largest] or [i for i in range(1, amount) if counts[i] < most]
        mass, budget = sum([loads[i] for i in free]), rest
        for i in free:
            extra = min(most - counts[i], max(1, budget * loads[i] // mass), rest)
            counts[i] = counts[i] + extra
            rest = rest - extra
    return np.array(counts)


def normal_values(stream_key, extent, deviation, most, cuts=(), held_as=jnp.bfloat16):
    loudness = levels(stream_key, extent, cuts, -0.22, 0.18) if cuts else 1.0
    array = jax.random.normal(stream_key, extent, jnp.float32) * deviation * loudness
    return jnp.minimum(jnp.maximum(array, -most), most).astype(held_as)


def setup_inputs(seed: int = 0) -> dict:
    key_list = jax.random.split(jax.random.key(seed), 10)
    pieces = normal_values(key_list[0], (PIECES, PR, PW), 3.0, 16.0, ((0, 32),))
    dest_keys = jax.random.split(jax.random.fold_in(key_list[1], 1), PIECES // PIECES_DEV)
    dest_turns = jax.random.permutation(jax.random.fold_in(key_list[1], 3), PIECES // PIECES_DEV)
    dest = jax.vmap(lambda own, number: deal_out(jax.random.fold_in(key_list[1], 2), own, number, PIECES_DEV, N_PATCH, 1, CAP, 2))(dest_keys, dest_turns).reshape((PIECES, 1))
    offsets = touch_ends(jax.random.randint(key_list[2], (PIECES,), 0, PH - PR + 1), jax.random.fold_in(key_list[2], 1), 0, PH - PR).astype(jnp.int32)
    kernel_index = touch_ends(jax.random.randint(key_list[3], (PIECES,), 0, NK), jax.random.fold_in(key_list[3], 1), 0, NK - 1).astype(jnp.int32)
    weights = jnp.clip(jnp.exp(math.log(4.0) - 2.7725887 * jax.random.uniform(key_list[4], (PIECES,), jnp.float32) ** levels(key_list[4], (PIECES,), ((0, 32),), -0.2, 0.2)), 0.25, 4.0).astype(jnp.bfloat16)
    basis_col = normal_values(key_list[5], (NB, TAPS), TAPS ** -0.5, 1.0)
    basis_row = normal_values(key_list[6], (NB, TAPS), TAPS ** -0.5, 1.0)
    coef_table = normal_values(key_list[7], (NK, NB), 0.4, 2.4, (), jnp.float32)
    det_taps = normal_values(key_list[8], (2, TD), TD ** -0.5, 1.25)
    return {"pieces": pieces, "dest": dest, "offsets": offsets, "kernel_index": kernel_index, "weights": weights, "basis_col": basis_col, "basis_row": basis_row, "coef_table": coef_table, "det_taps": det_taps}


def banded(tap_table, height, columns, center):
    offsets_grid = jnp.arange(columns)[None, :] - jnp.arange(height)[:, None] + center
    one_hot = (offsets_grid[:, :, None] == jnp.arange(tap_table.shape[1])[None, None, :]).astype(jnp.float32)
    return jnp.einsum('ijt,bt->bij', one_hot, tap_table.astype(jnp.float32), precision=lax.Precision.HIGHEST).astype(jnp.bfloat16)


def reference(pieces, dest, offsets, kernel_index, weights, basis_col, basis_row, coef_table, det_taps):
    half_taps = TAPS // 2
    col_bands = banded(basis_col, PW, PW, half_taps).astype(jnp.float32)
    row_bands = banded(basis_row, PR, PR, half_taps).astype(jnp.float32)
    number = pieces.shape[0]
    block_size = math.gcd(number, 64)
    steps_total = number // block_size
    operands = (pieces.reshape(steps_total, block_size, PR, PW), dest[:, 0].reshape(steps_total, block_size),
                offsets.reshape(steps_total, block_size), kernel_index.reshape(steps_total, block_size),
                weights.reshape(steps_total, block_size))

    def accumulate(carry, blocks):
        numerator, denominator = carry
        images, targets, starts, kinds, scales = blocks
        factors = coef_table[kinds]
        stacked = jnp.einsum('nrk,bkc->nbrc', images.astype(jnp.float32), col_bands, precision=lax.Precision.HIGHEST)
        stacked = lax.optimization_barrier(stacked.astype(jnp.bfloat16)).astype(jnp.float32)
        stacked = stacked.reshape(block_size, NB * PR, PW)
        row_kernel = (factors[:, None, :, None] * row_bands.transpose(1, 0, 2)[None]).reshape(block_size, PR, NB * PR)
        row_kernel = lax.optimization_barrier(row_kernel.astype(jnp.bfloat16)).astype(jnp.float32)
        matched = jnp.einsum('nrq,nqc->nrc', row_kernel, stacked, precision=lax.Precision.HIGHEST)
        matched = lax.optimization_barrier(matched.astype(jnp.bfloat16)).astype(jnp.float32)
        scale_float = scales.astype(jnp.float32)
        terms = (scale_float[:, None, None] * matched).reshape(block_size * PR, PW)
        row_index = (targets[:, None] * PH + starts[:, None] + jnp.arange(PR)[None, :]).reshape(-1).astype(jnp.int32)
        numerator = numerator.at[row_index].add(terms)
        denominator = denominator.at[row_index].add(jnp.repeat(scale_float, PR))
        return (numerator, denominator), None

    start_carry = (jnp.zeros((N_PATCH * PH, PW), jnp.float32), jnp.zeros((N_PATCH * PH,), jnp.float32))
    (numerator, denominator), _ = lax.scan(accumulate, start_carry, operands)
    coadd = numerator / (1.0 + denominator)[:, None]
    det_half = TD // 2
    det_cols = banded(det_taps[1:2], PW, PW, det_half)[0]
    det_rows = banded(det_taps[0:1], PH, PH, det_half)[0].astype(jnp.float32)
    coadd_low = coadd.astype(jnp.bfloat16)
    smoothed = jnp.dot(coadd_low, det_cols, preferred_element_type=jnp.float32).astype(jnp.bfloat16)
    smoothed = smoothed.astype(jnp.float32).reshape(N_PATCH, PH, PW)
    detection = jnp.einsum('rs,psc->prc', det_rows, smoothed, precision=lax.Precision.HIGHEST).reshape(N_PATCH * PH, PW)
    return coadd, detection
```

```python
from functools import partial
import math

import jax
import jax.numpy as jnp
from jax import lax
from jax.experimental import pallas as pl
from jax.experimental.pallas import tpu as pltpu
from jax.sharding import PartitionSpec as P

PH = 256
F32 = jnp.float32
BF16 = jnp.bfloat16


def iota(shape, dim):
    return lax.broadcasted_iota(jnp.int32, shape, dim)


def dot(a, b):
    return jnp.dot(a, b, preferred_element_type=F32)


def dot_nt(a, b):
    return lax.dot_general(a, b, (((1,), (1,)), ((), ())), preferred_element_type=F32)


def dot_tn(a, b):
    return lax.dot_general(a, b, (((0,), (0,)), ((), ())), preferred_element_type=F32)


def toeplitz(taps, rows, lanes, shift):
    first = pltpu.roll(jnp.broadcast_to(taps, (8, lanes)), 0, 1, stride=1, stride_axis=0)
    blocks = [pltpu.roll(first, (i + shift) % lanes, 1) for i in range(0, rows, 8)]
    return jnp.concatenate(blocks, axis=0)


def coadd_kernel(
    geometry,
    dest_s, off_s, pieces, dest_v, off_v, kind_v, weight_v, col, row, coef,
    out,
    bands, row_cat, factors, acc, den,
):
    patches, strips, halo, stride, chunk = geometry
    count, height, width = pieces.shape
    basis, taps = col.shape
    half = taps // 2
    strip = PH // strips
    span = out.shape[1]
    diff = iota((width, width), 1) - iota((width, width), 0)
    inside = jnp.abs(diff) <= half
    pad = jnp.zeros((basis, width - taps), F32)
    col_taps = jnp.concatenate([col[...].astype(F32), pad], axis=1)
    row_taps = jnp.concatenate([row[...].astype(F32), pad], axis=1)
    for b in range(basis):
        g = toeplitz(col_taps[b:b + 1], width, width, -half)
        bands[:, b * width:(b + 1) * width] = jnp.where(inside, g, 0.0).astype(BF16)
    per = width // height
    lane = iota((height, width), 1)
    sub = iota((height, width), 0)
    for first in range(0, basis, per):
        tile = jnp.zeros((height, width), F32)
        for b in range(first, min(basis, first + per)):
            at = (b - first) * height
            s = lane - at
            good = (s >= 0) & (s < height) & (jnp.abs(s - sub) <= half)
            tile = jnp.where(good, toeplitz(row_taps[b:b + 1], height, width, at - half), tile)
        row_cat[:, first * height:first * height + width] = tile
    kinds = coef.shape[0]
    full = row_cat.shape[1]
    spread = (iota((basis, full), 1) // height == iota((basis, full), 0)).astype(BF16)
    table = coef[...]
    high = table.astype(BF16)
    low = (table - high.astype(F32)).astype(BF16)
    weight = weight_v[...].astype(F32)
    picked = jnp.where(iota((kinds, count), 0) == kind_v[...], weight, 0.0).astype(BF16)
    factors[...] = dot_tn(picked, dot(high, spread).astype(BF16)) + dot_tn(
        picked, dot(low, spread).astype(BF16)
    )
    share = jnp.where(iota((patches, count), 0) == dest_v[...], weight, 0.0).astype(BF16)
    for v in range(strips):
        at = iota((width, count), 0) + (v * strip - halo) - off_v[...]
        covered = ((at >= 0) & (at < height)).astype(BF16)
        den[v] = dot_nt(share, covered)
    acc[...] = jnp.zeros_like(acc)

    def step(i, carry):
        images = pieces[pl.ds(i * chunk, chunk)].reshape(chunk * height, width)
        stacked = dot(images, bands[...]).astype(BF16)
        for j in range(chunk):
            n = i * chunk + j
            kernel = (row_cat[...] * factors[pl.ds(n, 1), :])[:, :basis * height].astype(BF16)
            piece = jnp.concatenate(
                [
                    stacked[j * height:(j + 1) * height, b * width:(b + 1) * width]
                    for b in range(basis)
                ],
                axis=0,
            )
            matched = dot(kernel, piece)
            place = pl.ds(dest_s[n] * stride + halo + off_s[n], height)
            acc[place, :] = acc[place, :] + matched
        return carry

    lax.fori_loop(0, count // chunk, step, 0)

    def finish(p, carry):
        for v in range(strips):
            base = pl.multiple_of(p * stride + v * strip, 16)
            body = acc[pl.ds(base, span - 8), :]
            tail = jnp.broadcast_to(den[v, pl.ds(p, 1), :], (8, width))
            out[p * strips + v] = jnp.concatenate([body, tail], axis=0).astype(BF16)
        return carry

    lax.fori_loop(0, patches, finish, 0)


def detect_kernel(halo, received, taps_ref, coadd, detection):
    span, width = received.shape[1:]
    strip = coadd.shape[0]
    taps = taps_ref.shape[1]
    total = jnp.sum(received[...].astype(F32), axis=0)
    rows = iota((span, width), 0)
    square = jnp.broadcast_to(total[span - 8:span - 7, :], (width, width))
    weight = jnp.transpose(square)[:span]
    value = jnp.where(rows < strip + 2 * halo, total / (1.0 + weight), 0.0)
    coadd[...] = value[halo:halo + strip]
    table = jnp.concatenate(
        [taps_ref[...].astype(F32), jnp.zeros((2, width - taps), F32)], axis=1
    )
    diff = iota((width, width), 1) - iota((width, width), 0)
    columns = jnp.where(
        jnp.abs(diff) <= halo, toeplitz(table[1:2], width, width, -halo), 0.0
    ).astype(BF16)
    smooth = dot(value.astype(BF16), columns).astype(BF16)
    diff = iota((strip, width), 1) - iota((strip, width), 0)
    filt = jnp.where((diff >= 0) & (diff < taps), toeplitz(table[0:1], strip, width, 0), 0.0)
    smooth = jnp.concatenate([smooth, jnp.zeros((width - span, width), BF16)], axis=0)
    detection[...] = dot(filt.astype(BF16), smooth)


def shards(
    pieces, dest, offsets, kernel_index, weights, basis_col, basis_row, coef_table, det_taps
):
    patches = lax.axis_size("patch")
    strips = lax.axis_size("visit")
    count, height, width = pieces.shape
    basis = basis_col.shape[0]
    halo = det_taps.shape[1] // 2
    strip = PH // strips
    span = -(-(strip + 2 * halo) // 8) * 8 + 8
    span = -(-span // 16) * 16
    stride = strip * (strips - 1) + span
    chunk = math.gcd(count, 8)
    full = -(-(basis * height) // width) * width
    smem = pl.BlockSpec(memory_space=pltpu.SMEM)
    vmem = pl.BlockSpec(memory_space=pltpu.VMEM)
    partial_sums = pl.pallas_call(
        partial(coadd_kernel, (patches, strips, halo, stride, chunk)),
        out_shape=jax.ShapeDtypeStruct((patches * strips, span, width), BF16),
        in_specs=[smem] * 2 + [vmem] * 8,
        out_specs=vmem,
        scratch_shapes=[
            pltpu.VMEM((width, basis * width), BF16),
            pltpu.VMEM((height, full), F32),
            pltpu.VMEM((count, full), F32),
            pltpu.VMEM((patches * stride, width), F32),
            pltpu.VMEM((strips, patches, width), F32),
        ],
        compiler_params=pltpu.CompilerParams(vmem_limit_bytes=48 * 1024 * 1024),
        name="coadd_partials",
    )(
        dest[:, 0], offsets, pieces,
        dest.reshape(1, count), offsets.reshape(1, count), kernel_index.reshape(1, count),
        weights.reshape(1, count), basis_col, basis_row, coef_table,
    )
    received = lax.all_to_all(
        partial_sums, ("patch", "visit"), split_axis=0, concat_axis=0, tiled=True
    )
    shape = jax.ShapeDtypeStruct((strip, width), F32)
    return pl.pallas_call(
        partial(detect_kernel, halo),
        out_shape=(shape, shape),
        in_specs=[vmem, vmem],
        out_specs=(vmem, vmem),
        compiler_params=pltpu.CompilerParams(vmem_limit_bytes=48 * 1024 * 1024),
        name="detect_strip",
    )(received, det_taps)


def solution(mesh):
    in_specs = (
        P(("patch", "visit"), None, None),
        P(("patch", "visit"), None),
        P(("patch", "visit")),
        P(("patch", "visit")),
        P(("patch", "visit")),
        P(),
        P(),
        P(),
        P(),
    )
    out_specs = (P(("patch", "visit"), None), P(("patch", "visit"), None))
    return jax.shard_map(shards, mesh=mesh, in_specs=in_specs, out_specs=out_specs, check_vma=False)
```

```python
from functools import partial
import math

import jax
import jax.numpy as jnp
from jax import lax
from jax.experimental import pallas as pl
from jax.experimental.pallas import tpu as pltpu
from jax.sharding import PartitionSpec as P

PH = 256
F32 = jnp.float32
BF16 = jnp.bfloat16


def iota(shape, dim):
    return lax.broadcasted_iota(jnp.int32, shape, dim)


def dot(a, b):
    return jnp.dot(a, b, preferred_element_type=F32)


def dot_nt(a, b):
    return lax.dot_general(a, b, (((1,), (1,)), ((), ())), preferred_element_type=F32)


def dot_tn(a, b):
    return lax.dot_general(a, b, (((0,), (0,)), ((), ())), preferred_element_type=F32)


def toeplitz(taps, rows, lanes, shift):
    first = pltpu.roll(jnp.broadcast_to(taps, (8, lanes)), 0, 1, stride=1, stride_axis=0)
    blocks = [pltpu.roll(first, (i + shift) % lanes, 1) for i in range(0, rows, 8)]
    return jnp.concatenate(blocks, axis=0)


def masked_bands(table, rows, lanes, shift, mask):
    padded = jnp.concatenate(
        [table, jnp.zeros((table.shape[0], lanes - table.shape[1]), F32)], axis=1
    )
    for b in range(table.shape[0]):
        yield b, jnp.where(mask, toeplitz(padded[b:b + 1], rows, lanes, shift), 0.0)


def split(x):
    high = x.astype(BF16)
    return high, (x - high.astype(F32)).astype(BF16)


def coadd_kernel(
    geometry,
    dest_h, off_h, pieces_h, dest_v, off_v, kind_v, weight_v, col, row, coef,
    out,
    pieces, dest_s, off_s, col_bands, row_bands, factors, scaled, acc, den, sems,
):
    patches, strips, halo, stride, group = geometry
    count, height, width = pieces.shape
    basis, taps = col.shape
    half = taps // 2
    strip = PH // strips
    span = out.shape[1]
    copies = [
        pltpu.make_async_copy(pieces_h, pieces, sems.at[0]),
        pltpu.make_async_copy(dest_h, dest_s, sems.at[1]),
        pltpu.make_async_copy(off_h, off_s, sems.at[2]),
    ]
    for copy in copies:
        copy.start()
    x, y = iota((width, width), 1), iota((width, width), 0)
    near = jnp.abs(x - y) <= half
    for b, band in masked_bands(col[...].astype(F32), width, width, -half, near):
        col_bands[b * width:(b + 1) * width, :] = band.astype(BF16)
    near = near & (x // height == y // height)
    for b, band in masked_bands(row[...].astype(F32), width, width, -half, near):
        row_bands[b * width:(b + 1) * width, :] = band.astype(BF16)
    kinds = coef.shape[1]
    weight = weight_v[...].astype(F32)
    picked = jnp.where(iota((kinds, count), 0) == kind_v[...], weight, 0.0).astype(BF16)
    high, low = split(coef[...])
    high, low = split(dot(high, picked) + dot(low, picked))
    spread = (
        iota((basis, basis * width), 1) // width == iota((basis, basis * width), 0)
    ).astype(BF16)
    factors[...] = dot_tn(high, spread) + dot_tn(low, spread)
    share = jnp.where(iota((patches, count), 0) == dest_v[...], weight, 0.0).astype(BF16)
    for v in range(strips):
        at = iota((width, count), 0) + (v * strip - halo) - off_v[...]
        covered = ((at >= 0) & (at < height)).astype(BF16)
        den[v] = dot_nt(share, covered)
    acc[...] = jnp.zeros_like(acc)
    for copy in copies:
        copy.wait()

    def step(i, carry):
        base = pl.multiple_of(i * 2 * group, 2 * group)
        images = jnp.concatenate(
            [
                pieces[pl.ds(base + g * group, group)].reshape(width, width)
                for g in range(2)
            ],
            axis=1,
        )
        for b in range(basis):
            at = slice(b * width, (b + 1) * width)
            rowed = dot(row_bands[at, :], images)
            scale = factors[pl.ds(base, 2 * group), at]
            for g in range(2):
                for j in range(group):
                    part = rowed[j * height:(j + 1) * height, g * width:(g + 1) * width]
                    part = part * scale[g * group + j:g * group + j + 1]
                    first = g * width + j * height
                    scaled[first:first + height, at] = part.astype(BF16)
        matched = dot(scaled[...], col_bands[...])
        for j in range(2 * group):
            place = pl.ds(dest_s[base + j] * stride + halo + off_s[base + j], height)
            acc[place, :] = acc[place, :] + matched[j * height:(j + 1) * height]
        return carry

    lax.fori_loop(0, count // (2 * group), step, 0)
    own = iota((span, width), 0) < strip + 2 * halo

    def finish(p, carry):
        for v in range(strips):
            base = pl.multiple_of(p * stride + v * strip, 8)
            total = jnp.where(own, acc[pl.ds(base, span), :], den[v, pl.ds(p, 1), :])
            out[p * strips + v] = total.astype(BF16)
        return carry

    lax.fori_loop(0, patches, finish, 0)


def detect_kernel(halo, received, taps_ref, coadd, detection):
    span, width = received.shape[1:]
    strip = coadd.shape[0]
    taps = taps_ref.shape[1]
    total = jnp.sum(received[...].astype(F32), axis=0)
    rows = iota((span, width), 0)
    square = jnp.broadcast_to(total[strip + 2 * halo:strip + 2 * halo + 1], (width, width))
    weight = jnp.transpose(square)[:span]
    value = jnp.where(rows < strip + 2 * halo, total / (1.0 + weight), 0.0)
    coadd[...] = value[halo:halo + strip]
    table = taps_ref[...].astype(F32)
    diff = iota((width, width), 1) - iota((width, width), 0)
    ((_, columns),) = masked_bands(table[1:2], width, width, -halo, jnp.abs(diff) <= halo)
    diff = iota((strip, width), 1) - iota((strip, width), 0)
    ((_, filt),) = masked_bands(table[0:1], strip, width, 0, (diff >= 0) & (diff < taps))
    columns, filt = columns.astype(BF16), filt.astype(BF16)
    high, low = split(value)
    smooth = dot(high, columns) + dot(low, columns)
    smooth = jnp.concatenate([smooth, jnp.zeros((width - span, width), F32)], axis=0)
    high, low = split(smooth)
    detection[...] = dot(filt, high) + dot(filt, low)


def shards(
    pieces, dest, offsets, kernel_index, weights, basis_col, basis_row, coef_table, det_taps
):
    patches = lax.axis_size("patch")
    strips = lax.axis_size("visit")
    count, height, width = pieces.shape
    basis = basis_col.shape[0]
    halo = det_taps.shape[1] // 2
    strip = PH // strips
    span = -(-(strip + 2 * halo + 1) // 8) * 8
    stride = strip * (strips - 1) + span
    group = width // height
    hbm = pl.BlockSpec(memory_space=pltpu.HBM)
    vmem = pl.BlockSpec(memory_space=pltpu.VMEM)
    partial_sums = pl.pallas_call(
        partial(coadd_kernel, (patches, strips, halo, stride, group)),
        out_shape=jax.ShapeDtypeStruct((patches * strips, span, width), BF16),
        in_specs=[hbm] * 3 + [vmem] * 7,
        out_specs=vmem,
        scratch_shapes=[
            pltpu.VMEM((count, height, width), BF16),
            pltpu.SMEM((count,), jnp.int32),
            pltpu.SMEM((count,), jnp.int32),
            pltpu.VMEM((basis * width, width), BF16),
            pltpu.VMEM((basis * width, width), BF16),
            pltpu.VMEM((count, basis * width), F32),
            pltpu.VMEM((2 * width, basis * width), BF16),
            pltpu.VMEM((patches * stride, width), F32),
            pltpu.VMEM((strips, patches, width), F32),
            pltpu.SemaphoreType.DMA((3,)),
        ],
        compiler_params=pltpu.CompilerParams(vmem_limit_bytes=48 * 1024 * 1024),
        name="coadd_partials",
    )(
        dest[:, 0], offsets, pieces,
        dest.reshape(1, count), offsets.reshape(1, count), kernel_index.reshape(1, count),
        weights.reshape(1, count), basis_col, basis_row, coef_table.T,
    )
    received = lax.all_to_all(
        partial_sums, ("patch", "visit"), split_axis=0, concat_axis=0, tiled=True
    )
    shape = jax.ShapeDtypeStruct((strip, width), F32)
    return pl.pallas_call(
        partial(detect_kernel, halo),
        out_shape=(shape, shape),
        in_specs=[vmem, vmem],
        out_specs=(vmem, vmem),
        compiler_params=pltpu.CompilerParams(vmem_limit_bytes=48 * 1024 * 1024),
        name="detect_strip",
    )(received, det_taps)


def solution(mesh):
    in_specs = (
        P(("patch", "visit"), None, None),
        P(("patch", "visit"), None),
        P(("patch", "visit")),
        P(("patch", "visit")),
        P(("patch", "visit")),
        P(),
        P(),
        P(),
        P(),
    )
    out_specs = (P(("patch", "visit"), None), P(("patch", "visit"), None))
    return jax.shard_map(shards, mesh=mesh, in_specs=in_specs, out_specs=out_specs, check_vma=False)
```

```python
from functools import partial
import math

import jax
import jax.numpy as jnp
from jax import lax
from jax.experimental import pallas as pl
from jax.experimental.pallas import tpu as pltpu
from jax.sharding import PartitionSpec as P

PH = 256
F32 = jnp.float32
BF16 = jnp.bfloat16


def iota(shape, dim):
    return lax.broadcasted_iota(jnp.int32, shape, dim)


def dot(a, b):
    return jnp.dot(a, b, preferred_element_type=F32)


def dot_nt(a, b):
    return lax.dot_general(a, b, (((1,), (1,)), ((), ())), preferred_element_type=F32)


def dot_tn(a, b):
    return lax.dot_general(a, b, (((0,), (0,)), ((), ())), preferred_element_type=F32)


def toeplitz(taps, rows, lanes, shift):
    first = pltpu.roll(jnp.broadcast_to(taps, (8, lanes)), 0, 1, stride=1, stride_axis=0)
    blocks = [pltpu.roll(first, (i + shift) % lanes, 1) for i in range(0, rows, 8)]
    return jnp.concatenate(blocks, axis=0)


def masked_bands(table, rows, lanes, shift, mask):
    padded = jnp.concatenate(
        [table, jnp.zeros((table.shape[0], lanes - table.shape[1]), F32)], axis=1
    )
    for b in range(table.shape[0]):
        yield b, jnp.where(mask, toeplitz(padded[b:b + 1], rows, lanes, shift), 0.0)


def split(x):
    high = x.astype(BF16)
    return high, (x - high.astype(F32)).astype(BF16)


def coadd_kernel(
    geometry,
    dest_h, off_h, pieces_h, dest_v, off_v, kind_v, weight_v, col, row, coef,
    kept, sent,
    pieces, dest_s, off_s, col_bands, row_bands, factors, scaled, acc, den, sems,
):
    patches, strips, halo, stride, group = geometry
    count, height, width = pieces.shape
    basis, taps = col.shape
    half = taps // 2
    strip = PH // strips
    span = kept.shape[1]
    copies = [
        pltpu.make_async_copy(pieces_h, pieces, sems.at[0]),
        pltpu.make_async_copy(dest_h, dest_s, sems.at[1]),
        pltpu.make_async_copy(off_h, off_s, sems.at[2]),
    ]
    for copy in copies:
        copy.start()
    x, y = iota((width, width), 1), iota((width, width), 0)
    near = jnp.abs(x - y) <= half
    for b, band in masked_bands(col[...].astype(F32), width, width, -half, near):
        col_bands[b * width:(b + 1) * width, :] = band.astype(BF16)
    near = near & (x // height == y // height)
    for b, band in masked_bands(row[...].astype(F32), width, width, -half, near):
        row_bands[b * width:(b + 1) * width, :] = band.astype(BF16)
    kinds = coef.shape[1]
    weight = weight_v[...].astype(F32)
    picked = jnp.where(iota((kinds, count), 0) == kind_v[...], weight, 0.0).astype(BF16)
    high, low = split(coef[...])
    high, low = split(dot(high, picked) + dot(low, picked))
    spread = (
        iota((basis, basis * width), 1) // width == iota((basis, basis * width), 0)
    ).astype(BF16)
    factors[...] = dot_tn(high, spread) + dot_tn(low, spread)
    share = jnp.where(iota((patches, count), 0) == dest_v[...], weight, 0.0).astype(BF16)
    for v in range(strips):
        at = iota((width, count), 0) + (v * strip - halo) - off_v[...]
        covered = ((at >= 0) & (at < height)).astype(BF16)
        den[v] = dot_nt(share, covered)
    acc[...] = jnp.zeros_like(acc)
    for copy in copies:
        copy.wait()

    def step(i, carry):
        base = pl.multiple_of(i * 2 * group, 2 * group)
        images = jnp.concatenate(
            [
                pieces[pl.ds(base + g * group, group)].reshape(width, width)
                for g in range(2)
            ],
            axis=1,
        )
        for b in range(basis):
            at = slice(b * width, (b + 1) * width)
            rowed = dot(row_bands[at, :], images)
            scale = factors[pl.ds(base, 2 * group), at]
            for g in range(2):
                for j in range(group):
                    part = rowed[j * height:(j + 1) * height, g * width:(g + 1) * width]
                    part = part * scale[g * group + j:g * group + j + 1]
                    first = g * width + j * height
                    scaled[first:first + height, at] = part.astype(BF16)
        matched = dot(scaled[...], col_bands[...])
        for j in range(2 * group):
            place = pl.ds(dest_s[base + j] * stride + halo + off_s[base + j], height)
            acc[place, :] = acc[place, :] + matched[j * height:(j + 1) * height]
        return carry

    lax.fori_loop(0, count // (2 * group), step, 0)
    own = iota((span, width), 0) < strip + 2 * halo

    mine = lax.rem(lax.axis_index("visit"), 2)

    def finish(p, carry):
        for u in range(strips // 2):
            for out, v in ((kept, 2 * u + mine), (sent, 2 * u + 1 - mine)):
                base = pl.multiple_of(p * stride + v * strip, 8)
                total = jnp.where(own, acc[pl.ds(base, span), :], den[v, pl.ds(p, 1), :])
                out[p * (strips // 2) + u] = total.astype(out.dtype)
        return carry

    lax.fori_loop(0, patches, finish, 0)


def detect_kernel(halo, received, taps_ref, coadd, detection):
    span, width = received.shape[1:]
    strip = coadd.shape[0]
    taps = taps_ref.shape[1]
    total = jnp.sum(received[...].astype(F32), axis=0)
    rows = iota((span, width), 0)
    square = jnp.broadcast_to(total[strip + 2 * halo:strip + 2 * halo + 1], (width, width))
    weight = jnp.transpose(square)[:span]
    value = jnp.where(rows < strip + 2 * halo, total / (1.0 + weight), 0.0)
    coadd[...] = value[halo:halo + strip]
    table = taps_ref[...].astype(F32)
    diff = iota((width, width), 1) - iota((width, width), 0)
    ((_, columns),) = masked_bands(table[1:2], width, width, -halo, jnp.abs(diff) <= halo)
    diff = iota((strip, width), 1) - iota((strip, width), 0)
    ((_, filt),) = masked_bands(table[0:1], strip, width, 0, (diff >= 0) & (diff < taps))
    columns, filt = columns.astype(BF16), filt.astype(BF16)
    high, low = split(value)
    smooth = dot(high, columns) + dot(low, columns)
    smooth = jnp.concatenate([smooth, jnp.zeros((width - span, width), F32)], axis=0)
    high, low = split(smooth)
    detection[...] = dot(filt, high) + dot(filt, low)


def shards(
    pieces, dest, offsets, kernel_index, weights, basis_col, basis_row, coef_table, det_taps
):
    patches = lax.axis_size("patch")
    strips = lax.axis_size("visit")
    count, height, width = pieces.shape
    basis = basis_col.shape[0]
    halo = det_taps.shape[1] // 2
    strip = PH // strips
    span = -(-(strip + 2 * halo + 1) // 8) * 8
    stride = strip * (strips - 1) + span
    group = width // height
    keep = partial(pltpu.with_memory_space_constraint, memory_space=pltpu.HBM)
    hbm = pl.BlockSpec(memory_space=pltpu.HBM)
    vmem = pl.BlockSpec(memory_space=pltpu.VMEM)
    shape = (patches * strips // 2, span, width)
    kept, sent = pl.pallas_call(
        partial(coadd_kernel, (patches, strips, halo, stride, group)),
        out_shape=(jax.ShapeDtypeStruct(shape, F32), jax.ShapeDtypeStruct(shape, BF16)),
        in_specs=[hbm] * 3 + [vmem] * 7,
        out_specs=(vmem, vmem),
        scratch_shapes=[
            pltpu.VMEM((count, height, width), BF16),
            pltpu.SMEM((count,), jnp.int32),
            pltpu.SMEM((count,), jnp.int32),
            pltpu.VMEM((basis * width, width), BF16),
            pltpu.VMEM((basis * width, width), BF16),
            pltpu.VMEM((count, basis * width), F32),
            pltpu.VMEM((2 * width, basis * width), BF16),
            pltpu.VMEM((patches * stride, width), F32),
            pltpu.VMEM((strips, patches, width), F32),
            pltpu.SemaphoreType.DMA((3,)),
        ],
        compiler_params=pltpu.CompilerParams(vmem_limit_bytes=48 * 1024 * 1024),
        name="coadd_partials",
    )(
        keep(dest[:, 0]), keep(offsets), keep(pieces),
        dest.reshape(1, count), offsets.reshape(1, count), kernel_index.reshape(1, count),
        weights.reshape(1, count), basis_col, basis_row, coef_table.T,
    )
    given = lax.ppermute(sent, "visit", [(v, v ^ 1) for v in range(strips)])
    partial_sums = (kept + given.astype(F32)).astype(BF16)
    everyone = range(patches * strips)
    received = lax.all_to_all(
        partial_sums, ("patch", "visit"), split_axis=0, concat_axis=0, tiled=True,
        axis_index_groups=[[d for d in everyone if d % 2 == c] for c in range(2)],
    )
    shape = jax.ShapeDtypeStruct((strip, width), F32)
    return pl.pallas_call(
        partial(detect_kernel, halo),
        out_shape=(shape, shape),
        in_specs=[vmem, vmem],
        out_specs=(vmem, vmem),
        compiler_params=pltpu.CompilerParams(vmem_limit_bytes=48 * 1024 * 1024),
        name="detect_strip",
    )(received, det_taps)


def solution(mesh):
    in_specs = (
        P(("patch", "visit"), None, None),
        P(("patch", "visit"), None),
        P(("patch", "visit")),
        P(("patch", "visit")),
        P(("patch", "visit")),
        P(),
        P(),
        P(),
        P(),
    )
    out_specs = (P(("patch", "visit"), None), P(("patch", "visit"), None))
    return jax.shard_map(shards, mesh=mesh, in_specs=in_specs, out_specs=out_specs, check_vma=False)
```

```python
from functools import partial
import math

import jax
import jax.numpy as jnp
from jax import lax
from jax.experimental import pallas as pl
from jax.experimental.pallas import tpu as pltpu
from jax.sharding import PartitionSpec as P

PH = 256
F32 = jnp.float32
BF16 = jnp.bfloat16


def iota(shape, dim):
    return lax.broadcasted_iota(jnp.int32, shape, dim)


def dot(a, b):
    return jnp.dot(a, b, preferred_element_type=F32)


def dot_nt(a, b):
    return lax.dot_general(a, b, (((1,), (1,)), ((), ())), preferred_element_type=F32)


def dot_tn(a, b):
    return lax.dot_general(a, b, (((0,), (0,)), ((), ())), preferred_element_type=F32)


def toeplitz(taps, rows, lanes, shift):
    first = pltpu.roll(jnp.broadcast_to(taps, (8, lanes)), 0, 1, stride=1, stride_axis=0)
    blocks = [pltpu.roll(first, (i + shift) % lanes, 1) for i in range(0, rows, 8)]
    return jnp.concatenate(blocks, axis=0)


def masked_bands(table, rows, lanes, shift, mask):
    padded = jnp.concatenate(
        [table, jnp.zeros((table.shape[0], lanes - table.shape[1]), F32)], axis=1
    )
    for b in range(table.shape[0]):
        yield b, jnp.where(mask, toeplitz(padded[b:b + 1], rows, lanes, shift), 0.0)


def split(x):
    high = x.astype(BF16)
    return high, (x - high.astype(F32)).astype(BF16)


def coadd_kernel(
    geometry,
    col_h, row_h, dest_h, off_h, kind_h, weight_h, coef_h, pieces_h, dest_s_h, off_s_h,
    kept, sent,
    col, row, dest_v, off_v, kind_v, weight_v, coef, pieces, dest_s, off_s,
    col_bands, row_bands, factors, scaled, acc, den, sems,
):
    patches, strips, halo, stride, group = geometry
    count, height, width = pieces.shape
    basis, taps = col.shape
    half = taps // 2
    strip = PH // strips
    span = kept.shape[1]
    sources = (
        col_h, row_h, dest_h, off_h, kind_h, weight_h, coef_h, pieces_h, dest_s_h, off_s_h
    )
    targets = (col, row, dest_v, off_v, kind_v, weight_v, coef, pieces, dest_s, off_s)
    copies = [
        pltpu.make_async_copy(source, target, sems.at[k])
        for k, (source, target) in enumerate(zip(sources, targets))
    ]
    for copy in copies:
        copy.start()
    acc[...] = jnp.zeros_like(acc)
    for copy in copies[:2]:
        copy.wait()
    x, y = iota((width, width), 1), iota((width, width), 0)
    near = jnp.abs(x - y) <= half
    for b, band in masked_bands(col[...].astype(F32), width, width, -half, near):
        col_bands[b * width:(b + 1) * width, :] = band.astype(BF16)
    near = near & (x // height == y // height)
    for b, band in masked_bands(row[...].astype(F32), width, width, -half, near):
        row_bands[b * width:(b + 1) * width, :] = band.astype(BF16)
    for copy in copies[2:]:
        copy.wait()
    kinds = coef.shape[1]
    weight = weight_v[...].astype(F32)
    picked = jnp.where(iota((kinds, count), 0) == kind_v[...], weight, 0.0).astype(BF16)
    high, low = split(coef[...])
    high, low = split(dot(high, picked) + dot(low, picked))
    spread = (
        iota((basis, basis * width), 1) // width == iota((basis, basis * width), 0)
    ).astype(BF16)
    factors[...] = dot_tn(high, spread) + dot_tn(low, spread)
    share = jnp.where(iota((patches, count), 0) == dest_v[...], weight, 0.0).astype(BF16)
    for v in range(strips):
        at = iota((width, count), 0) + (v * strip - halo) - off_v[...]
        covered = ((at >= 0) & (at < height)).astype(BF16)
        den[v] = dot_nt(share, covered)

    def step(i, carry):
        base = pl.multiple_of(i * 2 * group, 2 * group)
        images = jnp.concatenate(
            [
                pieces[pl.ds(base + g * group, group)].reshape(width, width)
                for g in range(2)
            ],
            axis=1,
        )
        for b in range(basis):
            at = slice(b * width, (b + 1) * width)
            rowed = dot(row_bands[at, :], images)
            scale = factors[pl.ds(base, 2 * group), at]
            for g in range(2):
                for j in range(group):
                    part = rowed[j * height:(j + 1) * height, g * width:(g + 1) * width]
                    part = part * scale[g * group + j:g * group + j + 1]
                    first = g * width + j * height
                    scaled[first:first + height, at] = part.astype(BF16)
        matched = dot(scaled[...], col_bands[...])
        for j in range(2 * group):
            place = pl.ds(dest_s[base + j] * stride + halo + off_s[base + j], height)
            acc[place, :] = acc[place, :] + matched[j * height:(j + 1) * height]
        return carry

    lax.fori_loop(0, count // (2 * group), step, 0)
    own = iota((span, width), 0) < strip + 2 * halo

    me = lax.axis_index("patch") * strips + lax.axis_index("visit")
    parts = patches * strips
    bits = parts.bit_length() - 1

    def strip_at(position):
        away = 0
        for k in range(bits):
            away = away | (((position >> k) & 1) << (bits - 1 - k))
        device = away ^ me
        p, v = device // strips, lax.rem(device, strips)
        base = pl.multiple_of(p * stride + v * strip, 8)
        return jnp.where(own, acc[pl.ds(base, span), :], den[v, pl.ds(p, 1), :])

    def finish(i, carry):
        sent[i] = strip_at(i + parts // 2).astype(BF16)
        kept[i] = strip_at(i)
        return carry

    lax.fori_loop(0, parts // 2, finish, 0)


def detect_kernel(halo, kept, given, taps_ref, coadd, detection):
    span, width = kept.shape[1:]
    strip = coadd.shape[0]
    taps = taps_ref.shape[1]
    total = kept[0] + given[0].astype(F32)
    rows = iota((span, width), 0)
    square = jnp.broadcast_to(total[strip + 2 * halo:strip + 2 * halo + 1], (width, width))
    weight = jnp.transpose(square)[:span]
    value = jnp.where(rows < strip + 2 * halo, total / (1.0 + weight), 0.0)
    coadd[...] = value[halo:halo + strip]
    table = taps_ref[...].astype(F32)
    diff = iota((width, width), 1) - iota((width, width), 0)
    ((_, columns),) = masked_bands(table[1:2], width, width, -halo, jnp.abs(diff) <= halo)
    diff = iota((strip, width), 1) - iota((strip, width), 0)
    ((_, filt),) = masked_bands(table[0:1], strip, width, 0, (diff >= 0) & (diff < taps))
    columns, filt = columns.astype(BF16), filt.astype(BF16)
    high, low = split(value)
    smooth = dot(high, columns) + dot(low, columns)
    smooth = jnp.concatenate([smooth, jnp.zeros((width - span, width), F32)], axis=0)
    high, low = split(smooth)
    detection[...] = dot(filt, high) + dot(filt, low)


def shards(
    pieces, dest, offsets, kernel_index, weights, basis_col, basis_row, coef_table, det_taps
):
    patches = lax.axis_size("patch")
    strips = lax.axis_size("visit")
    count, height, width = pieces.shape
    basis = basis_col.shape[0]
    halo = det_taps.shape[1] // 2
    strip = PH // strips
    span = -(-(strip + 2 * halo + 1) // 8) * 8
    stride = strip * (strips - 1) + span
    group = width // height
    parts = patches * strips
    vmem = pl.BlockSpec(memory_space=pltpu.VMEM)
    inputs = (
        basis_col, basis_row, dest.reshape(1, count), offsets.reshape(1, count),
        kernel_index.reshape(1, count), weights.reshape(1, count), coef_table.T, pieces,
        dest[:, 0], offsets,
    )
    shape = (parts // 2, span, width)
    kept, sent = pl.pallas_call(
        partial(coadd_kernel, (patches, strips, halo, stride, group)),
        out_shape=(jax.ShapeDtypeStruct(shape, F32), jax.ShapeDtypeStruct(shape, BF16)),
        in_specs=[pl.BlockSpec(memory_space=pltpu.HBM)] * len(inputs),
        out_specs=(vmem, vmem),
        scratch_shapes=[pltpu.VMEM(x.shape, x.dtype) for x in inputs[:-2]]
        + [pltpu.SMEM(x.shape, x.dtype) for x in inputs[-2:]]
        + [
            pltpu.VMEM((basis * width, width), BF16),
            pltpu.VMEM((basis * width, width), BF16),
            pltpu.VMEM((count, basis * width), F32),
            pltpu.VMEM((2 * width, basis * width), BF16),
            pltpu.VMEM((patches * stride, width), F32),
            pltpu.VMEM((strips, patches, width), F32),
            pltpu.SemaphoreType.DMA((len(inputs),)),
        ],
        compiler_params=pltpu.CompilerParams(vmem_limit_bytes=48 * 1024 * 1024),
        name="coadd_partials",
    )(*[pltpu.with_memory_space_constraint(x, pltpu.HBM) for x in inputs])
    bit, left = 1, parts // 2
    while True:
        axis, hop = ("visit", bit) if bit < strips else ("patch", bit // strips)
        pairs = [(i, i ^ hop) for i in range(lax.axis_size(axis))]
        given = lax.ppermute(sent, axis, pairs)
        if left == 1:
            break
        left = left // 2
        sent = (kept[left:] + given[left:].astype(F32)).astype(BF16)
        kept = kept[:left] + given[:left].astype(F32)
        bit = bit * 2
    shape = jax.ShapeDtypeStruct((strip, width), F32)
    return pl.pallas_call(
        partial(detect_kernel, halo),
        out_shape=(shape, shape),
        in_specs=[vmem] * 3,
        out_specs=(vmem, vmem),
        compiler_params=pltpu.CompilerParams(vmem_limit_bytes=48 * 1024 * 1024),
        name="detect_strip",
    )(kept, given, det_taps)


def solution(mesh):
    in_specs = (
        P(("patch", "visit"), None, None),
        P(("patch", "visit"), None),
        P(("patch", "visit")),
        P(("patch", "visit")),
        P(("patch", "visit")),
        P(),
        P(),
        P(),
        P(),
    )
    out_specs = (P(("patch", "visit"), None), P(("patch", "visit"), None))
    return jax.shard_map(shards, mesh=mesh, in_specs=in_specs, out_specs=out_specs, check_vma=False)
```

```python
from functools import partial
import math

import jax
import jax.numpy as jnp
from jax import lax
from jax.experimental import pallas as pl
from jax.experimental.pallas import tpu as pltpu
from jax.sharding import PartitionSpec as P

PH = 256
F32 = jnp.float32
BF16 = jnp.bfloat16


def iota(shape, dim):
    return lax.broadcasted_iota(jnp.int32, shape, dim)


def dot(a, b):
    return jnp.dot(a, b, preferred_element_type=F32)


def dot_nt(a, b):
    return lax.dot_general(a, b, (((1,), (1,)), ((), ())), preferred_element_type=F32)


def dot_tn(a, b):
    return lax.dot_general(a, b, (((0,), (0,)), ((), ())), preferred_element_type=F32)


def toeplitz(taps, rows, lanes, shift):
    first = pltpu.roll(jnp.broadcast_to(taps, (8, lanes)), 0, 1, stride=1, stride_axis=0)
    blocks = [pltpu.roll(first, (i + shift) % lanes, 1) for i in range(0, rows, 8)]
    return jnp.concatenate(blocks, axis=0)


def masked_bands(table, rows, lanes, shift, mask):
    padded = jnp.concatenate(
        [table, jnp.zeros((table.shape[0], lanes - table.shape[1]), F32)], axis=1
    )
    for b in range(table.shape[0]):
        yield b, jnp.where(mask, toeplitz(padded[b:b + 1], rows, lanes, shift), 0.0)


def split(x):
    high = x.astype(BF16)
    return high, (x - high.astype(F32)).astype(BF16)


def coadd_kernel(
    geometry,
    col_h, row_h, dest_h, off_h, kind_h, weight_h, coef_h, taps_h, pieces_h,
    dest_s_h, off_s_h,
    kept_0, sent_0, kept_1, sent_1, across, along,
    col, row, dest_v, off_v, kind_v, weight_v, coef, det_taps, pieces, dest_s, off_s,
    col_bands, row_bands, factors, even, odd, acc, den, sems,
):
    patches, strips, halo, stride, group, orders, cuts = geometry
    outs = ((kept_0, sent_0), (kept_1, sent_1))
    count, height, width = pieces.shape
    basis, taps = col.shape
    half = taps // 2
    strip = PH // strips
    span = cuts[-1][1]
    sources = (
        col_h, row_h, dest_h, off_h, kind_h, weight_h, coef_h, taps_h, pieces_h, dest_s_h,
        off_s_h,
    )
    targets = (
        col, row, dest_v, off_v, kind_v, weight_v, coef, det_taps, pieces, dest_s, off_s
    )
    copies = [
        pltpu.make_async_copy(source, target, sems.at[k])
        for k, (source, target) in enumerate(zip(sources, targets))
    ]
    for copy in copies:
        copy.start()
    acc[...] = jnp.zeros_like(acc)
    for copy in copies[:2]:
        copy.wait()
    x, y = iota((width, width), 1), iota((width, width), 0)
    near = jnp.abs(x - y) <= half
    for b, band in masked_bands(col[...].astype(F32), width, width, -half, near):
        col_bands[b * width:(b + 1) * width, :] = band.astype(BF16)
    near = near & (x // height == y // height)
    for b, band in masked_bands(row[...].astype(F32), width, width, -half, near):
        row_bands[b * width:(b + 1) * width, :] = band.astype(BF16)
    for copy in copies[2:]:
        copy.wait()
    table, detect = det_taps[...].astype(F32), det_taps.shape[1]
    ((_, band),) = masked_bands(table[1:2], width, width, -halo, jnp.abs(x - y) <= halo)
    across[...] = band.astype(BF16)
    diff = iota((strip, width), 1) - iota((strip, width), 0)
    ((_, band),) = masked_bands(table[0:1], strip, width, 0, (diff >= 0) & (diff < detect))
    along[...] = band.astype(BF16)
    kinds = coef.shape[1]
    weight = weight_v[...].astype(F32)
    picked = jnp.where(iota((kinds, count), 0) == kind_v[...], weight, 0.0).astype(BF16)
    high, low = split(coef[...])
    high, low = split(dot(high, picked) + dot(low, picked))
    spread = (
        iota((basis, basis * width), 1) // width == iota((basis, basis * width), 0)
    ).astype(BF16)
    factors[...] = dot_tn(high, spread) + dot_tn(low, spread)
    share = jnp.where(iota((patches, count), 0) == dest_v[...], weight, 0.0).astype(BF16)
    for v in range(strips):
        at = iota((width, count), 0) + (v * strip - halo) - off_v[...]
        covered = ((at >= 0) & (at < height)).astype(BF16)
        den[v] = dot_nt(share, covered)

    def row_step(i, scaled):
        base = pl.multiple_of(i * 2 * group, 2 * group)
        images = jnp.concatenate(
            [
                pieces[pl.ds(base + g * group, group)].reshape(width, width)
                for g in range(2)
            ],
            axis=1,
        )
        for b in range(basis):
            at = slice(b * width, (b + 1) * width)
            rowed = dot(row_bands[at, :], images)
            scale = factors[pl.ds(base, 2 * group), at]
            for g in range(2):
                for j in range(group):
                    part = rowed[j * height:(j + 1) * height, g * width:(g + 1) * width]
                    part = part * scale[g * group + j:g * group + j + 1]
                    first = g * width + j * height
                    scaled[first:first + height, at] = part.astype(BF16)

    def column_step(i, scaled):
        base = i * 2 * group
        matched = dot(scaled[...], col_bands[...])
        for j in range(2 * group):
            place = pl.ds(dest_s[base + j] * stride + halo + off_s[base + j], height)
            acc[place, :] = acc[place, :] + matched[j * height:(j + 1) * height]

    chunks = count // (2 * group)
    row_step(0, even)

    def two(k, carry):
        row_step(2 * k + 1, odd)
        column_step(2 * k, even)
        row_step(2 * k + 2, even)
        column_step(2 * k + 1, odd)
        return carry

    lax.fori_loop(0, chunks // 2 - 1, two, 0)
    row_step(chunks - 1, odd)
    column_step(chunks - 2, even)
    column_step(chunks - 1, odd)
    own = iota((span, width), 0) < strip + 2 * halo
    me = lax.axis_index("patch") * strips + lax.axis_index("visit")
    parts = patches * strips

    def strip_at(position, order):
        away = 0
        for k, bit in enumerate(reversed(order)):
            away = away | (((position >> k) & 1) << bit)
        device = away ^ me
        p, v = device // strips, lax.rem(device, strips)
        base = pl.multiple_of(p * stride + v * strip, 8)
        return jnp.where(own, acc[pl.ds(base, span), :], den[v, pl.ds(p, 1), :])

    def finish(i, carry):
        for (kept, sent), order, (low, high) in zip(outs, orders, cuts):
            sent[i] = strip_at(i + parts // 2, order)[low:high].astype(BF16)
            kept[i] = strip_at(i, order)[low:high]
        return carry

    lax.fori_loop(0, parts // 2, finish, 0, unroll=2)


def detect_kernel(halo, kept_0, given_0, kept_1, given_1, across, along, coadd, detection):
    width = kept_0.shape[2]
    span = kept_0.shape[1] + kept_1.shape[1]
    strip = coadd.shape[0]
    total = jnp.concatenate(
        [kept_0[0] + given_0[0].astype(F32), kept_1[0] + given_1[0].astype(F32)], axis=0
    )
    rows = iota((span, width), 0)
    square = jnp.broadcast_to(total[strip + 2 * halo:strip + 2 * halo + 1], (width, width))
    weight = jnp.transpose(square)[:span]
    value = jnp.where(rows < strip + 2 * halo, total / (1.0 + weight), 0.0)
    coadd[...] = value[halo:halo + strip]
    columns, filt = across[...], along[...]
    high, low = split(value)
    smooth = dot(high, columns) + dot(low, columns)
    smooth = jnp.concatenate([smooth, jnp.zeros((width - span, width), F32)], axis=0)
    high, low = split(smooth)
    detection[...] = dot(filt, high) + dot(filt, low)


def shards(
    pieces, dest, offsets, kernel_index, weights, basis_col, basis_row, coef_table, det_taps
):
    patches = lax.axis_size("patch")
    strips = lax.axis_size("visit")
    count, height, width = pieces.shape
    basis = basis_col.shape[0]
    halo = det_taps.shape[1] // 2
    strip = PH // strips
    span = -(-(strip + 2 * halo + 1) // 8) * 8
    stride = strip * (strips - 1) + span
    group = width // height
    parts = patches * strips
    vmem = pl.BlockSpec(memory_space=pltpu.VMEM)
    inputs = (
        basis_col, basis_row, dest.reshape(1, count), offsets.reshape(1, count),
        kernel_index.reshape(1, count), weights.reshape(1, count), coef_table.T, det_taps, pieces,
        dest[:, 0], offsets,
    )
    bits = parts.bit_length() - 1
    swapped = list(range(bits))
    for k in range(1, bits - 1, 2):
        swapped[k], swapped[k + 1] = k + 1, k
    orders = (tuple(range(bits)), tuple(swapped))
    middle = (span + 16) // 32 * 16
    cuts = ((0, middle), (middle, span))
    shapes = []
    for low, high in cuts:
        shape = (parts // 2, high - low, width)
        shapes += [jax.ShapeDtypeStruct(shape, F32), jax.ShapeDtypeStruct(shape, BF16)]
    shapes += [jax.ShapeDtypeStruct((rows, width), BF16) for rows in (width, strip)]
    *partial_sums, across, along = pl.pallas_call(
        partial(coadd_kernel, (patches, strips, halo, stride, group, orders, cuts)),
        out_shape=shapes,
        in_specs=[pl.BlockSpec(memory_space=pltpu.HBM)] * len(inputs),
        out_specs=[vmem] * 6,
        scratch_shapes=[pltpu.VMEM(x.shape, x.dtype) for x in inputs[:-2]]
        + [pltpu.SMEM(x.shape, x.dtype) for x in inputs[-2:]]
        + [
            pltpu.VMEM((basis * width, width), BF16),
            pltpu.VMEM((basis * width, width), BF16),
            pltpu.VMEM((count, basis * width), F32),
            pltpu.VMEM((2 * width, basis * width), BF16),
            pltpu.VMEM((2 * width, basis * width), BF16),
            pltpu.VMEM((patches * stride, width), F32),
            pltpu.VMEM((strips, patches, width), F32),
            pltpu.SemaphoreType.DMA((len(inputs),)),
        ],
        compiler_params=pltpu.CompilerParams(vmem_limit_bytes=48 * 1024 * 1024),
        name="coadd_partials",
    )(*[pltpu.with_memory_space_constraint(x, pltpu.HBM) for x in inputs])
    kept, sent, given = list(partial_sums[0::2]), list(partial_sums[1::2]), [None, None]
    left = parts // 2
    for stage in range(bits):
        for c in range(2):
            bit = 1 << orders[c][stage]
            axis, hop = ("visit", bit) if bit < strips else ("patch", bit // strips)
            pairs = [(i, i ^ hop) for i in range(lax.axis_size(axis))]
            given[c] = lax.ppermute(sent[c], axis, pairs)
        left = left // 2
        for c in range(2 if left else 0):
            sent[c] = (kept[c][left:] + given[c][left:].astype(F32)).astype(BF16)
            kept[c] = kept[c][:left] + given[c][:left].astype(F32)
    shape = jax.ShapeDtypeStruct((strip, width), F32)
    return pl.pallas_call(
        partial(detect_kernel, halo),
        out_shape=(shape, shape),
        in_specs=[vmem] * 6,
        out_specs=(vmem, vmem),
        compiler_params=pltpu.CompilerParams(vmem_limit_bytes=48 * 1024 * 1024),
        name="detect_strip",
    )(kept[0], given[0], kept[1], given[1], across, along)


def solution(mesh):
    in_specs = (
        P(("patch", "visit"), None, None),
        P(("patch", "visit"), None),
        P(("patch", "visit")),
        P(("patch", "visit")),
        P(("patch", "visit")),
        P(),
        P(),
        P(),
        P(),
    )
    out_specs = (P(("patch", "visit"), None), P(("patch", "visit"), None))
    return jax.shard_map(shards, mesh=mesh, in_specs=in_specs, out_specs=out_specs, check_vma=False)
```

```python
from functools import partial
import math

import jax
import jax.numpy as jnp
from jax import lax
from jax.experimental import pallas as pl
from jax.experimental.pallas import tpu as pltpu
from jax.sharding import PartitionSpec as P

PH = 256
F32 = jnp.float32
BF16 = jnp.bfloat16


def iota(shape, dim):
    return lax.broadcasted_iota(jnp.int32, shape, dim)


def dot(a, b):
    return jnp.dot(a, b, preferred_element_type=F32)


def dot_nt(a, b):
    return lax.dot_general(a, b, (((1,), (1,)), ((), ())), preferred_element_type=F32)


def dot_tn(a, b):
    return lax.dot_general(a, b, (((0,), (0,)), ((), ())), preferred_element_type=F32)


def toeplitz(taps, rows, lanes, shift):
    first = pltpu.roll(jnp.broadcast_to(taps, (8, lanes)), 0, 1, stride=1, stride_axis=0)
    blocks = [pltpu.roll(first, (i + shift) % lanes, 1) for i in range(0, rows, 8)]
    return jnp.concatenate(blocks, axis=0)


def masked_bands(table, rows, lanes, shift, mask):
    padded = jnp.concatenate(
        [table, jnp.zeros((table.shape[0], lanes - table.shape[1]), F32)], axis=1
    )
    for b in range(table.shape[0]):
        yield b, jnp.where(mask, toeplitz(padded[b:b + 1], rows, lanes, shift), 0.0)


def split(x):
    high = x.astype(BF16)
    return high, (x - high.astype(F32)).astype(BF16)


def coadd_kernel(
    geometry,
    col_h, row_h, dest_h, off_h, kind_h, weight_h, coef_h, taps_h, pieces_h,
    dest_s_h, off_s_h,
    kept, sent, across, along,
    col, row, dest_v, off_v, kind_v, weight_v, coef, det_taps, pieces, dest_s, off_s,
    col_bands, row_bands, factors, even, odd, acc, den, sems,
):
    patches, strips, halo, stride, group, order = geometry
    count, height, width = pieces.shape
    basis, taps = col.shape
    half = taps // 2
    strip = PH // strips
    span = kept.shape[1]
    sources = (
        col_h, row_h, dest_h, off_h, kind_h, weight_h, coef_h, taps_h, pieces_h, dest_s_h,
        off_s_h,
    )
    targets = (
        col, row, dest_v, off_v, kind_v, weight_v, coef, det_taps, pieces, dest_s, off_s
    )
    copies = [
        pltpu.make_async_copy(source, target, sems.at[k])
        for k, (source, target) in enumerate(zip(sources, targets))
    ]
    for copy in copies:
        copy.start()
    acc[...] = jnp.zeros_like(acc)
    for copy in copies[:2]:
        copy.wait()
    x, y = iota((width, width), 1), iota((width, width), 0)
    near = jnp.abs(x - y) <= half
    for b, band in masked_bands(col[...].astype(F32), width, width, -half, near):
        col_bands[b * width:(b + 1) * width, :] = band.astype(BF16)
    near = near & (x // height == y // height)
    for b, band in masked_bands(row[...].astype(F32), width, width, -half, near):
        row_bands[b * width:(b + 1) * width, :] = band.astype(BF16)
    for copy in copies[2:]:
        copy.wait()
    table, detect = det_taps[...].astype(F32), det_taps.shape[1]
    ((_, band),) = masked_bands(table[1:2], width, width, -halo, jnp.abs(x - y) <= halo)
    across[...] = band.astype(BF16)
    diff = iota((strip, width), 1) - iota((strip, width), 0)
    ((_, band),) = masked_bands(table[0:1], strip, width, 0, (diff >= 0) & (diff < detect))
    along[...] = band.astype(BF16)
    kinds = coef.shape[1]
    weight = weight_v[...].astype(F32)
    picked = jnp.where(iota((kinds, count), 0) == kind_v[...], weight, 0.0).astype(BF16)
    high, low = split(coef[...])
    high, low = split(dot(high, picked) + dot(low, picked))
    spread = (
        iota((basis, basis * width), 1) // width == iota((basis, basis * width), 0)
    ).astype(BF16)
    factors[...] = dot_tn(high, spread) + dot_tn(low, spread)
    share = jnp.where(iota((patches, count), 0) == dest_v[...], weight, 0.0).astype(BF16)
    for v in range(strips):
        at = iota((width, count), 0) + (v * strip - halo) - off_v[...]
        covered = ((at >= 0) & (at < height)).astype(BF16)
        den[v] = dot_nt(share, covered)

    def row_step(i, scaled):
        base = pl.multiple_of(i * 2 * group, 2 * group)
        images = jnp.concatenate(
            [
                pieces[pl.ds(base + g * group, group)].reshape(width, width)
                for g in range(2)
            ],
            axis=1,
        )
        for b in range(basis):
            at = slice(b * width, (b + 1) * width)
            rowed = dot(row_bands[at, :], images)
            scale = factors[pl.ds(base, 2 * group), at]
            for g in range(2):
                for j in range(group):
                    part = rowed[j * height:(j + 1) * height, g * width:(g + 1) * width]
                    part = part * scale[g * group + j:g * group + j + 1]
                    first = g * width + j * height
                    scaled[first:first + height, at] = part.astype(BF16)

    def column_step(i, scaled):
        base = i * 2 * group
        matched = dot(scaled[...], col_bands[...])
        for j in range(2 * group):
            place = pl.ds(dest_s[base + j] * stride + halo + off_s[base + j], height)
            acc[place, :] = acc[place, :] + matched[j * height:(j + 1) * height]

    chunks = count // (2 * group)
    row_step(0, even)

    def two(k, carry):
        row_step(2 * k + 1, odd)
        column_step(2 * k, even)
        row_step(2 * k + 2, even)
        column_step(2 * k + 1, odd)
        return carry

    lax.fori_loop(0, chunks // 2 - 1, two, 0)
    row_step(chunks - 1, odd)
    column_step(chunks - 2, even)
    column_step(chunks - 1, odd)
    own = iota((span, width), 0) < strip + 2 * halo
    me = lax.axis_index("patch") * strips + lax.axis_index("visit")
    parts = patches * strips

    def strip_at(position):
        away = 0
        for k, bit in enumerate(reversed(order)):
            away = away | (((position >> k) & 1) << bit)
        device = away ^ me
        p, v = device // strips, lax.rem(device, strips)
        base = pl.multiple_of(p * stride + v * strip, 8)
        return jnp.where(own, acc[pl.ds(base, span), :], den[v, pl.ds(p, 1), :])

    def finish(i, carry):
        sent[i] = strip_at(i + parts // 2).astype(BF16)
        kept[i] = strip_at(i)
        return carry

    lax.fori_loop(0, parts // 2, finish, 0, unroll=4)


def detect_kernel(halo, *refs):
    *terms, across, along, coadd, detection = refs
    span, width = terms[0].shape[1:]
    strip = coadd.shape[0]
    total = terms[0][0]
    for term in terms[1:]:
        total = total + term[0].astype(F32)
    rows = iota((span, width), 0)
    square = jnp.broadcast_to(total[strip + 2 * halo:strip + 2 * halo + 1], (width, width))
    weight = jnp.transpose(square)[:span]
    value = jnp.where(rows < strip + 2 * halo, total / (1.0 + weight), 0.0)
    coadd[...] = value[halo:halo + strip]
    columns, filt = across[...], along[...]
    high, low = split(value)
    smooth = dot(high, columns) + dot(low, columns)
    smooth = jnp.concatenate([smooth, jnp.zeros((width - span, width), F32)], axis=0)
    high, low = split(smooth)
    detection[...] = dot(filt, high) + dot(filt, low)


def direct_order(k):
    return (k & 7).bit_count() * 16 + (k & 7) * 2 + (k < 8)


def shards(
    pieces, dest, offsets, kernel_index, weights, basis_col, basis_row, coef_table, det_taps
):
    patches = lax.axis_size("patch")
    strips = lax.axis_size("visit")
    count, height, width = pieces.shape
    basis = basis_col.shape[0]
    halo = det_taps.shape[1] // 2
    strip = PH // strips
    span = -(-(strip + 2 * halo + 1) // 8) * 8
    stride = strip * (strips - 1) + span
    group = width // height
    parts = patches * strips
    vmem = pl.BlockSpec(memory_space=pltpu.VMEM)
    inputs = (
        basis_col, basis_row, dest.reshape(1, count), offsets.reshape(1, count),
        kernel_index.reshape(1, count), weights.reshape(1, count), coef_table.T, det_taps, pieces,
        dest[:, 0], offsets,
    )
    bits = parts.bit_length() - 1
    halved = max(1, bits - 4)
    order = tuple(range(halved)) + tuple(reversed(range(halved, bits)))
    shape = (parts // 2, span, width)
    shapes = [jax.ShapeDtypeStruct(shape, F32), jax.ShapeDtypeStruct(shape, BF16)]
    shapes += [jax.ShapeDtypeStruct((rows, width), BF16) for rows in (width, strip)]
    kept, sent, across, along = pl.pallas_call(
        partial(coadd_kernel, (patches, strips, halo, stride, group, order)),
        out_shape=shapes,
        in_specs=[pl.BlockSpec(memory_space=pltpu.HBM)] * len(inputs),
        out_specs=[vmem] * 4,
        scratch_shapes=[pltpu.VMEM(x.shape, x.dtype) for x in inputs[:-2]]
        + [pltpu.SMEM(x.shape, x.dtype) for x in inputs[-2:]]
        + [
            pltpu.VMEM((basis * width, width), BF16),
            pltpu.VMEM((basis * width, width), BF16),
            pltpu.VMEM((count, basis * width), F32),
            pltpu.VMEM((2 * width, basis * width), BF16),
            pltpu.VMEM((2 * width, basis * width), BF16),
            pltpu.VMEM((patches * stride, width), F32),
            pltpu.VMEM((strips, patches, width), F32),
            pltpu.SemaphoreType.DMA((len(inputs),)),
        ],
        compiler_params=pltpu.CompilerParams(vmem_limit_bytes=48 * 1024 * 1024),
        name="coadd_partials",
    )(*[pltpu.with_memory_space_constraint(x, pltpu.HBM) for x in inputs])
    def exchange(x, hop):
        return lax.ppermute(x, ("patch", "visit"), [(d, d ^ hop) for d in range(parts)])

    left = parts // 2
    for bit in range(halved):
        given = exchange(sent, 1 << bit)
        if bit + 1 < halved:
            left = left // 2
            sent = (kept[left:] + given[left:].astype(F32)).astype(BF16)
            kept, given = kept[:left], given[:left]
            kept = kept + given.astype(F32)
    terms = [kept[:1] + given[:1].astype(F32)]
    for k in sorted(range(1, left), key=direct_order):
        strip_sum = (kept[k:k + 1] + given[k:k + 1].astype(F32)).astype(BF16)
        terms.append(exchange(strip_sum, k << halved))
    shape = jax.ShapeDtypeStruct((strip, width), F32)
    return pl.pallas_call(
        partial(detect_kernel, halo),
        out_shape=(shape, shape),
        in_specs=[vmem] * (len(terms) + 2),
        out_specs=(vmem, vmem),
        compiler_params=pltpu.CompilerParams(vmem_limit_bytes=48 * 1024 * 1024),
        name="detect_strip",
    )(*terms, across, along)


def solution(mesh):
    in_specs = (
        P(("patch", "visit"), None, None),
        P(("patch", "visit"), None),
        P(("patch", "visit")),
        P(("patch", "visit")),
        P(("patch", "visit")),
        P(),
        P(),
        P(),
        P(),
    )
    out_specs = (P(("patch", "visit"), None), P(("patch", "visit"), None))
    return jax.shard_map(shards, mesh=mesh, in_specs=in_specs, out_specs=out_specs, check_vma=False)
```

```python
from functools import partial
import math

import jax
import jax.numpy as jnp
from jax import lax
from jax.experimental import pallas as pl
from jax.experimental.pallas import tpu as pltpu
from jax.sharding import PartitionSpec as P

PH = 256
F32 = jnp.float32
BF16 = jnp.bfloat16


def iota(shape, dim):
    return lax.broadcasted_iota(jnp.int32, shape, dim)


def dot(a, b):
    return jnp.dot(a, b, preferred_element_type=F32)


def dot_nt(a, b):
    return lax.dot_general(a, b, (((1,), (1,)), ((), ())), preferred_element_type=F32)


def dot_tn(a, b):
    return lax.dot_general(a, b, (((0,), (0,)), ((), ())), preferred_element_type=F32)


def toeplitz(taps, rows, lanes, shift):
    first = pltpu.roll(jnp.broadcast_to(taps, (8, lanes)), 0, 1, stride=1, stride_axis=0)
    blocks = [pltpu.roll(first, (i + shift) % lanes, 1) for i in range(0, rows, 8)]
    return jnp.concatenate(blocks, axis=0)


def masked_bands(table, rows, lanes, shift, mask):
    padded = jnp.concatenate(
        [table, jnp.zeros((table.shape[0], lanes - table.shape[1]), F32)], axis=1
    )
    for b in range(table.shape[0]):
        yield b, jnp.where(mask, toeplitz(padded[b:b + 1], rows, lanes, shift), 0.0)


def split(x):
    high = x.astype(BF16)
    return high, (x - high.astype(F32)).astype(BF16)


def coadd_kernel(
    geometry,
    col_h, row_h, dest_h, off_h, kind_h, weight_h, coef_h, taps_h, pieces_h,
    dest_s_h, off_s_h,
    kept_0, kept_1, sent_0, sent_1, across, along,
    col, row, dest_v, off_v, kind_v, weight_v, coef, det_taps, pieces, dest_s, off_s,
    col_bands, row_bands, factors, scaled_0, scaled_1, acc, den, sems,
):
    patches, strips, halo, stride, group, orders, cuts = geometry
    count, height, width = pieces.shape
    basis, taps = col.shape
    half = taps // 2
    strip = PH // strips
    span = cuts[-1][1]
    sources = (
        col_h, row_h, dest_h, off_h, kind_h, weight_h, coef_h, taps_h, pieces_h, dest_s_h,
        off_s_h,
    )
    targets = (
        col, row, dest_v, off_v, kind_v, weight_v, coef, det_taps, pieces, dest_s, off_s
    )
    copies = [
        pltpu.make_async_copy(source, target, sems.at[k])
        for k, (source, target) in enumerate(zip(sources, targets))
    ]
    for copy in copies:
        copy.start()
    acc[...] = jnp.zeros_like(acc)
    for copy in copies[:2]:
        copy.wait()
    x, y = iota((width, width), 1), iota((width, width), 0)
    near = jnp.abs(x - y) <= half
    for b, band in masked_bands(col[...].astype(F32), width, width, -half, near):
        col_bands[b * width:(b + 1) * width, :] = band.astype(BF16)
    near = near & (x // height == y // height)
    for b, band in masked_bands(row[...].astype(F32), width, width, -half, near):
        row_bands[b * width:(b + 1) * width, :] = band.astype(BF16)
    for copy in copies[2:]:
        copy.wait()
    table, detect = det_taps[...].astype(F32), det_taps.shape[1]
    ((_, band),) = masked_bands(table[1:2], width, width, -halo, jnp.abs(x - y) <= halo)
    across[...] = band.astype(BF16)
    diff = iota((strip, width), 1) - iota((strip, width), 0)
    ((_, band),) = masked_bands(table[0:1], strip, width, 0, (diff >= 0) & (diff < detect))
    along[...] = band.astype(BF16)
    kinds = coef.shape[1]
    weight = weight_v[...].astype(F32)
    picked = jnp.where(iota((kinds, count), 0) == kind_v[...], weight, 0.0).astype(BF16)
    high, low = split(coef[...])
    high, low = split(dot(high, picked) + dot(low, picked))
    spread = (
        iota((basis, basis * width), 1) // width == iota((basis, basis * width), 0)
    ).astype(BF16)
    factors[...] = dot_tn(high, spread) + dot_tn(low, spread)
    share = jnp.where(iota((patches, count), 0) == dest_v[...], weight, 0.0).astype(BF16)
    for v in range(strips):
        at = iota((width, count), 0) + (v * strip - halo) - off_v[...]
        covered = ((at >= 0) & (at < height)).astype(BF16)
        den[v] = dot_nt(share, covered)

    def row_step(i, scaled):
        base = pl.multiple_of(i * 2 * group, 2 * group)
        images = jnp.concatenate(
            [
                pieces[pl.ds(base + g * group, group)].reshape(width, width)
                for g in range(2)
            ],
            axis=1,
        )
        for b in range(basis):
            at = slice(b * width, (b + 1) * width)
            rowed = dot(row_bands[at, :], images)
            scale = factors[pl.ds(base, 2 * group), at]
            for g in range(2):
                for j in range(group):
                    part = rowed[j * height:(j + 1) * height, g * width:(g + 1) * width]
                    part = part * scale[g * group + j:g * group + j + 1]
                    first = g * width + j * height
                    scaled[first:first + height, at] = part.astype(BF16)

    def column_step(i, scaled):
        base = i * 2 * group
        matched = dot(scaled[...], col_bands[...])
        for j in range(2 * group):
            place = pl.ds(dest_s[base + j] * stride + halo + off_s[base + j], height)
            acc[place, :] = acc[place, :] + matched[j * height:(j + 1) * height]

    chunks = count // (2 * group)
    row_step(0, scaled_0)

    def two(k, carry):
        row_step(2 * k + 1, scaled_1)
        column_step(2 * k, scaled_0)
        row_step(2 * k + 2, scaled_0)
        column_step(2 * k + 1, scaled_1)
        return carry

    lax.fori_loop(0, chunks // 2 - 1, two, 0)
    row_step(chunks - 1, scaled_1)
    column_step(chunks - 2, scaled_0)
    column_step(chunks - 1, scaled_1)
    own = iota((span, width), 0) < strip + 2 * halo
    me = lax.axis_index("patch") * strips + lax.axis_index("visit")
    parts = patches * strips
    gatherer = me | 1

    def strip_at(position, order):
        away = 0
        for k, bit in enumerate(reversed(order)):
            away = away | (((position >> k) & 1) << bit)
        device = away ^ gatherer
        p, v = device // strips, lax.rem(device, strips)
        base = pl.multiple_of(p * stride + v * strip, 8)
        return jnp.where(own, acc[pl.ds(base, span), :], den[v, pl.ds(p, 1), :])

    def finish(outs):
        def place(i, carry):
            for out, order, (low, high) in zip(outs, orders, cuts):
                out[i] = strip_at(i, order)[low:high].astype(out.dtype)
            return carry

        lax.fori_loop(0, parts, place, 0, unroll=4)

    odd = lax.rem(me, 2) == 1
    pl.when(odd)(lambda: finish((kept_0, kept_1)))
    pl.when(jnp.logical_not(odd))(lambda: finish((sent_0, sent_1)))


def detect_kernel(halo, kept, given, across, along, coadd, detection):
    span, width = kept.shape
    strip = coadd.shape[0]
    odd = lax.rem(lax.axis_index("visit"), 2) == 1
    total = jnp.where(odd, kept[...], given[...])
    rows = iota((span, width), 0)
    square = jnp.broadcast_to(total[strip + 2 * halo:strip + 2 * halo + 1], (width, width))
    weight = jnp.transpose(square)[:span]
    value = jnp.where(rows < strip + 2 * halo, total / (1.0 + weight), 0.0)
    coadd[...] = value[halo:halo + strip]
    columns, filt = across[...], along[...]
    high, low = split(value)
    smooth = dot(high, columns) + dot(low, columns)
    smooth = jnp.concatenate([smooth, jnp.zeros((width - span, width), F32)], axis=0)
    high, low = split(smooth)
    detection[...] = dot(filt, high) + dot(filt, low)


def shards(
    pieces, dest, offsets, kernel_index, weights, basis_col, basis_row, coef_table, det_taps
):
    patches = lax.axis_size("patch")
    strips = lax.axis_size("visit")
    count, height, width = pieces.shape
    basis = basis_col.shape[0]
    halo = det_taps.shape[1] // 2
    strip = PH // strips
    span = -(-(strip + 2 * halo + 1) // 8) * 8
    stride = strip * (strips - 1) + span
    group = width // height
    parts = patches * strips
    vmem = pl.BlockSpec(memory_space=pltpu.VMEM)
    inputs = (
        basis_col, basis_row, dest.reshape(1, count), offsets.reshape(1, count),
        kernel_index.reshape(1, count), weights.reshape(1, count), coef_table.T, det_taps, pieces,
        dest[:, 0], offsets,
    )
    bits = parts.bit_length() - 1
    stages = list(range(1, bits))
    swapped = list(stages)
    for k in range(0, bits - 2, 2):
        swapped[k], swapped[k + 1] = stages[k + 1], stages[k]
    orders = (tuple(stages) + (0,), tuple(swapped) + (0,))
    middle = (span + 16) // 32 * 16
    cuts = ((0, middle), (middle, span))
    shapes = [
        jax.ShapeDtypeStruct((parts, high - low, width), dtype)
        for dtype in (F32, BF16)
        for low, high in cuts
    ]
    shapes += [jax.ShapeDtypeStruct((rows, width), BF16) for rows in (width, strip)]
    grant = 8 * 1024 * 1024 + 6 * parts * span * width + 4 * patches * stride * width
    *partial_sums, across, along = pl.pallas_call(
        partial(coadd_kernel, (patches, strips, halo, stride, group, orders, cuts)),
        out_shape=shapes,
        in_specs=[pl.BlockSpec(memory_space=pltpu.HBM)] * len(inputs),
        out_specs=[vmem] * 6,
        scratch_shapes=[pltpu.VMEM(x.shape, x.dtype) for x in inputs[:-2]]
        + [pltpu.SMEM(x.shape, x.dtype) for x in inputs[-2:]]
        + [
            pltpu.VMEM((basis * width, width), BF16),
            pltpu.VMEM((basis * width, width), BF16),
            pltpu.VMEM((count, basis * width), F32),
            pltpu.VMEM((2 * width, basis * width), BF16),
            pltpu.VMEM((2 * width, basis * width), BF16),
            pltpu.VMEM((patches * stride, width), F32),
            pltpu.VMEM((strips, patches, width), F32),
            pltpu.SemaphoreType.DMA((len(inputs),)),
        ],
        compiler_params=pltpu.CompilerParams(vmem_limit_bytes=grant),
        name="coadd_partials",
    )(*[pltpu.with_memory_space_constraint(x, pltpu.HBM) for x in inputs])
    def exchange(x, pairs):
        return lax.ppermute(x, ("patch", "visit"), pairs)

    kept, sent = list(partial_sums[:2]), list(partial_sums[2:])
    given = [exchange(x, [(d, d + 1) for d in range(0, parts, 2)]) for x in sent]
    left = parts
    for stage in range(bits - 1):
        left = left // 2
        for c in range(2):
            hop = 1 << orders[c][stage]
            sent = (kept[c][left:] + given[c][left:].astype(F32)).astype(BF16)
            kept[c] = kept[c][:left] + given[c][:left].astype(F32)
            given[c] = exchange(sent, [(d, d ^ hop) for d in range(1, parts, 2)])
    total = jnp.concatenate(
        [kept[c] + given[c].astype(F32) for c in range(2)], axis=1
    )
    passed = exchange(total[1], [(d, d - 1) for d in range(1, parts, 2)])
    shape = jax.ShapeDtypeStruct((strip, width), F32)
    return pl.pallas_call(
        partial(detect_kernel, halo),
        out_shape=(shape, shape),
        in_specs=[vmem] * 4,
        out_specs=(vmem, vmem),
        compiler_params=pltpu.CompilerParams(vmem_limit_bytes=48 * 1024 * 1024),
        name="detect_strip",
    )(total[0], passed, across, along)


def solution(mesh):
    in_specs = (
        P(("patch", "visit"), None, None),
        P(("patch", "visit"), None),
        P(("patch", "visit")),
        P(("patch", "visit")),
        P(("patch", "visit")),
        P(),
        P(),
        P(),
        P(),
    )
    out_specs = (P(("patch", "visit"), None), P(("patch", "visit"), None))
    return jax.shard_map(shards, mesh=mesh, in_specs=in_specs, out_specs=out_specs, check_vma=False)
```

```python
from functools import partial
import math

import jax
import jax.numpy as jnp
from jax import lax
from jax.experimental import pallas as pl
from jax.experimental.pallas import tpu as pltpu
from jax.sharding import PartitionSpec as P

PH = 256
F32 = jnp.float32
BF16 = jnp.bfloat16


def iota(shape, dim):
    return lax.broadcasted_iota(jnp.int32, shape, dim)


def dot(a, b):
    return jnp.dot(a, b, preferred_element_type=F32)


def dot_nt(a, b):
    return lax.dot_general(a, b, (((1,), (1,)), ((), ())), preferred_element_type=F32)


def dot_tn(a, b):
    return lax.dot_general(a, b, (((0,), (0,)), ((), ())), preferred_element_type=F32)


def toeplitz(taps, rows, lanes, shift):
    first = pltpu.roll(jnp.broadcast_to(taps, (8, lanes)), 0, 1, stride=1, stride_axis=0)
    blocks = [pltpu.roll(first, (i + shift) % lanes, 1) for i in range(0, rows, 8)]
    return jnp.concatenate(blocks, axis=0)


def masked_bands(table, rows, lanes, shift, mask):
    padded = jnp.concatenate(
        [table, jnp.zeros((table.shape[0], lanes - table.shape[1]), F32)], axis=1
    )
    for b in range(table.shape[0]):
        yield b, jnp.where(mask, toeplitz(padded[b:b + 1], rows, lanes, shift), 0.0)


def split(x):
    high = x.astype(BF16)
    return high, (x - high.astype(F32)).astype(BF16)


def coadd_kernel(
    geometry,
    col_h, row_h, dest_h, off_h, kind_h, weight_h, coef_h, taps_h, pieces_h,
    dest_s_h, off_s_h,
    kept_0, sent_0, kept_1, sent_1, across, along,
    col, row, dest_v, off_v, kind_v, weight_v, coef, det_taps, pieces, dest_s, off_s,
    col_bands, row_bands, factors, even, odd, acc, den, sems,
):
    patches, strips, halo, stride, group, orders, direct, cuts = geometry
    outs = ((kept_0, sent_0), (kept_1, sent_1))
    count, height, width = pieces.shape
    basis, taps = col.shape
    half = taps // 2
    strip = PH // strips
    span = cuts[-1][1]
    sources = (
        col_h, row_h, dest_h, off_h, kind_h, weight_h, coef_h, taps_h, pieces_h, dest_s_h,
        off_s_h,
    )
    targets = (
        col, row, dest_v, off_v, kind_v, weight_v, coef, det_taps, pieces, dest_s, off_s
    )
    copies = [
        pltpu.make_async_copy(source, target, sems.at[k])
        for k, (source, target) in enumerate(zip(sources, targets))
    ]
    for copy in copies:
        copy.start()
    acc[...] = jnp.zeros_like(acc)
    for copy in copies[:2]:
        copy.wait()
    x, y = iota((width, width), 1), iota((width, width), 0)
    near = jnp.abs(x - y) <= half
    for b, band in masked_bands(col[...].astype(F32), width, width, -half, near):
        col_bands[b * width:(b + 1) * width, :] = band.astype(BF16)
    near = near & (x // height == y // height)
    for b, band in masked_bands(row[...].astype(F32), width, width, -half, near):
        row_bands[b * width:(b + 1) * width, :] = band.astype(BF16)
    for copy in copies[2:]:
        copy.wait()
    table, detect = det_taps[...].astype(F32), det_taps.shape[1]
    ((_, band),) = masked_bands(table[1:2], width, width, -halo, jnp.abs(x - y) <= halo)
    across[...] = band.astype(BF16)
    diff = iota((strip, width), 1) - iota((strip, width), 0)
    ((_, band),) = masked_bands(table[0:1], strip, width, 0, (diff >= 0) & (diff < detect))
    along[...] = band.astype(BF16)
    kinds = coef.shape[1]
    weight = weight_v[...].astype(F32)
    picked = jnp.where(iota((kinds, count), 0) == kind_v[...], weight, 0.0).astype(BF16)
    high, low = split(coef[...])
    high, low = split(dot(high, picked) + dot(low, picked))
    spread = (
        iota((basis, basis * width), 1) // width == iota((basis, basis * width), 0)
    ).astype(BF16)
    factors[...] = dot_tn(high, spread) + dot_tn(low, spread)
    share = jnp.where(iota((patches, count), 0) == dest_v[...], weight, 0.0).astype(BF16)
    for v in range(strips):
        at = iota((width, count), 0) + (v * strip - halo) - off_v[...]
        covered = ((at >= 0) & (at < height)).astype(BF16)
        den[v] = dot_nt(share, covered)

    def row_step(i, scaled):
        base = pl.multiple_of(i * 2 * group, 2 * group)
        images = jnp.concatenate(
            [
                pieces[pl.ds(base + g * group, group)].reshape(width, width)
                for g in range(2)
            ],
            axis=1,
        )
        for b in range(basis):
            at = slice(b * width, (b + 1) * width)
            rowed = dot(row_bands[at, :], images)
            scale = factors[pl.ds(base, 2 * group), at]
            for g in range(2):
                for j in range(group):
                    part = rowed[j * height:(j + 1) * height, g * width:(g + 1) * width]
                    part = part * scale[g * group + j:g * group + j + 1]
                    first = g * width + j * height
                    scaled[first:first + height, at] = part.astype(BF16)

    def column_step(i, scaled):
        base = i * 2 * group
        matched = dot(scaled[...], col_bands[...])
        for j in range(2 * group):
            place = pl.ds(dest_s[base + j] * stride + halo + off_s[base + j], height)
            acc[place, :] = acc[place, :] + matched[j * height:(j + 1) * height]

    chunks = count // (2 * group)
    row_step(0, even)

    def two(k, carry):
        row_step(2 * k + 1, odd)
        column_step(2 * k, even)
        row_step(2 * k + 2, even)
        column_step(2 * k + 1, odd)
        return carry

    lax.fori_loop(0, chunks // 2 - 1, two, 0)
    row_step(chunks - 1, odd)
    column_step(chunks - 2, even)
    column_step(chunks - 1, odd)
    own = iota((span, width), 0) < strip + 2 * halo
    me = lax.axis_index("patch") * strips + lax.axis_index("visit")
    parts = patches * strips

    def strip_at(position, order):
        rest = position & ((1 << direct) - 1)
        away = (rest << len(order)) | jnp.minimum(rest, 1)
        for k, mask in enumerate(reversed(order)):
            away = away ^ (((position >> (k + direct)) & 1) * mask)
        device = away ^ me
        p, v = device // strips, lax.rem(device, strips)
        base = pl.multiple_of(p * stride + v * strip, 8)
        return jnp.where(own, acc[pl.ds(base, span), :], den[v, pl.ds(p, 1), :])

    def finish(i, carry):
        for (kept, sent), order, (low, high) in zip(outs, orders, cuts):
            sent[i] = strip_at(i + parts // 2, order)[low:high].astype(BF16)
            kept[i] = strip_at(i, order)[low:high]
        return carry

    lax.fori_loop(0, parts // 2, finish, 0, unroll=2)


def detect_kernel(halo, *refs):
    *terms, across, along, coadd, detection = refs
    span, width = terms[0].shape
    strip = coadd.shape[0]
    total = terms[0][...]
    for term in terms[1:]:
        total = total + term[...].astype(F32)
    rows = iota((span, width), 0)
    square = jnp.broadcast_to(total[strip + 2 * halo:strip + 2 * halo + 1], (width, width))
    weight = jnp.transpose(square)[:span]
    value = jnp.where(rows < strip + 2 * halo, total / (1.0 + weight), 0.0)
    coadd[...] = value[halo:halo + strip]
    columns, filt = across[...], along[...]
    high, low = split(value)
    smooth = dot(high, columns) + dot(low, columns)
    smooth = jnp.concatenate([smooth, jnp.zeros((width - span, width), F32)], axis=0)
    high, low = split(smooth)
    detection[...] = dot(filt, high) + dot(filt, low)


def shards(
    pieces, dest, offsets, kernel_index, weights, basis_col, basis_row, coef_table, det_taps
):
    patches = lax.axis_size("patch")
    strips = lax.axis_size("visit")
    count, height, width = pieces.shape
    basis = basis_col.shape[0]
    halo = det_taps.shape[1] // 2
    strip = PH // strips
    span = -(-(strip + 2 * halo + 1) // 8) * 8
    stride = strip * (strips - 1) + span
    group = width // height
    parts = patches * strips
    vmem = pl.BlockSpec(memory_space=pltpu.VMEM)
    inputs = (
        basis_col, basis_row, dest.reshape(1, count), offsets.reshape(1, count),
        kernel_index.reshape(1, count), weights.reshape(1, count), coef_table.T, det_taps, pieces,
        dest[:, 0], offsets,
    )
    bits = parts.bit_length() - 1
    direct = min(2, bits - 1)
    stages = [1 << k | 1 for k in range(bits - direct)]
    swapped = list(stages)
    for k in range(1, len(stages) - 1, 2):
        swapped[k], swapped[k + 1] = stages[k + 1], stages[k]
    orders = (tuple(stages), tuple(swapped))
    middle = (span + 16) // 32 * 16
    cuts = ((0, middle), (middle, span))
    shapes = []
    for low, high in cuts:
        shape = (parts // 2, high - low, width)
        shapes += [jax.ShapeDtypeStruct(shape, F32), jax.ShapeDtypeStruct(shape, BF16)]
    shapes += [jax.ShapeDtypeStruct((rows, width), BF16) for rows in (width, strip)]
    *partial_sums, across, along = pl.pallas_call(
        partial(coadd_kernel, (patches, strips, halo, stride, group, orders, direct, cuts)),
        out_shape=shapes,
        in_specs=[pl.BlockSpec(memory_space=pltpu.HBM)] * len(inputs),
        out_specs=[vmem] * 6,
        scratch_shapes=[pltpu.VMEM(x.shape, x.dtype) for x in inputs[:-2]]
        + [pltpu.SMEM(x.shape, x.dtype) for x in inputs[-2:]]
        + [
            pltpu.VMEM((basis * width, width), BF16),
            pltpu.VMEM((basis * width, width), BF16),
            pltpu.VMEM((count, basis * width), F32),
            pltpu.VMEM((2 * width, basis * width), BF16),
            pltpu.VMEM((2 * width, basis * width), BF16),
            pltpu.VMEM((patches * stride, width), F32),
            pltpu.VMEM((strips, patches, width), F32),
            pltpu.SemaphoreType.DMA((len(inputs),)),
        ],
        compiler_params=pltpu.CompilerParams(vmem_limit_bytes=48 * 1024 * 1024),
        name="coadd_partials",
    )(*[pltpu.with_memory_space_constraint(x, pltpu.HBM) for x in inputs])
    def exchange(x, mask):
        return lax.ppermute(x, ("patch", "visit"), [(d, d ^ mask) for d in range(parts)])

    kept, sent, given = list(partial_sums[0::2]), list(partial_sums[1::2]), [None, None]
    left = parts // 2
    for stage in range(len(stages)):
        for c in range(2):
            if stage:
                sent[c] = (kept[c][left:] + given[c][left:].astype(F32)).astype(BF16)
                kept[c] = kept[c][:left] + given[c][:left].astype(F32)
            given[c] = exchange(sent[c], orders[c][stage])
        left = left // 2
    terms = []
    for k in range(1 << direct):
        strip_sum = jnp.concatenate(
            [kept[c][k] + given[c][k].astype(F32) for c in range(2)], axis=0
        )
        terms.append(
            exchange(strip_sum.astype(BF16), k << len(stages) | 1) if k else strip_sum
        )
    shape = jax.ShapeDtypeStruct((strip, width), F32)
    return pl.pallas_call(
        partial(detect_kernel, halo),
        out_shape=(shape, shape),
        in_specs=[vmem] * (len(terms) + 2),
        out_specs=(vmem, vmem),
        compiler_params=pltpu.CompilerParams(vmem_limit_bytes=48 * 1024 * 1024),
        name="detect_strip",
    )(*terms, across, along)


def solution(mesh):
    in_specs = (
        P(("patch", "visit"), None, None),
        P(("patch", "visit"), None),
        P(("patch", "visit")),
        P(("patch", "visit")),
        P(("patch", "visit")),
        P(),
        P(),
        P(),
        P(),
    )
    out_specs = (P(("patch", "visit"), None), P(("patch", "visit"), None))
    return jax.shard_map(shards, mesh=mesh, in_specs=in_specs, out_specs=out_specs, check_vma=False)
```

```python
from functools import partial
import math

import jax
import jax.numpy as jnp
from jax import lax
from jax.experimental import pallas as pl
from jax.experimental.pallas import tpu as pltpu
from jax.sharding import PartitionSpec as P

PH = 256
F32 = jnp.float32
BF16 = jnp.bfloat16


def iota(shape, dim):
    return lax.broadcasted_iota(jnp.int32, shape, dim)


def dot(a, b):
    return jnp.dot(a, b, preferred_element_type=F32)


def dot_nt(a, b):
    return lax.dot_general(a, b, (((1,), (1,)), ((), ())), preferred_element_type=F32)


def dot_tn(a, b):
    return lax.dot_general(a, b, (((0,), (0,)), ((), ())), preferred_element_type=F32)


def toeplitz(taps, rows, lanes, shift):
    first = pltpu.roll(jnp.broadcast_to(taps, (8, lanes)), 0, 1, stride=1, stride_axis=0)
    blocks = [pltpu.roll(first, (i + shift) % lanes, 1) for i in range(0, rows, 8)]
    return jnp.concatenate(blocks, axis=0)


def masked_bands(table, rows, lanes, shift, mask):
    padded = jnp.concatenate(
        [table, jnp.zeros((table.shape[0], lanes - table.shape[1]), F32)], axis=1
    )
    for b in range(table.shape[0]):
        yield b, jnp.where(mask, toeplitz(padded[b:b + 1], rows, lanes, shift), 0.0)


def split(x):
    high = x.astype(BF16)
    return high, (x - high.astype(F32)).astype(BF16)


def coadd_kernel(
    geometry,
    col_h, row_h, dest_h, off_h, kind_h, weight_h, coef_h, taps_h, pieces_h,
    dest_s_h, off_s_h,
    kept_0, sent_0, kept_1, sent_1, across, along,
    col, row, dest_v, off_v, kind_v, weight_v, coef, det_taps, pieces, dest_s, off_s,
    col_bands, row_bands, factors, even, odd, acc_0, acc_1, den, sems,
):
    patches, strips, halo, stride, group, orders, direct, cuts = geometry
    outs = ((kept_0, sent_0), (kept_1, sent_1))
    count, height, width = pieces.shape
    basis, taps = col.shape
    half = taps // 2
    strip = PH // strips
    span = cuts[-1][1]
    sources = (
        col_h, row_h, dest_h, off_h, kind_h, weight_h, coef_h, taps_h, pieces_h, dest_s_h,
        off_s_h,
    )
    targets = (
        col, row, dest_v, off_v, kind_v, weight_v, coef, det_taps, pieces, dest_s, off_s
    )
    copies = [
        pltpu.make_async_copy(source, target, sems.at[k])
        for k, (source, target) in enumerate(zip(sources, targets))
    ]
    for copy in copies:
        copy.start()
    acc_0[...] = jnp.zeros_like(acc_0)
    acc_1[...] = jnp.zeros_like(acc_1)
    for copy in copies[:2]:
        copy.wait()
    x, y = iota((width, width), 1), iota((width, width), 0)
    near = jnp.abs(x - y) <= half
    for b, band in masked_bands(col[...].astype(F32), width, width, -half, near):
        col_bands[b * width:(b + 1) * width, :] = band.astype(BF16)
    near = near & (x // height == y // height)
    for b, band in masked_bands(row[...].astype(F32), width, width, -half, near):
        row_bands[b * width:(b + 1) * width, :] = band.astype(BF16)
    for copy in copies[2:]:
        copy.wait()
    table, detect = det_taps[...].astype(F32), det_taps.shape[1]
    ((_, band),) = masked_bands(table[1:2], width, width, -halo, jnp.abs(x - y) <= halo)
    across[...] = band.astype(BF16)
    diff = iota((strip, width), 1) - iota((strip, width), 0)
    ((_, band),) = masked_bands(table[0:1], strip, width, 0, (diff >= 0) & (diff < detect))
    along[...] = band.astype(BF16)
    kinds = coef.shape[1]
    weight = weight_v[...].astype(F32)
    picked = jnp.where(iota((kinds, count), 0) == kind_v[...], weight, 0.0).astype(BF16)
    high, low = split(coef[...])
    high, low = split(dot(high, picked) + dot(low, picked))
    spread = (
        iota((basis, basis * width), 1) // width == iota((basis, basis * width), 0)
    ).astype(BF16)
    factors[...] = dot_tn(high, spread) + dot_tn(low, spread)
    share = jnp.where(iota((patches, count), 0) == dest_v[...], weight, 0.0).astype(BF16)
    for v in range(strips):
        at = iota((width, count), 0) + (v * strip - halo) - off_v[...]
        covered = ((at >= 0) & (at < height)).astype(BF16)
        den[v] = dot_nt(share, covered)

    def row_step(i, scaled):
        base = pl.multiple_of(i * 2 * group, 2 * group)
        images = jnp.concatenate(
            [
                pieces[pl.ds(base + g * group, group)].reshape(width, width)
                for g in range(2)
            ],
            axis=1,
        )
        for b in range(basis):
            at = slice(b * width, (b + 1) * width)
            rowed = dot(row_bands[at, :], images)
            scale = factors[pl.ds(base, 2 * group), at]
            for g in range(2):
                for j in range(group):
                    part = rowed[j * height:(j + 1) * height, g * width:(g + 1) * width]
                    part = part * scale[g * group + j:g * group + j + 1]
                    first = g * width + j * height
                    scaled[first:first + height, at] = part.astype(BF16)

    def column_step(i, scaled):
        base = i * 2 * group
        matched = dot(scaled[...], col_bands[...])
        for j in range(2 * group):
            place = pl.ds(dest_s[base + j] * stride + halo + off_s[base + j], height)
            acc = (acc_0, acc_1)[j % 2]
            acc[place, :] = acc[place, :] + matched[j * height:(j + 1) * height]

    chunks = count // (2 * group)
    row_step(0, even)

    def two(k, carry):
        row_step(2 * k + 1, odd)
        column_step(2 * k, even)
        row_step(2 * k + 2, even)
        column_step(2 * k + 1, odd)
        return carry

    lax.fori_loop(0, chunks // 2 - 1, two, 0)
    row_step(chunks - 1, odd)
    column_step(chunks - 2, even)
    column_step(chunks - 1, odd)
    own = iota((span, width), 0) < strip + 2 * halo
    me = lax.axis_index("patch") * strips + lax.axis_index("visit")
    parts = patches * strips

    def strip_at(position, order):
        rest = position & ((1 << direct) - 1)
        away = (rest << len(order)) | jnp.minimum(rest, 1)
        for k, mask in enumerate(reversed(order)):
            away = away ^ (((position >> (k + direct)) & 1) * mask)
        device = away ^ me
        p, v = device // strips, lax.rem(device, strips)
        base = pl.multiple_of(p * stride + v * strip, 8)
        total = acc_0[pl.ds(base, span), :] + acc_1[pl.ds(base, span), :]
        return jnp.where(own, total, den[v, pl.ds(p, 1), :])

    def finish(i, carry):
        for (kept, sent), order, (low, high) in zip(outs, orders, cuts):
            sent[i] = strip_at(i + parts // 2, order)[low:high].astype(BF16)
            kept[i] = strip_at(i, order)[low:high]
        return carry

    lax.fori_loop(0, parts // 2, finish, 0, unroll=2)


def detect_kernel(halo, *refs):
    *terms, across, along, coadd, detection = refs
    span, width = terms[0].shape
    strip = coadd.shape[0]
    total = terms[0][...]
    for term in terms[1:]:
        total = total + term[...].astype(F32)
    rows = iota((span, width), 0)
    square = jnp.broadcast_to(total[strip + 2 * halo:strip + 2 * halo + 1], (width, width))
    weight = jnp.transpose(square)[:span]
    value = jnp.where(rows < strip + 2 * halo, total / (1.0 + weight), 0.0)
    coadd[...] = value[halo:halo + strip]
    columns, filt = across[...], along[...]
    high, low = split(value)
    smooth = dot(high, columns) + dot(low, columns)
    smooth = jnp.concatenate([smooth, jnp.zeros((width - span, width), F32)], axis=0)
    high, low = split(smooth)
    detection[...] = dot(filt, high) + dot(filt, low)


def shards(
    pieces, dest, offsets, kernel_index, weights, basis_col, basis_row, coef_table, det_taps
):
    patches = lax.axis_size("patch")
    strips = lax.axis_size("visit")
    count, height, width = pieces.shape
    basis = basis_col.shape[0]
    halo = det_taps.shape[1] // 2
    strip = PH // strips
    span = -(-(strip + 2 * halo + 1) // 8) * 8
    stride = strip * (strips - 1) + span
    group = width // height
    parts = patches * strips
    vmem = pl.BlockSpec(memory_space=pltpu.VMEM)
    inputs = (
        basis_col, basis_row, dest.reshape(1, count), offsets.reshape(1, count),
        kernel_index.reshape(1, count), weights.reshape(1, count), coef_table.T, det_taps, pieces,
        dest[:, 0], offsets,
    )
    bits = parts.bit_length() - 1
    direct = min(2, bits - 1)
    stages = [1 << k | 1 for k in range(bits - direct)]
    swapped = list(stages)
    for k in range(1, len(stages) - 1, 2):
        swapped[k], swapped[k + 1] = stages[k + 1], stages[k]
    orders = (tuple(stages), tuple(swapped))
    middle = (span + 16) // 32 * 16
    cuts = ((0, middle), (middle, span))
    shapes = []
    for low, high in cuts:
        shape = (parts // 2, high - low, width)
        shapes += [jax.ShapeDtypeStruct(shape, F32), jax.ShapeDtypeStruct(shape, BF16)]
    shapes += [jax.ShapeDtypeStruct((rows, width), BF16) for rows in (width, strip)]
    grant = 8 * 1024 * 1024 + 3 * parts * span * width + 8 * patches * stride * width
    *partial_sums, across, along = pl.pallas_call(
        partial(coadd_kernel, (patches, strips, halo, stride, group, orders, direct, cuts)),
        out_shape=shapes,
        in_specs=[pl.BlockSpec(memory_space=pltpu.HBM)] * len(inputs),
        out_specs=[vmem] * 6,
        scratch_shapes=[pltpu.VMEM(x.shape, x.dtype) for x in inputs[:-2]]
        + [pltpu.SMEM(x.shape, x.dtype) for x in inputs[-2:]]
        + [
            pltpu.VMEM((basis * width, width), BF16),
            pltpu.VMEM((basis * width, width), BF16),
            pltpu.VMEM((count, basis * width), F32),
            pltpu.VMEM((2 * width, basis * width), BF16),
            pltpu.VMEM((2 * width, basis * width), BF16),
            pltpu.VMEM((patches * stride, width), F32),
            pltpu.VMEM((patches * stride, width), F32),
            pltpu.VMEM((strips, patches, width), F32),
            pltpu.SemaphoreType.DMA((len(inputs),)),
        ],
        compiler_params=pltpu.CompilerParams(vmem_limit_bytes=grant),
        name="coadd_partials",
    )(*[pltpu.with_memory_space_constraint(x, pltpu.HBM) for x in inputs])
    def exchange(x, mask):
        return lax.ppermute(x, ("patch", "visit"), [(d, d ^ mask) for d in range(parts)])

    kept, sent, given = list(partial_sums[0::2]), list(partial_sums[1::2]), [None, None]
    left = parts // 2
    for stage in range(len(stages)):
        for c in range(2):
            if stage:
                sent[c] = (kept[c][left:] + given[c][left:].astype(F32)).astype(BF16)
                kept[c] = kept[c][:left] + given[c][:left].astype(F32)
            given[c] = exchange(sent[c], orders[c][stage])
        left = left // 2
    terms = []
    for k in [0] + list(reversed(range(1, 1 << direct))):
        strip_sum = jnp.concatenate(
            [kept[c][k] + given[c][k].astype(F32) for c in range(2)], axis=0
        )
        terms.append(
            exchange(strip_sum.astype(BF16), k << len(stages) | 1) if k else strip_sum
        )
    shape = jax.ShapeDtypeStruct((strip, width), F32)
    return pl.pallas_call(
        partial(detect_kernel, halo),
        out_shape=(shape, shape),
        in_specs=[vmem] * (len(terms) + 2),
        out_specs=(vmem, vmem),
        compiler_params=pltpu.CompilerParams(vmem_limit_bytes=48 * 1024 * 1024),
        name="detect_strip",
    )(*terms, across, along)


def solution(mesh):
    in_specs = (
        P(("patch", "visit"), None, None),
        P(("patch", "visit"), None),
        P(("patch", "visit")),
        P(("patch", "visit")),
        P(("patch", "visit")),
        P(),
        P(),
        P(),
        P(),
    )
    out_specs = (P(("patch", "visit"), None), P(("patch", "visit"), None))
    return jax.shard_map(shards, mesh=mesh, in_specs=in_specs, out_specs=out_specs, check_vma=False)
```

```python
from functools import partial
import math

import jax
import jax.numpy as jnp
from jax import lax
from jax.experimental import pallas as pl
from jax.experimental.pallas import tpu as pltpu
from jax.sharding import PartitionSpec as P

PH = 256
F32 = jnp.float32
BF16 = jnp.bfloat16


def iota(shape, dim):
    return lax.broadcasted_iota(jnp.int32, shape, dim)


def dot(a, b):
    return jnp.dot(a, b, preferred_element_type=F32)


def dot_nt(a, b):
    return lax.dot_general(a, b, (((1,), (1,)), ((), ())), preferred_element_type=F32)


def dot_tn(a, b):
    return lax.dot_general(a, b, (((0,), (0,)), ((), ())), preferred_element_type=F32)


def toeplitz(taps, rows, lanes, shift):
    first = pltpu.roll(jnp.broadcast_to(taps, (8, lanes)), 0, 1, stride=1, stride_axis=0)
    blocks = [pltpu.roll(first, (i + shift) % lanes, 1) for i in range(0, rows, 8)]
    return jnp.concatenate(blocks, axis=0)


def masked_bands(table, rows, lanes, shift, mask):
    padded = jnp.concatenate(
        [table, jnp.zeros((table.shape[0], lanes - table.shape[1]), F32)], axis=1
    )
    for b in range(table.shape[0]):
        yield b, jnp.where(mask, toeplitz(padded[b:b + 1], rows, lanes, shift), 0.0)


def split(x):
    high = x.astype(BF16)
    return high, (x - high.astype(F32)).astype(BF16)


def coadd_kernel(
    geometry,
    col_h, row_h, dest_h, off_h, kind_h, weight_h, coef_h, taps_h, pieces_h,
    dest_s_h, off_s_h,
    kept_0, sent_0, kept_1, sent_1, across, along,
    col, row, dest_v, off_v, kind_v, weight_v, coef, det_taps, pieces, dest_s, off_s,
    col_bands, row_bands, factors, even, odd, acc_0, acc_1, den, sems,
):
    patches, strips, halo, stride, group, groups, orders, direct, cuts = geometry
    outs = ((kept_0, sent_0), (kept_1, sent_1))
    count, height, width = pieces.shape
    basis, taps = col.shape
    half = taps // 2
    strip = PH // strips
    span = cuts[-1][1]
    sources = (
        col_h, row_h, dest_h, off_h, kind_h, weight_h, coef_h, taps_h, pieces_h, dest_s_h,
        off_s_h,
    )
    targets = (
        col, row, dest_v, off_v, kind_v, weight_v, coef, det_taps, pieces, dest_s, off_s
    )
    copies = [
        pltpu.make_async_copy(source, target, sems.at[k])
        for k, (source, target) in enumerate(zip(sources, targets))
    ]
    for copy in copies:
        copy.start()
    acc_0[...] = jnp.zeros_like(acc_0)
    acc_1[...] = jnp.zeros_like(acc_1)
    for copy in copies[:2]:
        copy.wait()
    x, y = iota((width, width), 1), iota((width, width), 0)
    near = jnp.abs(x - y) <= half
    for b, band in masked_bands(col[...].astype(F32), width, width, -half, near):
        col_bands[b * width:(b + 1) * width, :] = band.astype(BF16)
    near = near & (x // height == y // height)
    for b, band in masked_bands(row[...].astype(F32), width, width, -half, near):
        row_bands[b * width:(b + 1) * width, :] = band.astype(BF16)
    for copy in copies[2:]:
        copy.wait()
    table, detect = det_taps[...].astype(F32), det_taps.shape[1]
    ((_, band),) = masked_bands(table[1:2], width, width, -halo, jnp.abs(x - y) <= halo)
    across[...] = band.astype(BF16)
    diff = iota((strip, width), 1) - iota((strip, width), 0)
    ((_, band),) = masked_bands(table[0:1], strip, width, 0, (diff >= 0) & (diff < detect))
    along[...] = band.astype(BF16)
    kinds = coef.shape[1]
    weight = weight_v[...].astype(F32)
    picked = jnp.where(iota((kinds, count), 0) == kind_v[...], weight, 0.0).astype(BF16)
    high, low = split(coef[...])
    high, low = split(dot(high, picked) + dot(low, picked))
    spread = (
        iota((basis, basis * width), 1) // width == iota((basis, basis * width), 0)
    ).astype(BF16)
    factors[...] = dot_tn(high, spread) + dot_tn(low, spread)
    share = jnp.where(iota((patches, count), 0) == dest_v[...], weight, 0.0).astype(BF16)
    for v in range(strips):
        at = iota((width, count), 0) + (v * strip - halo) - off_v[...]
        covered = ((at >= 0) & (at < height)).astype(BF16)
        den[v] = dot_nt(share, covered)

    chunk, together = groups * group, 2

    def row_step(i, scaled):
        base = pl.multiple_of(i * chunk, chunk)
        images = jnp.concatenate(
            [
                pieces[pl.ds(base + g * group, group)].reshape(width, width)
                for g in range(groups)
            ],
            axis=1,
        )
        for start in range(0, basis, together):
            stop = min(start + together, basis)
            rowed = dot(row_bands[start * width:stop * width, :], images)
            for b in range(start, stop):
                at = slice(b * width, (b + 1) * width)
                scale = factors[pl.ds(base, chunk), at]
                for g in range(groups):
                    for j in range(group):
                        top = (b - start) * width + j * height
                        part = rowed[top:top + height, g * width:(g + 1) * width]
                        part = part * scale[g * group + j:g * group + j + 1]
                        first = g * width + j * height
                        scaled[first:first + height, at] = part.astype(BF16)

    def column_step(i, scaled):
        base = i * chunk
        matched = dot(scaled[...], col_bands[...])
        for j in range(chunk):
            place = pl.ds(dest_s[base + j] * stride + halo + off_s[base + j], height)
            acc = (acc_0, acc_1)[j % 2]
            acc[place, :] = acc[place, :] + matched[j * height:(j + 1) * height]

    chunks = count // chunk
    row_step(0, even)

    def two(k, carry):
        row_step(2 * k + 1, odd)
        column_step(2 * k, even)
        row_step(2 * k + 2, even)
        column_step(2 * k + 1, odd)
        return carry

    lax.fori_loop(0, chunks // 2 - 1, two, 0)
    row_step(chunks - 1, odd)
    column_step(chunks - 2, even)
    column_step(chunks - 1, odd)
    own = iota((span, width), 0) < strip + 2 * halo
    me = lax.axis_index("patch") * strips + lax.axis_index("visit")
    parts = patches * strips

    def strip_at(position, order):
        rest = position & ((1 << direct) - 1)
        away = (rest << len(order)) | jnp.minimum(rest, 1)
        for k, mask in enumerate(reversed(order)):
            away = away ^ (((position >> (k + direct)) & 1) * mask)
        device = away ^ me
        p, v = device // strips, lax.rem(device, strips)
        base = pl.multiple_of(p * stride + v * strip, 8)
        total = acc_0[pl.ds(base, span), :] + acc_1[pl.ds(base, span), :]
        return jnp.where(own, total, den[v, pl.ds(p, 1), :])

    def finish(i, carry):
        for (kept, sent), order, (low, high) in zip(outs, orders, cuts):
            sent[i] = strip_at(i + parts // 2, order)[low:high].astype(BF16)
            kept[i] = strip_at(i, order)[low:high]
        return carry

    lax.fori_loop(0, parts // 2, finish, 0, unroll=2)


def detect_kernel(halo, *refs):
    *terms, across, along, coadd, detection = refs
    span, width = terms[0].shape
    strip = coadd.shape[0]
    total = terms[0][...]
    for term in terms[1:]:
        total = total + term[...].astype(F32)
    rows = iota((span, width), 0)
    square = jnp.broadcast_to(total[strip + 2 * halo:strip + 2 * halo + 1], (width, width))
    weight = jnp.transpose(square)[:span]
    value = jnp.where(rows < strip + 2 * halo, total / (1.0 + weight), 0.0)
    coadd[...] = value[halo:halo + strip]
    columns, filt = across[...], along[...]
    high, low = split(value)
    smooth = dot(high, columns) + dot(low, columns)
    smooth = jnp.concatenate([smooth, jnp.zeros((width - span, width), F32)], axis=0)
    high, low = split(smooth)
    detection[...] = dot(filt, high) + dot(filt, low)


def shards(
    pieces, dest, offsets, kernel_index, weights, basis_col, basis_row, coef_table, det_taps
):
    patches = lax.axis_size("patch")
    strips = lax.axis_size("visit")
    count, height, width = pieces.shape
    basis = basis_col.shape[0]
    halo = det_taps.shape[1] // 2
    strip = PH // strips
    span = -(-(strip + 2 * halo + 1) // 8) * 8
    stride = strip * (strips - 1) + span
    group = width // height
    groups = 4
    parts = patches * strips
    vmem = pl.BlockSpec(memory_space=pltpu.VMEM)
    inputs = (
        basis_col, basis_row, dest.reshape(1, count), offsets.reshape(1, count),
        kernel_index.reshape(1, count), weights.reshape(1, count), coef_table.T, det_taps, pieces,
        dest[:, 0], offsets,
    )
    bits = parts.bit_length() - 1
    direct = min(2, bits - 1)
    stages = [1 << k | 1 for k in range(bits - direct)]
    swapped = list(stages)
    for k in range(1, len(stages) - 1, 2):
        swapped[k], swapped[k + 1] = stages[k + 1], stages[k]
    orders = (tuple(stages), tuple(swapped))
    middle = (span + 16) // 32 * 16
    cuts = ((0, middle), (middle, span))
    shapes = []
    for low, high in cuts:
        shape = (parts // 2, high - low, width)
        shapes += [jax.ShapeDtypeStruct(shape, F32), jax.ShapeDtypeStruct(shape, BF16)]
    shapes += [jax.ShapeDtypeStruct((rows, width), BF16) for rows in (width, strip)]
    grant = 10 * 1024 * 1024 + 3 * parts * span * width + 8 * patches * stride * width
    *partial_sums, across, along = pl.pallas_call(
        partial(coadd_kernel, (patches, strips, halo, stride, group, groups, orders, direct, cuts)),
        out_shape=shapes,
        in_specs=[pl.BlockSpec(memory_space=pltpu.HBM)] * len(inputs),
        out_specs=[vmem] * 6,
        scratch_shapes=[pltpu.VMEM(x.shape, x.dtype) for x in inputs[:-2]]
        + [pltpu.SMEM(x.shape, x.dtype) for x in inputs[-2:]]
        + [
            pltpu.VMEM((basis * width, width), BF16),
            pltpu.VMEM((basis * width, width), BF16),
            pltpu.VMEM((count, basis * width), F32),
            pltpu.VMEM((groups * width, basis * width), BF16),
            pltpu.VMEM((groups * width, basis * width), BF16),
            pltpu.VMEM((patches * stride, width), F32),
            pltpu.VMEM((patches * stride, width), F32),
            pltpu.VMEM((strips, patches, width), F32),
            pltpu.SemaphoreType.DMA((len(inputs),)),
        ],
        compiler_params=pltpu.CompilerParams(vmem_limit_bytes=grant),
        name="coadd_partials",
    )(*[pltpu.with_memory_space_constraint(x, pltpu.HBM) for x in inputs])
    def exchange(x, mask):
        return lax.ppermute(x, ("patch", "visit"), [(d, d ^ mask) for d in range(parts)])

    kept, sent, given = list(partial_sums[0::2]), list(partial_sums[1::2]), [None, None]
    left = parts // 2
    for stage in range(len(stages)):
        for c in range(2):
            if stage:
                sent[c] = (kept[c][left:] + given[c][left:].astype(F32)).astype(BF16)
                kept[c] = kept[c][:left] + given[c][:left].astype(F32)
            given[c] = exchange(sent[c], orders[c][stage])
        left = left // 2
    terms = []
    for k in [0] + list(reversed(range(1, 1 << direct))):
        strip_sum = jnp.concatenate(
            [kept[c][k] + given[c][k].astype(F32) for c in range(2)], axis=0
        )
        terms.append(
            exchange(strip_sum.astype(BF16), k << len(stages) | 1) if k else strip_sum
        )
    shape = jax.ShapeDtypeStruct((strip, width), F32)
    return pl.pallas_call(
        partial(detect_kernel, halo),
        out_shape=(shape, shape),
        in_specs=[vmem] * (len(terms) + 2),
        out_specs=(vmem, vmem),
        compiler_params=pltpu.CompilerParams(vmem_limit_bytes=48 * 1024 * 1024),
        name="detect_strip",
    )(*terms, across, along)


def solution(mesh):
    in_specs = (
        P(("patch", "visit"), None, None),
        P(("patch", "visit"), None),
        P(("patch", "visit")),
        P(("patch", "visit")),
        P(("patch", "visit")),
        P(),
        P(),
        P(),
        P(),
    )
    out_specs = (P(("patch", "visit"), None), P(("patch", "visit"), None))
    return jax.shard_map(shards, mesh=mesh, in_specs=in_specs, out_specs=out_specs, check_vma=False)
```

```python
from functools import partial
import math

import jax
import jax.numpy as jnp
from jax import lax
from jax.experimental import pallas as pl
from jax.experimental.pallas import tpu as pltpu
from jax.sharding import PartitionSpec as P

PH = 256
F32 = jnp.float32
BF16 = jnp.bfloat16


def iota(shape, dim):
    return lax.broadcasted_iota(jnp.int32, shape, dim)


def dot(a, b):
    return jnp.dot(a, b, preferred_element_type=F32)


def dot_nt(a, b):
    return lax.dot_general(a, b, (((1,), (1,)), ((), ())), preferred_element_type=F32)


def dot_tn(a, b):
    return lax.dot_general(a, b, (((0,), (0,)), ((), ())), preferred_element_type=F32)


def toeplitz(taps, rows, lanes, shift):
    first = pltpu.roll(jnp.broadcast_to(taps, (8, lanes)), 0, 1, stride=1, stride_axis=0)
    blocks = [pltpu.roll(first, (i + shift) % lanes, 1) for i in range(0, rows, 8)]
    return jnp.concatenate(blocks, axis=0)


def masked_bands(table, rows, lanes, shift, mask):
    padded = jnp.concatenate(
        [table, jnp.zeros((table.shape[0], lanes - table.shape[1]), F32)], axis=1
    )
    for b in range(table.shape[0]):
        yield b, jnp.where(mask, toeplitz(padded[b:b + 1], rows, lanes, shift), 0.0)


def split(x):
    high = x.astype(BF16)
    return high, (x - high.astype(F32)).astype(BF16)


def coadd_kernel(
    geometry,
    col_h, row_h, dest_h, off_h, kind_h, weight_h, coef_h, taps_h, pieces_h,
    dest_s_h, off_s_h,
    kept, sent, across, along,
    col, row, dest_v, off_v, kind_v, weight_v, coef, det_taps, pieces, dest_s, off_s,
    col_bands, row_bands, factors, even, odd, acc_0, acc_1, den, sems,
):
    patches, strips, halo, stride, group, groups, halved = geometry
    count, height, width = pieces.shape
    basis, taps = col.shape
    half = taps // 2
    strip = PH // strips
    span = kept.shape[1]
    sources = (
        col_h, row_h, dest_h, off_h, kind_h, weight_h, coef_h, taps_h, pieces_h, dest_s_h,
        off_s_h,
    )
    targets = (
        col, row, dest_v, off_v, kind_v, weight_v, coef, det_taps, pieces, dest_s, off_s
    )
    copies = [
        pltpu.make_async_copy(source, target, sems.at[k])
        for k, (source, target) in enumerate(zip(sources, targets))
    ]
    for copy in copies:
        copy.start()
    acc_0[...] = jnp.zeros_like(acc_0)
    acc_1[...] = jnp.zeros_like(acc_1)
    for copy in copies[:2]:
        copy.wait()
    x, y = iota((width, width), 1), iota((width, width), 0)
    near = jnp.abs(x - y) <= half
    for b, band in masked_bands(col[...].astype(F32), width, width, -half, near):
        col_bands[b * width:(b + 1) * width, :] = band.astype(BF16)
    near = near & (x // height == y // height)
    for b, band in masked_bands(row[...].astype(F32), width, width, -half, near):
        row_bands[b * width:(b + 1) * width, :] = band.astype(BF16)
    for copy in copies[2:]:
        copy.wait()
    table, detect = det_taps[...].astype(F32), det_taps.shape[1]
    ((_, band),) = masked_bands(table[1:2], width, width, -halo, jnp.abs(x - y) <= halo)
    across[...] = band.astype(BF16)
    diff = iota((strip, width), 1) - iota((strip, width), 0)
    ((_, band),) = masked_bands(table[0:1], strip, width, 0, (diff >= 0) & (diff < detect))
    along[...] = band.astype(BF16)
    kinds = coef.shape[1]
    weight = weight_v[...].astype(F32)
    picked = jnp.where(iota((kinds, count), 0) == kind_v[...], weight, 0.0).astype(BF16)
    high, low = split(coef[...])
    high, low = split(dot(high, picked) + dot(low, picked))
    spread = (
        iota((basis, basis * width), 1) // width == iota((basis, basis * width), 0)
    ).astype(BF16)
    factors[...] = dot_tn(high, spread) + dot_tn(low, spread)
    share = jnp.where(iota((patches, count), 0) == dest_v[...], weight, 0.0).astype(BF16)
    for v in range(strips):
        at = iota((width, count), 0) + (v * strip - halo) - off_v[...]
        covered = ((at >= 0) & (at < height)).astype(BF16)
        den[v] = dot_nt(share, covered)

    chunk, together = groups * group, 2

    def row_step(i, scaled):
        base = pl.multiple_of(i * chunk, chunk)
        images = jnp.concatenate(
            [
                pieces[pl.ds(base + g * group, group)].reshape(width, width)
                for g in range(groups)
            ],
            axis=1,
        )
        for start in range(0, basis, together):
            stop = min(start + together, basis)
            rowed = dot(row_bands[start * width:stop * width, :], images)
            for b in range(start, stop):
                at = slice(b * width, (b + 1) * width)
                scale = factors[pl.ds(base, chunk), at]
                for g in range(groups):
                    for j in range(group):
                        top = (b - start) * width + j * height
                        part = rowed[top:top + height, g * width:(g + 1) * width]
                        part = part * scale[g * group + j:g * group + j + 1]
                        first = g * width + j * height
                        scaled[first:first + height, at] = part.astype(BF16)

    def column_step(i, scaled):
        base = i * chunk
        matched = dot(scaled[...], col_bands[...])
        for j in range(chunk):
            place = pl.ds(dest_s[base + j] * stride + halo + off_s[base + j], height)
            acc = (acc_0, acc_1)[j % 2]
            acc[place, :] = acc[place, :] + matched[j * height:(j + 1) * height]

    chunks = count // chunk
    row_step(0, even)

    def two(k, carry):
        row_step(2 * k + 1, odd)
        column_step(2 * k, even)
        row_step(2 * k + 2, even)
        column_step(2 * k + 1, odd)
        return carry

    lax.fori_loop(0, chunks // 2 - 1, two, 0)
    row_step(chunks - 1, odd)
    column_step(chunks - 2, even)
    column_step(chunks - 1, odd)
    own = iota((span, width), 0) < strip + 2 * halo
    me = lax.axis_index("patch") * strips + lax.axis_index("visit")
    parts = patches * strips

    def strip_at(position):
        away = 0
        for stage, mask in enumerate(halving_masks(halved)):
            away = away ^ (((position >> (halved + 3 - stage)) & 1) * mask)
        for k in range(2):
            away = away ^ direct_mask(halved, k, (position >> (2 - 2 * k)) & 3)
        device = away ^ me
        p, v = device // strips, lax.rem(device, strips)
        base = pl.multiple_of(p * stride + v * strip, 8)
        total = acc_0[pl.ds(base, span), :] + acc_1[pl.ds(base, span), :]
        return jnp.where(own, total, den[v, pl.ds(p, 1), :])

    def finish(i, carry):
        sent[i] = strip_at(i + parts // 2).astype(BF16)
        kept[i] = strip_at(i)
        return carry

    lax.fori_loop(0, parts // 2, finish, 0, unroll=4)


def detect_kernel(halo, *refs):
    *terms, across, along, coadd, detection = refs
    span, width = terms[0].shape
    strip = coadd.shape[0]
    total = terms[0][...]
    for term in terms[1:]:
        total = total + term[...].astype(F32)
    rows = iota((span, width), 0)
    square = jnp.broadcast_to(total[strip + 2 * halo:strip + 2 * halo + 1], (width, width))
    weight = jnp.transpose(square)[:span]
    value = jnp.where(rows < strip + 2 * halo, total / (1.0 + weight), 0.0)
    coadd[...] = value[halo:halo + strip]
    columns, filt = across[...], along[...]
    high, low = split(value)
    smooth = dot(high, columns) + dot(low, columns)
    smooth = jnp.concatenate([smooth, jnp.zeros((width - span, width), F32)], axis=0)
    high, low = split(smooth)
    detection[...] = dot(filt, high) + dot(filt, low)


def halving_masks(halved):
    return [1 << k | 1 for k in range(halved)]


def direct_mask(halved, k, member):
    return (member << (halved + 2 * k)) | ((member | (member >> 1)) & 1)


def exchange(x, mask):
    parts = lax.axis_size("patch") * lax.axis_size("visit")
    return lax.ppermute(x, ("patch", "visit"), [(d, d ^ mask) for d in range(parts)])


def exchange_direct(sums, mask, order):
    return [sums[0]] + [exchange(sums[k].astype(BF16), mask(k)) for k in order]


def shards(
    pieces, dest, offsets, kernel_index, weights, basis_col, basis_row, coef_table, det_taps
):
    patches = lax.axis_size("patch")
    strips = lax.axis_size("visit")
    count, height, width = pieces.shape
    basis = basis_col.shape[0]
    halo = det_taps.shape[1] // 2
    strip = PH // strips
    span = -(-(strip + 2 * halo + 1) // 8) * 8
    stride = strip * (strips - 1) + span
    group = width // height
    groups = 4
    parts = patches * strips
    vmem = pl.BlockSpec(memory_space=pltpu.VMEM)
    inputs = (
        basis_col, basis_row, dest.reshape(1, count), offsets.reshape(1, count),
        kernel_index.reshape(1, count), weights.reshape(1, count), coef_table.T, det_taps, pieces,
        dest[:, 0], offsets,
    )
    bits = parts.bit_length() - 1
    halved = bits - 4
    shape = (parts // 2, span, width)
    shapes = [jax.ShapeDtypeStruct(shape, F32), jax.ShapeDtypeStruct(shape, BF16)]
    shapes += [jax.ShapeDtypeStruct((rows, width), BF16) for rows in (width, strip)]
    grant = 10 * 1024 * 1024 + 3 * parts * span * width + 8 * patches * stride * width
    kept, sent, across, along = pl.pallas_call(
        partial(coadd_kernel, (patches, strips, halo, stride, group, groups, halved)),
        out_shape=shapes,
        in_specs=[pl.BlockSpec(memory_space=pltpu.HBM)] * len(inputs),
        out_specs=[vmem] * 4,
        scratch_shapes=[pltpu.VMEM(x.shape, x.dtype) for x in inputs[:-2]]
        + [pltpu.SMEM(x.shape, x.dtype) for x in inputs[-2:]]
        + [
            pltpu.VMEM((basis * width, width), BF16),
            pltpu.VMEM((basis * width, width), BF16),
            pltpu.VMEM((count, basis * width), F32),
            pltpu.VMEM((groups * width, basis * width), BF16),
            pltpu.VMEM((groups * width, basis * width), BF16),
            pltpu.VMEM((patches * stride, width), F32),
            pltpu.VMEM((patches * stride, width), F32),
            pltpu.VMEM((strips, patches, width), F32),
            pltpu.SemaphoreType.DMA((len(inputs),)),
        ],
        compiler_params=pltpu.CompilerParams(vmem_limit_bytes=grant),
        name="coadd_partials",
    )(*[pltpu.with_memory_space_constraint(x, pltpu.HBM) for x in inputs])
    def exchange(x, mask):
        return lax.ppermute(x, ("patch", "visit"), [(d, d ^ mask) for d in range(parts)])

    for stage, mask in enumerate(halving_masks(halved)):
        if stage:
            left = kept.shape[0] // 2
            sent = (kept[left:] + given[left:].astype(F32)).astype(BF16)
            kept = kept[:left] + given[:left].astype(F32)
        given = exchange(sent, mask)
    sums = [kept[4 * k:4 * k + 4] + given[4 * k:4 * k + 4].astype(F32) for k in range(4)]
    terms = exchange_direct(sums, partial(direct_mask, halved, 0), (1, 3, 2))
    total = terms[0]
    for term in terms[1:]:
        total = total + term.astype(F32)
    total = [total[k] for k in range(4)]
    terms = exchange_direct(total, partial(direct_mask, halved, 1), (2, 3, 1))
    shape = jax.ShapeDtypeStruct((strip, width), F32)
    return pl.pallas_call(
        partial(detect_kernel, halo),
        out_shape=(shape, shape),
        in_specs=[vmem] * (len(terms) + 2),
        out_specs=(vmem, vmem),
        compiler_params=pltpu.CompilerParams(vmem_limit_bytes=48 * 1024 * 1024),
        name="detect_strip",
    )(*terms, across, along)


def solution(mesh):
    in_specs = (
        P(("patch", "visit"), None, None),
        P(("patch", "visit"), None),
        P(("patch", "visit")),
        P(("patch", "visit")),
        P(("patch", "visit")),
        P(),
        P(),
        P(),
        P(),
    )
    out_specs = (P(("patch", "visit"), None), P(("patch", "visit"), None))
    return jax.shard_map(shards, mesh=mesh, in_specs=in_specs, out_specs=out_specs, check_vma=False)
```

```python
from functools import partial
import math

import jax
import jax.numpy as jnp
from jax import lax
from jax.experimental import pallas as pl
from jax.experimental.pallas import tpu as pltpu
from jax.sharding import PartitionSpec as P

PH = 256
F32 = jnp.float32
BF16 = jnp.bfloat16


def iota(shape, dim):
    return lax.broadcasted_iota(jnp.int32, shape, dim)


def dot(a, b):
    return jnp.dot(a, b, preferred_element_type=F32)


def dot_nt(a, b):
    return lax.dot_general(a, b, (((1,), (1,)), ((), ())), preferred_element_type=F32)


def dot_tn(a, b):
    return lax.dot_general(a, b, (((0,), (0,)), ((), ())), preferred_element_type=F32)


def toeplitz(taps, rows, lanes, shift):
    first = pltpu.roll(jnp.broadcast_to(taps, (8, lanes)), 0, 1, stride=1, stride_axis=0)
    blocks = [pltpu.roll(first, (i + shift) % lanes, 1) for i in range(0, rows, 8)]
    return jnp.concatenate(blocks, axis=0)


def masked_bands(table, rows, lanes, shift, mask):
    padded = jnp.concatenate(
        [table, jnp.zeros((table.shape[0], lanes - table.shape[1]), F32)], axis=1
    )
    for b in range(table.shape[0]):
        yield b, jnp.where(mask, toeplitz(padded[b:b + 1], rows, lanes, shift), 0.0)


def split(x):
    high = x.astype(BF16)
    return high, (x - high.astype(F32)).astype(BF16)


def coadd_kernel(
    geometry,
    col_h, row_h, dest_h, off_h, kind_h, weight_h, coef_h, taps_h, pieces_h,
    dest_s_h, off_s_h,
    kept, sent, across, along,
    col, row, dest_v, off_v, kind_v, weight_v, coef, det_taps, pieces, dest_s, off_s,
    col_bands, row_bands, factors, even, odd, acc, den, sems,
):
    patches, strips, halo, stride, group, groups, halved = geometry
    count, height, width = pieces.shape
    basis, taps = col.shape
    half = taps // 2
    strip = PH // strips
    span = kept.shape[1]
    sources = (
        col_h, row_h, dest_h, off_h, kind_h, weight_h, coef_h, taps_h, pieces_h, dest_s_h,
        off_s_h,
    )
    targets = (
        col, row, dest_v, off_v, kind_v, weight_v, coef, det_taps, pieces, dest_s, off_s
    )
    copies = [
        pltpu.make_async_copy(source, target, sems.at[k])
        for k, (source, target) in enumerate(zip(sources, targets))
    ]
    for copy in copies:
        copy.start()
    acc[...] = jnp.zeros_like(acc)
    for copy in copies[:2]:
        copy.wait()
    x, y = iota((width, width), 1), iota((width, width), 0)
    near = jnp.abs(x - y) <= half
    for b, band in masked_bands(col[...].astype(F32), width, width, -half, near):
        col_bands[b * width:(b + 1) * width, :] = band.astype(BF16)
    near = near & (x // height == y // height)
    for b, band in masked_bands(row[...].astype(F32), width, width, -half, near):
        row_bands[b * width:(b + 1) * width, :] = band.astype(BF16)
    for copy in copies[2:]:
        copy.wait()
    table, detect = det_taps[...].astype(F32), det_taps.shape[1]
    ((_, band),) = masked_bands(table[1:2], width, width, -halo, jnp.abs(x - y) <= halo)
    across[...] = band.astype(BF16)
    diff = iota((strip, width), 1) - iota((strip, width), 0)
    ((_, band),) = masked_bands(table[0:1], strip, width, 0, (diff >= 0) & (diff < detect))
    along[...] = band.astype(BF16)
    kinds = coef.shape[1]
    weight = weight_v[...].astype(F32)
    picked = jnp.where(iota((kinds, count), 0) == kind_v[...], weight, 0.0).astype(BF16)
    high, low = split(coef[...])
    high, low = split(dot(high, picked) + dot(low, picked))
    spread = (
        iota((basis, basis * width), 1) // width == iota((basis, basis * width), 0)
    ).astype(BF16)
    factors[...] = (dot_tn(high, spread) + dot_tn(low, spread)).reshape(factors.shape)
    share = jnp.where(iota((patches, count), 0) == dest_v[...], weight, 0.0).astype(BF16)
    for v in range(strips):
        at = iota((width, count), 0) + (v * strip - halo) - off_v[...]
        covered = ((at >= 0) & (at < height)).astype(BF16)
        den[v] = dot_nt(share, covered)

    chunk, together = groups * group, 7

    def row_step(i, scaled):
        base = pl.multiple_of(i * chunk, chunk)
        images = jnp.concatenate(
            [
                pieces[pl.ds(base + g * group, group)].reshape(width, width)
                for g in range(groups)
            ],
            axis=1,
        )
        for start in range(0, basis, together):
            stop = min(start + together, basis)
            rowed = dot(row_bands[start * width:stop * width, :], images)
            for b in range(start, stop):
                at = slice(b * width, (b + 1) * width)
                for g in range(groups):
                    for j in range(group):
                        top = (b - start) * width + j * height
                        part = rowed[top:top + height, g * width:(g + 1) * width]
                        row = g * group + j
                        part = part * factors[i, row:row + 1, at]
                        first = g * width + j * height
                        scaled[first:first + height, at] = part.astype(BF16)

    def column_step(i, scaled):
        base = i * chunk
        matched = dot(scaled[...], col_bands[...])
        for j in range(chunk):
            place = pl.ds(dest_s[base + j] * stride + halo + off_s[base + j], height)
            acc[place, :] = acc[place, :] + matched[j * height:(j + 1) * height]

    chunks = count // chunk
    row_step(0, even)

    def two(k, carry):
        row_step(2 * k + 1, odd)
        column_step(2 * k, even)
        row_step(2 * k + 2, even)
        column_step(2 * k + 1, odd)
        return carry

    lax.fori_loop(0, chunks // 2 - 1, two, 0)
    row_step(chunks - 1, odd)
    column_step(chunks - 2, even)
    column_step(chunks - 1, odd)
    own = iota((span, width), 0) < strip + 2 * halo
    me = lax.axis_index("patch") * strips + lax.axis_index("visit")
    parts = patches * strips

    def strip_at(position):
        away = 0
        for stage, mask in enumerate(halving_masks(halved)):
            away = away ^ (((position >> (halved + 3 - stage)) & 1) * mask)
        for k in range(2):
            away = away ^ direct_mask(halved, k, (position >> (2 - 2 * k)) & 3)
        device = away ^ me
        p, v = device // strips, lax.rem(device, strips)
        base = pl.multiple_of(p * stride + v * strip, 8)
        return jnp.where(own, acc[pl.ds(base, span), :], den[v, pl.ds(p, 1), :])

    def finish(i, carry):
        sent[i] = strip_at(i + parts // 2).astype(BF16)
        kept[i] = strip_at(i)
        return carry

    lax.fori_loop(0, parts // 2, finish, 0, unroll=4)


def detect_kernel(halo, *refs):
    *terms, across, along, coadd, detection = refs
    span, width = terms[0].shape
    strip = coadd.shape[0]
    total = terms[0][...]
    for term in terms[1:]:
        total = total + term[...].astype(F32)
    rows = iota((span, width), 0)
    square = jnp.broadcast_to(total[strip + 2 * halo:strip + 2 * halo + 1], (width, width))
    weight = jnp.transpose(square)[:span]
    value = jnp.where(rows < strip + 2 * halo, total / (1.0 + weight), 0.0)
    coadd[...] = value[halo:halo + strip]
    columns, filt = across[...], along[...]
    high, low = split(value)
    smooth = dot(high, columns) + dot(low, columns)
    smooth = jnp.concatenate([smooth, jnp.zeros((width - span, width), F32)], axis=0)
    high, low = split(smooth)
    detection[...] = dot(filt, high) + dot(filt, low)


def halving_masks(halved):
    return [1 << k | 1 for k in range(halved)]


def direct_mask(halved, k, member):
    return (member << (halved + 2 * k)) | ((member | (member >> 1)) & 1)


def exchange(x, mask):
    parts = lax.axis_size("patch") * lax.axis_size("visit")
    return lax.ppermute(x, ("patch", "visit"), [(d, d ^ mask) for d in range(parts)])


def exchange_direct(sums, mask, order):
    return [sums[0]] + [exchange(sums[k].astype(BF16), mask(k)) for k in order]


def shards(
    pieces, dest, offsets, kernel_index, weights, basis_col, basis_row, coef_table, det_taps
):
    patches = lax.axis_size("patch")
    strips = lax.axis_size("visit")
    count, height, width = pieces.shape
    basis = basis_col.shape[0]
    halo = det_taps.shape[1] // 2
    strip = PH // strips
    span = -(-(strip + 2 * halo + 1) // 8) * 8
    stride = strip * (strips - 1) + span
    group = width // height
    groups = 4
    parts = patches * strips
    vmem = pl.BlockSpec(memory_space=pltpu.VMEM)
    inputs = (
        basis_col, basis_row, dest.reshape(1, count), offsets.reshape(1, count),
        kernel_index.reshape(1, count), weights.reshape(1, count), coef_table.T, det_taps, pieces,
        dest[:, 0], offsets,
    )
    bits = parts.bit_length() - 1
    halved = bits - 4
    shape = (parts // 2, span, width)
    shapes = [jax.ShapeDtypeStruct(shape, F32), jax.ShapeDtypeStruct(shape, BF16)]
    shapes += [jax.ShapeDtypeStruct((rows, width), BF16) for rows in (width, strip)]
    grant = 10 * 1024 * 1024 + 3 * parts * span * width + 4 * patches * stride * width
    kept, sent, across, along = pl.pallas_call(
        partial(coadd_kernel, (patches, strips, halo, stride, group, groups, halved)),
        out_shape=shapes,
        in_specs=[pl.BlockSpec(memory_space=pltpu.HBM)] * len(inputs),
        out_specs=[vmem] * 4,
        scratch_shapes=[pltpu.VMEM(x.shape, x.dtype) for x in inputs[:-2]]
        + [pltpu.SMEM(x.shape, x.dtype) for x in inputs[-2:]]
        + [
            pltpu.VMEM((basis * width, width), BF16),
            pltpu.VMEM((basis * width, width), BF16),
            pltpu.VMEM((count // (groups * group), groups * group, basis * width), F32),
            pltpu.VMEM((groups * width, basis * width), BF16),
            pltpu.VMEM((groups * width, basis * width), BF16),
            pltpu.VMEM((patches * stride, width), F32),
            pltpu.VMEM((strips, patches, width), F32),
            pltpu.SemaphoreType.DMA((len(inputs),)),
        ],
        compiler_params=pltpu.CompilerParams(vmem_limit_bytes=grant),
        name="coadd_partials",
    )(*[pltpu.with_memory_space_constraint(x, pltpu.HBM) for x in inputs])
    def exchange(x, mask):
        return lax.ppermute(x, ("patch", "visit"), [(d, d ^ mask) for d in range(parts)])

    for stage, mask in enumerate(halving_masks(halved)):
        if stage:
            left = kept.shape[0] // 2
            sent = (kept[left:] + given[left:].astype(F32)).astype(BF16)
            kept = kept[:left] + given[:left].astype(F32)
        given = exchange(sent, mask)
    sums = [kept[4 * k:4 * k + 4] + given[4 * k:4 * k + 4].astype(F32) for k in range(4)]
    terms = exchange_direct(sums, partial(direct_mask, halved, 0), (1, 3, 2))
    total = terms[0]
    for term in terms[1:]:
        total = total + term.astype(F32)
    total = [total[k] for k in range(4)]
    terms = exchange_direct(total, partial(direct_mask, halved, 1), (2, 3, 1))
    shape = jax.ShapeDtypeStruct((strip, width), F32)
    return pl.pallas_call(
        partial(detect_kernel, halo),
        out_shape=(shape, shape),
        in_specs=[vmem] * (len(terms) + 2),
        out_specs=(vmem, vmem),
        compiler_params=pltpu.CompilerParams(vmem_limit_bytes=48 * 1024 * 1024),
        name="detect_strip",
    )(*terms, across, along)


def solution(mesh):
    in_specs = (
        P(("patch", "visit"), None, None),
        P(("patch", "visit"), None),
        P(("patch", "visit")),
        P(("patch", "visit")),
        P(("patch", "visit")),
        P(),
        P(),
        P(),
        P(),
    )
    out_specs = (P(("patch", "visit"), None), P(("patch", "visit"), None))
    return jax.shard_map(shards, mesh=mesh, in_specs=in_specs, out_specs=out_specs, check_vma=False)
```

```python
from functools import partial
import math

import jax
import jax.numpy as jnp
from jax import lax
from jax.experimental import pallas as pl
from jax.experimental.pallas import tpu as pltpu
from jax.sharding import PartitionSpec as P

PH = 256
F32 = jnp.float32
BF16 = jnp.bfloat16


def iota(shape, dim):
    return lax.broadcasted_iota(jnp.int32, shape, dim)


def dot(a, b):
    return jnp.dot(a, b, preferred_element_type=F32)


def dot_nt(a, b):
    return lax.dot_general(a, b, (((1,), (1,)), ((), ())), preferred_element_type=F32)


def dot_tn(a, b):
    return lax.dot_general(a, b, (((0,), (0,)), ((), ())), preferred_element_type=F32)


def toeplitz(taps, rows, lanes, shift):
    first = pltpu.roll(jnp.broadcast_to(taps, (8, lanes)), 0, 1, stride=1, stride_axis=0)
    blocks = [pltpu.roll(first, (i + shift) % lanes, 1) for i in range(0, rows, 8)]
    return jnp.concatenate(blocks, axis=0)


def masked_bands(table, rows, lanes, shift, mask):
    padded = jnp.concatenate(
        [table, jnp.zeros((table.shape[0], lanes - table.shape[1]), F32)], axis=1
    )
    for b in range(table.shape[0]):
        yield b, jnp.where(mask, toeplitz(padded[b:b + 1], rows, lanes, shift), 0.0)


def split(x):
    high = x.astype(BF16)
    return high, (x - high.astype(F32)).astype(BF16)


def coadd_kernel(
    geometry,
    col_h, row_h, dest_h, off_h, kind_h, weight_h, coef_h, taps_h, pieces_h,
    dest_s_h, off_s_h,
    kept, sent, across, along,
    col, row, dest_v, off_v, kind_v, weight_v, coef, det_taps, pieces, dest_s, off_s,
    col_bands, row_bands, factors, even, odd, acc, den, sems,
):
    patches, strips, halo, stride, group, groups, halved = geometry
    count, height, width = pieces.shape
    basis, taps = col.shape
    half = taps // 2
    strip = PH // strips
    span = kept.shape[1]
    sources = (
        col_h, row_h, dest_h, off_h, kind_h, weight_h, coef_h, taps_h, pieces_h, dest_s_h,
        off_s_h,
    )
    targets = (
        col, row, dest_v, off_v, kind_v, weight_v, coef, det_taps, pieces, dest_s, off_s
    )
    copies = [
        pltpu.make_async_copy(source, target, sems.at[k])
        for k, (source, target) in enumerate(zip(sources, targets))
    ]
    for copy in copies:
        copy.start()
    acc[...] = jnp.zeros_like(acc)
    for copy in copies:
        copy.wait()
    x, y = iota((width, width), 1), iota((width, width), 0)
    near = jnp.abs(x - y) <= half
    for b, band in masked_bands(col[...].astype(F32), width, width, -half, near):
        col_bands[b * width:(b + 1) * width, :] = band.astype(BF16)
    near = near & (x // height == y // height)
    for b, band in masked_bands(row[...].astype(F32), width, width, -half, near):
        row_bands[b * width:(b + 1) * width, :] = band.astype(BF16)
    table, detect = det_taps[...].astype(F32), det_taps.shape[1]
    ((_, band),) = masked_bands(table[1:2], width, width, -halo, jnp.abs(x - y) <= halo)
    across[...] = band.astype(BF16)
    diff = iota((strip, width), 1) - iota((strip, width), 0)
    ((_, band),) = masked_bands(table[0:1], strip, width, 0, (diff >= 0) & (diff < detect))
    along[...] = band.astype(BF16)
    kinds = coef.shape[1]
    weight = weight_v[...].astype(F32)
    picked = jnp.where(iota((kinds, count), 0) == kind_v[...], weight, 0.0).astype(BF16)
    high, low = split(coef[...])
    high, low = split(dot(high, picked) + dot(low, picked))
    spread = (
        iota((basis, basis * width), 1) // width == iota((basis, basis * width), 0)
    ).astype(BF16)
    factors[...] = (dot_tn(high, spread) + dot_tn(low, spread)).reshape(factors.shape)
    share = jnp.where(iota((patches, count), 0) == dest_v[...], weight, 0.0).astype(BF16)
    for v in range(strips):
        at = iota((width, count), 0) + (v * strip - halo) - off_v[...]
        covered = ((at >= 0) & (at < height)).astype(BF16)
        den[v] = dot_nt(share, covered)

    chunk, together = groups * group, 7

    def row_step(i, scaled):
        base = pl.multiple_of(i * chunk, chunk)
        images = jnp.concatenate(
            [
                pieces[pl.ds(base + g * group, group)].reshape(width, width)
                for g in range(groups)
            ],
            axis=1,
        )
        for start in range(0, basis, together):
            stop = min(start + together, basis)
            rowed = dot(row_bands[start * width:stop * width, :], images)
            for b in range(start, stop):
                at = slice(b * width, (b + 1) * width)
                for g in range(groups):
                    for j in range(group):
                        top = (b - start) * width + j * height
                        part = rowed[top:top + height, g * width:(g + 1) * width]
                        row = g * group + j
                        part = part * factors[i, row:row + 1, at]
                        first = g * width + j * height
                        scaled[first:first + height, at] = part.astype(BF16)

    def column_step(i, scaled):
        base = i * chunk
        matched = dot(scaled[...], col_bands[...])
        for j in range(chunk):
            place = pl.ds(dest_s[base + j] * stride + halo + off_s[base + j], height)
            acc[place, :] = acc[place, :] + matched[j * height:(j + 1) * height]

    chunks = count // chunk
    row_step(0, even)

    def two(k, carry):
        row_step(2 * k + 1, odd)
        column_step(2 * k, even)
        row_step(2 * k + 2, even)
        column_step(2 * k + 1, odd)
        return carry

    lax.fori_loop(0, chunks // 2 - 1, two, 0)
    row_step(chunks - 1, odd)
    column_step(chunks - 2, even)
    column_step(chunks - 1, odd)
    own = iota((span, width), 0) < strip + 2 * halo
    me = lax.axis_index("patch") * strips + lax.axis_index("visit")
    parts = patches * strips

    def strip_at(position):
        away = 0
        for stage, mask in enumerate(halving_masks(halved)):
            away = away ^ (((position >> (halved + 3 - stage)) & 1) * mask)
        away = away ^ direct_mask(halved, 0, position >> 2 & 3)
        away = away ^ direct_mask(halved, 1, position & 3 ^ me >> (halved + 2))
        device = away ^ me
        p, v = device // strips, lax.rem(device, strips)
        base = pl.multiple_of(p * stride + v * strip, 8)
        return jnp.where(own, acc[pl.ds(base, span), :], den[v, pl.ds(p, 1), :])

    def finish(i, carry):
        sent[i] = strip_at(i + parts // 2).astype(BF16)
        kept[i] = strip_at(i)
        return carry

    lax.fori_loop(0, parts // 2, finish, 0, unroll=4)


def detect_kernel(halo, terms, across, along, coadd, detection):
    span, width = terms.shape[1:]
    strip = coadd.shape[0]
    total = jnp.sum(terms[...].astype(F32), axis=0)
    rows = iota((span, width), 0)
    square = jnp.broadcast_to(total[strip + 2 * halo:strip + 2 * halo + 1], (width, width))
    weight = jnp.transpose(square)[:span]
    value = jnp.where(rows < strip + 2 * halo, total / (1.0 + weight), 0.0)
    coadd[...] = value[halo:halo + strip]
    columns, filt = across[...], along[...]
    high, low = split(value)
    smooth = dot(high, columns) + dot(low, columns)
    smooth = jnp.concatenate([smooth, jnp.zeros((width - span, width), F32)], axis=0)
    high, low = split(smooth)
    detection[...] = dot(filt, high) + dot(filt, low)


def halving_masks(halved):
    return [1 << k | 1 for k in range(halved)]


def direct_mask(halved, k, member):
    return (member << (halved + 2 * k)) | ((member ^ (member >> 1)) & 1)


def exchange(x, mask):
    parts = lax.axis_size("patch") * lax.axis_size("visit")
    return lax.ppermute(x, ("patch", "visit"), [(d, d ^ mask) for d in range(parts)])


def exchange_direct(sums, mask, order):
    return [sums[0]] + [exchange(sums[k].astype(BF16), mask(k)) for k in order]


def shards(
    pieces, dest, offsets, kernel_index, weights, basis_col, basis_row, coef_table, det_taps
):
    patches = lax.axis_size("patch")
    strips = lax.axis_size("visit")
    count, height, width = pieces.shape
    basis = basis_col.shape[0]
    halo = det_taps.shape[1] // 2
    strip = PH // strips
    span = -(-(strip + 2 * halo + 1) // 8) * 8
    stride = strip * (strips - 1) + span
    group = width // height
    groups = 4
    parts = patches * strips
    vmem = pl.BlockSpec(memory_space=pltpu.VMEM)
    inputs = (
        basis_col, basis_row, dest.reshape(1, count), offsets.reshape(1, count),
        kernel_index.reshape(1, count), weights.reshape(1, count), coef_table.T, det_taps, pieces,
        dest[:, 0], offsets,
    )
    bits = parts.bit_length() - 1
    halved = bits - 4
    shape = (parts // 2, span, width)
    shapes = [jax.ShapeDtypeStruct(shape, F32), jax.ShapeDtypeStruct(shape, BF16)]
    shapes += [jax.ShapeDtypeStruct((rows, width), BF16) for rows in (width, strip)]
    grant = 10 * 1024 * 1024 + 3 * parts * span * width + 4 * patches * stride * width
    kept, sent, across, along = pl.pallas_call(
        partial(coadd_kernel, (patches, strips, halo, stride, group, groups, halved)),
        out_shape=shapes,
        in_specs=[pl.BlockSpec(memory_space=pltpu.HBM)] * len(inputs),
        out_specs=[vmem] * 4,
        scratch_shapes=[pltpu.VMEM(x.shape, x.dtype) for x in inputs[:-2]]
        + [pltpu.SMEM(x.shape, x.dtype) for x in inputs[-2:]]
        + [
            pltpu.VMEM((basis * width, width), BF16),
            pltpu.VMEM((basis * width, width), BF16),
            pltpu.VMEM((count // (groups * group), groups * group, basis * width), F32),
            pltpu.VMEM((groups * width, basis * width), BF16),
            pltpu.VMEM((groups * width, basis * width), BF16),
            pltpu.VMEM((patches * stride, width), F32),
            pltpu.VMEM((strips, patches, width), F32),
            pltpu.SemaphoreType.DMA((len(inputs),)),
        ],
        compiler_params=pltpu.CompilerParams(vmem_limit_bytes=grant),
        name="coadd_partials",
    )(*[pltpu.with_memory_space_constraint(x, pltpu.HBM) for x in inputs])
    def exchange(x, mask):
        return lax.ppermute(x, ("patch", "visit"), [(d, d ^ mask) for d in range(parts)])

    for stage, mask in enumerate(halving_masks(halved)):
        if stage:
            left = kept.shape[0] // 2
            sent = (kept[left:] + given[left:].astype(F32)).astype(BF16)
            kept = kept[:left] + given[:left].astype(F32)
        given = exchange(sent, mask)
    sums = [kept[4 * k:4 * k + 4] + given[4 * k:4 * k + 4].astype(F32) for k in range(4)]
    terms = exchange_direct(sums, partial(direct_mask, halved, 0), (1, 3, 2))
    total = terms[0]
    for term in terms[1:]:
        total = total + term.astype(F32)
    quarter = parts // 4
    final = lax.all_to_all(
        total.astype(BF16), ("patch", "visit"), split_axis=0, concat_axis=0, tiled=True,
        axis_index_groups=[
            [d ^ direct_mask(halved, 1, k) for k in range(4)] for d in range(quarter)
        ],
    )
    shape = jax.ShapeDtypeStruct((strip, width), F32)
    return pl.pallas_call(
        partial(detect_kernel, halo),
        out_shape=(shape, shape),
        in_specs=[vmem] * 3,
        out_specs=(vmem, vmem),
        compiler_params=pltpu.CompilerParams(vmem_limit_bytes=48 * 1024 * 1024),
        name="detect_strip",
    )(final, across, along)


def solution(mesh):
    in_specs = (
        P(("patch", "visit"), None, None),
        P(("patch", "visit"), None),
        P(("patch", "visit")),
        P(("patch", "visit")),
        P(("patch", "visit")),
        P(),
        P(),
        P(),
        P(),
    )
    out_specs = (P(("patch", "visit"), None), P(("patch", "visit"), None))
    return jax.shard_map(shards, mesh=mesh, in_specs=in_specs, out_specs=out_specs, check_vma=False)
```

```python
from functools import partial
import math

import jax
import jax.numpy as jnp
from jax import lax
from jax.experimental import pallas as pl
from jax.experimental.pallas import tpu as pltpu
from jax.sharding import PartitionSpec as P

PH = 256
F32 = jnp.float32
BF16 = jnp.bfloat16


def iota(shape, dim):
    return lax.broadcasted_iota(jnp.int32, shape, dim)


def dot(a, b):
    return jnp.dot(a, b, preferred_element_type=F32)


def dot_nt(a, b):
    return lax.dot_general(a, b, (((1,), (1,)), ((), ())), preferred_element_type=F32)


def dot_tn(a, b):
    return lax.dot_general(a, b, (((0,), (0,)), ((), ())), preferred_element_type=F32)


def toeplitz(taps, rows, lanes, shift):
    first = pltpu.roll(jnp.broadcast_to(taps, (8, lanes)), 0, 1, stride=1, stride_axis=0)
    blocks = [pltpu.roll(first, (i + shift) % lanes, 1) for i in range(0, rows, 8)]
    return jnp.concatenate(blocks, axis=0)


def masked_bands(table, rows, lanes, shift, mask):
    padded = jnp.concatenate(
        [table, jnp.zeros((table.shape[0], lanes - table.shape[1]), F32)], axis=1
    )
    for b in range(table.shape[0]):
        yield b, jnp.where(mask, toeplitz(padded[b:b + 1], rows, lanes, shift), 0.0)


def split(x):
    high = x.astype(BF16)
    return high, (x - high.astype(F32)).astype(BF16)


def coadd_kernel(
    geometry,
    col_h, row_h, dest_h, off_h, kind_h, weight_h, coef_h, taps_h, pieces_h,
    dest_s_h, off_s_h,
    kept, sent, across, along,
    col, row, dest_v, off_v, kind_v, weight_v, coef, det_taps, pieces, dest_s, off_s,
    col_bands, row_bands, factors, even, odd, acc, den, sems,
):
    patches, strips, halo, stride, group, groups, halved = geometry
    count, height, width = pieces.shape
    basis, taps = col.shape
    half = taps // 2
    strip = PH // strips
    span = kept.shape[1]
    sources = (
        col_h, row_h, dest_h, off_h, kind_h, weight_h, coef_h, taps_h, pieces_h, dest_s_h,
        off_s_h,
    )
    targets = (
        col, row, dest_v, off_v, kind_v, weight_v, coef, det_taps, pieces, dest_s, off_s
    )
    copies = [
        pltpu.make_async_copy(source, target, sems.at[k])
        for k, (source, target) in enumerate(zip(sources, targets))
    ]
    for copy in copies:
        copy.start()
    acc[...] = jnp.zeros_like(acc)
    for copy in copies[:2]:
        copy.wait()
    x, y = iota((width, width), 1), iota((width, width), 0)
    near = jnp.abs(x - y) <= half
    for b, band in masked_bands(col[...].astype(F32), width, width, -half, near):
        col_bands[b * width:(b + 1) * width, :] = band.astype(BF16)
    near = near & (x // height == y // height)
    for b, band in masked_bands(row[...].astype(F32), width, width, -half, near):
        row_bands[b * width:(b + 1) * width, :] = band.astype(BF16)
    for copy in copies[2:]:
        copy.wait()
    table, detect = det_taps[...].astype(F32), det_taps.shape[1]
    ((_, band),) = masked_bands(table[1:2], width, width, -halo, jnp.abs(x - y) <= halo)
    across[...] = band.astype(BF16)
    diff = iota((strip, width), 1) - iota((strip, width), 0)
    ((_, band),) = masked_bands(table[0:1], strip, width, 0, (diff >= 0) & (diff < detect))
    along[...] = band.astype(BF16)
    kinds = coef.shape[1]
    weight = weight_v[...].astype(F32)
    picked = jnp.where(iota((kinds, count), 0) == kind_v[...], weight, 0.0).astype(BF16)
    high, low = split(coef[...])
    high, low = split(dot(high, picked) + dot(low, picked))
    spread = (
        iota((basis, basis * width), 1) // width == iota((basis, basis * width), 0)
    ).astype(BF16)
    factors[...] = (dot_tn(high, spread) + dot_tn(low, spread)).reshape(factors.shape)
    share = jnp.where(iota((patches, count), 0) == dest_v[...], weight, 0.0).astype(BF16)
    for v in range(strips):
        at = iota((width, count), 0) + (v * strip - halo) - off_v[...]
        covered = ((at >= 0) & (at < height)).astype(BF16)
        den[v] = dot_nt(share, covered)

    chunk, together = groups * group, 7

    def row_step(i, scaled):
        base = pl.multiple_of(i * chunk, chunk)
        images = jnp.concatenate(
            [
                pieces[pl.ds(base + g * group, group)].reshape(width, width)
                for g in range(groups)
            ],
            axis=1,
        )
        for start in range(0, basis, together):
            stop = min(start + together, basis)
            rowed = dot(row_bands[start * width:stop * width, :], images)
            for b in range(start, stop):
                at = slice(b * width, (b + 1) * width)
                for g in range(groups):
                    for j in range(group):
                        top = (b - start) * width + j * height
                        part = rowed[top:top + height, g * width:(g + 1) * width]
                        row = g * group + j
                        part = part * factors[i, row:row + 1, at]
                        first = g * width + j * height
                        scaled[first:first + height, at] = part.astype(BF16)

    def column_step(i, scaled):
        base = i * chunk
        matched = dot(scaled[...], col_bands[...])
        for j in range(chunk):
            place = pl.ds(dest_s[base + j] * stride + halo + off_s[base + j], height)
            acc[place, :] = acc[place, :] + matched[j * height:(j + 1) * height]

    chunks = count // chunk
    row_step(0, even)

    def two(k, carry):
        row_step(2 * k + 1, odd)
        column_step(2 * k, even)
        row_step(2 * k + 2, even)
        column_step(2 * k + 1, odd)
        return carry

    lax.fori_loop(0, chunks // 2 - 1, two, 0)
    row_step(chunks - 1, odd)
    column_step(chunks - 2, even)
    column_step(chunks - 1, odd)
    own = iota((span, width), 0) < strip + 2 * halo
    me = lax.axis_index("patch") * strips + lax.axis_index("visit")
    parts = patches * strips

    def strip_at(position):
        away = 0
        for stage, mask in enumerate(halving_masks(halved)):
            away = away ^ (((position >> (halved + 3 - stage)) & 1) * mask)
        for k in range(2):
            away = away ^ direct_mask(halved, k, (position >> (2 - 2 * k)) & 3)
        device = away ^ me
        p, v = device // strips, lax.rem(device, strips)
        base = pl.multiple_of(p * stride + v * strip, 8)
        return jnp.where(own, acc[pl.ds(base, span), :], den[v, pl.ds(p, 1), :])

    def finish(i, carry):
        sent[i] = strip_at(i + parts // 2).astype(BF16)
        kept[i] = strip_at(i)
        return carry

    lax.fori_loop(0, parts // 2, finish, 0, unroll=4)


def detect_kernel(halo, *refs):
    *terms, across, along, coadd, detection = refs
    span, width = terms[0].shape
    strip = coadd.shape[0]
    total = terms[0][...]
    for term in terms[1:]:
        total = total + term[...].astype(F32)
    rows = iota((span, width), 0)
    square = jnp.broadcast_to(total[strip + 2 * halo:strip + 2 * halo + 1], (width, width))
    weight = jnp.transpose(square)[:span]
    value = jnp.where(rows < strip + 2 * halo, total / (1.0 + weight), 0.0)
    coadd[...] = value[halo:halo + strip]
    columns, filt = across[...], along[...]
    high, low = split(value)
    smooth = dot(high, columns) + dot(low, columns)
    smooth = jnp.concatenate([smooth, jnp.zeros((width - span, width), F32)], axis=0)
    high, low = split(smooth)
    detection[...] = dot(filt, high) + dot(filt, low)


def halving_masks(halved):
    return [1 << k | 1 for k in range(halved)]


def direct_mask(halved, k, member):
    return (member << (halved + 2 * k)) | ((member | (member >> 1)) & 1)


def exchange(x, mask):
    parts = lax.axis_size("patch") * lax.axis_size("visit")
    return lax.ppermute(x, ("patch", "visit"), [(d, d ^ mask) for d in range(parts)])


def exchange_direct(sums, mask, order):
    return [sums[0]] + [exchange(sums[k].astype(BF16), mask(k)) for k in order]


def shards(
    pieces, dest, offsets, kernel_index, weights, basis_col, basis_row, coef_table, det_taps
):
    patches = lax.axis_size("patch")
    strips = lax.axis_size("visit")
    count, height, width = pieces.shape
    basis = basis_col.shape[0]
    halo = det_taps.shape[1] // 2
    strip = PH // strips
    span = -(-(strip + 2 * halo + 1) // 8) * 8
    stride = strip * (strips - 1) + span
    group = width // height
    groups = 6
    parts = patches * strips
    vmem = pl.BlockSpec(memory_space=pltpu.VMEM)
    inputs = (
        basis_col, basis_row, dest.reshape(1, count), offsets.reshape(1, count),
        kernel_index.reshape(1, count), weights.reshape(1, count), coef_table.T, det_taps, pieces,
        dest[:, 0], offsets,
    )
    bits = parts.bit_length() - 1
    halved = bits - 4
    shape = (parts // 2, span, width)
    shapes = [jax.ShapeDtypeStruct(shape, F32), jax.ShapeDtypeStruct(shape, BF16)]
    shapes += [jax.ShapeDtypeStruct((rows, width), BF16) for rows in (width, strip)]
    grant = 12 * 1024 * 1024 + 3 * parts * span * width + 4 * patches * stride * width
    kept, sent, across, along = pl.pallas_call(
        partial(coadd_kernel, (patches, strips, halo, stride, group, groups, halved)),
        out_shape=shapes,
        in_specs=[pl.BlockSpec(memory_space=pltpu.HBM)] * len(inputs),
        out_specs=[vmem] * 4,
        scratch_shapes=[pltpu.VMEM(x.shape, x.dtype) for x in inputs[:-2]]
        + [pltpu.SMEM(x.shape, x.dtype) for x in inputs[-2:]]
        + [
            pltpu.VMEM((basis * width, width), BF16),
            pltpu.VMEM((basis * width, width), BF16),
            pltpu.VMEM((count // (groups * group), groups * group, basis * width), F32),
            pltpu.VMEM((groups * width, basis * width), BF16),
            pltpu.VMEM((groups * width, basis * width), BF16),
            pltpu.VMEM((patches * stride, width), F32),
            pltpu.VMEM((strips, patches, width), F32),
            pltpu.SemaphoreType.DMA((len(inputs),)),
        ],
        compiler_params=pltpu.CompilerParams(vmem_limit_bytes=grant),
        name="coadd_partials",
    )(*[pltpu.with_memory_space_constraint(x, pltpu.HBM) for x in inputs])
    def exchange(x, mask):
        return lax.ppermute(x, ("patch", "visit"), [(d, d ^ mask) for d in range(parts)])

    for stage, mask in enumerate(halving_masks(halved)):
        if stage:
            left = kept.shape[0] // 2
            sent = (kept[left:] + given[left:].astype(F32)).astype(BF16)
            kept = kept[:left] + given[:left].astype(F32)
        given = exchange(sent, mask)
    sums = [kept[4 * k:4 * k + 4] + given[4 * k:4 * k + 4].astype(F32) for k in range(4)]
    terms = exchange_direct(sums, partial(direct_mask, halved, 0), (1, 3, 2))
    total = terms[0]
    for term in terms[1:]:
        total = total + term.astype(F32)
    total = [total[k] for k in range(4)]
    terms = exchange_direct(total, partial(direct_mask, halved, 1), (2, 3, 1))
    shape = jax.ShapeDtypeStruct((strip, width), F32)
    return pl.pallas_call(
        partial(detect_kernel, halo),
        out_shape=(shape, shape),
        in_specs=[vmem] * (len(terms) + 2),
        out_specs=(vmem, vmem),
        compiler_params=pltpu.CompilerParams(vmem_limit_bytes=48 * 1024 * 1024),
        name="detect_strip",
    )(*terms, across, along)


def solution(mesh):
    in_specs = (
        P(("patch", "visit"), None, None),
        P(("patch", "visit"), None),
        P(("patch", "visit")),
        P(("patch", "visit")),
        P(("patch", "visit")),
        P(),
        P(),
        P(),
        P(),
    )
    out_specs = (P(("patch", "visit"), None), P(("patch", "visit"), None))
    return jax.shard_map(shards, mesh=mesh, in_specs=in_specs, out_specs=out_specs, check_vma=False)
```

```python
from functools import partial
import math

import jax
import jax.numpy as jnp
from jax import lax
from jax.experimental import pallas as pl
from jax.experimental.pallas import tpu as pltpu
from jax.sharding import PartitionSpec as P

PH = 256
F32 = jnp.float32
BF16 = jnp.bfloat16


def iota(shape, dim):
    return lax.broadcasted_iota(jnp.int32, shape, dim)


def dot(a, b):
    return jnp.dot(a, b, preferred_element_type=F32)


def dot_nt(a, b):
    return lax.dot_general(a, b, (((1,), (1,)), ((), ())), preferred_element_type=F32)


def dot_tn(a, b):
    return lax.dot_general(a, b, (((0,), (0,)), ((), ())), preferred_element_type=F32)


def toeplitz(taps, rows, lanes, shift):
    first = pltpu.roll(jnp.broadcast_to(taps, (8, lanes)), 0, 1, stride=1, stride_axis=0)
    blocks = [pltpu.roll(first, (i + shift) % lanes, 1) for i in range(0, rows, 8)]
    return jnp.concatenate(blocks, axis=0)


def masked_bands(table, rows, lanes, shift, mask):
    padded = jnp.concatenate(
        [table, jnp.zeros((table.shape[0], lanes - table.shape[1]), F32)], axis=1
    )
    for b in range(table.shape[0]):
        yield b, jnp.where(mask, toeplitz(padded[b:b + 1], rows, lanes, shift), 0.0)


def split(x):
    high = x.astype(BF16)
    return high, (x - high.astype(F32)).astype(BF16)


def coadd_kernel(
    geometry,
    col_h, row_h, dest_h, off_h, kind_h, weight_h, coef_h, taps_h, pieces_h,
    dest_s_h, off_s_h,
    kept, sent, across, along,
    col, row, dest_v, off_v, kind_v, weight_v, coef, det_taps, pieces, dest_s, off_s,
    col_bands, row_bands, factors, even, odd, acc, den, sems,
):
    patches, strips, halo, stride, group, groups, halved = geometry
    count, height, width = pieces.shape
    basis, taps = col.shape
    half = taps // 2
    strip = PH // strips
    span = kept.shape[1]
    sources = (
        col_h, row_h, dest_h, off_h, kind_h, weight_h, coef_h, taps_h, pieces_h, dest_s_h,
        off_s_h,
    )
    targets = (
        col, row, dest_v, off_v, kind_v, weight_v, coef, det_taps, pieces, dest_s, off_s
    )
    copies = [
        pltpu.make_async_copy(source, target, sems.at[k])
        for k, (source, target) in enumerate(zip(sources, targets))
    ]
    for copy in copies:
        copy.start()
    acc[...] = jnp.zeros_like(acc)
    for copy in copies[:2]:
        copy.wait()
    x, y = iota((width, width), 1), iota((width, width), 0)
    near = jnp.abs(x - y) <= half
    for b, band in masked_bands(col[...].astype(F32), width, width, -half, near):
        col_bands[b * width:(b + 1) * width, :] = band.astype(BF16)
    near = near & (x // height == y // height)
    for b, band in masked_bands(row[...].astype(F32), width, width, -half, near):
        row_bands[b * width:(b + 1) * width, :] = band.astype(BF16)
    for copy in copies[2:]:
        copy.wait()
    table, detect = det_taps[...].astype(F32), det_taps.shape[1]
    ((_, band),) = masked_bands(table[1:2], width, width, -halo, jnp.abs(x - y) <= halo)
    across[...] = band.astype(BF16)
    diff = iota((strip, width), 1) - iota((strip, width), 0)
    ((_, band),) = masked_bands(table[0:1], strip, width, 0, (diff >= 0) & (diff < detect))
    along[...] = band.astype(BF16)
    kinds = coef.shape[1]
    weight = weight_v[...].astype(F32)
    picked = jnp.where(iota((kinds, count), 0) == kind_v[...], weight, 0.0).astype(BF16)
    high, low = split(coef[...])
    high, low = split(dot(high, picked) + dot(low, picked))
    spread = (
        iota((basis, basis * width), 1) // width == iota((basis, basis * width), 0)
    ).astype(BF16)
    factors[...] = (dot_tn(high, spread) + dot_tn(low, spread)).reshape(factors.shape)
    share = jnp.where(iota((patches, count), 0) == dest_v[...], weight, 0.0).astype(BF16)
    for v in range(strips):
        at = iota((width, count), 0) + (v * strip - halo) - off_v[...]
        covered = ((at >= 0) & (at < height)).astype(BF16)
        den[v] = dot_nt(share, covered)

    chunk, together = groups * group, 2

    def row_step(i, scaled):
        base = pl.multiple_of(i * chunk, chunk)
        images = jnp.concatenate(
            [
                pieces[pl.ds(base + g * group, group)].reshape(width, width)
                for g in range(groups)
            ],
            axis=1,
        )
        for start in range(0, basis, together):
            stop = min(start + together, basis)
            rowed = dot(row_bands[start * width:stop * width, :], images)
            for b in range(start, stop):
                at = slice(b * width, (b + 1) * width)
                for g in range(groups):
                    for j in range(group):
                        top = (b - start) * width + j * height
                        part = rowed[top:top + height, g * width:(g + 1) * width]
                        row = g * group + j
                        part = part * factors[i, row:row + 1, at]
                        first = g * width + j * height
                        scaled[first:first + height, at] = part.astype(BF16)

    def column_step(i, scaled):
        base = i * chunk
        matched = dot(scaled[...], col_bands[...])
        for j in range(chunk):
            place = pl.ds(dest_s[base + j] * stride + halo + off_s[base + j], height)
            acc[place, :] = acc[place, :] + matched[j * height:(j + 1) * height]

    chunks = count // chunk
    row_step(0, even)

    def two(k, carry):
        row_step(2 * k + 1, odd)
        column_step(2 * k, even)
        row_step(2 * k + 2, even)
        column_step(2 * k + 1, odd)
        return carry

    if chunks > 2:
        lax.fori_loop(0, chunks // 2 - 1, two, 0)
    row_step(chunks - 1, odd)
    column_step(chunks - 2, even)
    column_step(chunks - 1, odd)
    own = iota((span, width), 0) < strip + 2 * halo
    me = lax.axis_index("patch") * strips + lax.axis_index("visit")
    parts = patches * strips

    def strip_at(position):
        away = 0
        for stage, mask in enumerate(halving_masks(halved)):
            away = away ^ (((position >> (halved + 3 - stage)) & 1) * mask)
        for k in range(2):
            away = away ^ direct_mask(halved, k, (position >> (2 - 2 * k)) & 3)
        device = away ^ me
        p, v = device // strips, lax.rem(device, strips)
        base = pl.multiple_of(p * stride + v * strip, 8)
        return jnp.where(own, acc[pl.ds(base, span), :], den[v, pl.ds(p, 1), :])

    def finish(i, carry):
        sent[i] = strip_at(i + parts // 2).astype(BF16)
        kept[i] = strip_at(i)
        return carry

    if parts <= 32:
        for i in range(parts // 2):
            finish(i, 0)
    else:
        lax.fori_loop(0, parts // 2, finish, 0, unroll=4)


def detect_kernel(halo, *refs):
    *terms, across, along, coadd, detection = refs
    span, width = terms[0].shape
    strip = coadd.shape[0]
    total = terms[0][...]
    for term in terms[1:]:
        total = total + term[...].astype(F32)
    rows = iota((span, width), 0)
    square = jnp.broadcast_to(total[strip + 2 * halo:strip + 2 * halo + 1], (width, width))
    weight = jnp.transpose(square)[:span]
    value = jnp.where(rows < strip + 2 * halo, total / (1.0 + weight), 0.0)
    coadd[...] = value[halo:halo + strip]
    columns, filt = across[...], along[...]
    high, low = split(value)
    smooth = dot(high, columns) + dot(low, columns)
    smooth = jnp.concatenate([smooth, jnp.zeros((width - span, width), F32)], axis=0)
    high, low = split(smooth)
    detection[...] = dot(filt, high) + dot(filt, low)


def halving_masks(halved):
    return [1 << k | 1 for k in range(halved)]


def direct_mask(halved, k, member):
    return (member << (halved + 2 * k)) | ((member | (member >> 1)) & 1)


def exchange(x, mask):
    parts = lax.axis_size("patch") * lax.axis_size("visit")
    return lax.ppermute(x, ("patch", "visit"), [(d, d ^ mask) for d in range(parts)])


def exchange_direct(sums, mask, order):
    return [sums[0]] + [exchange(sums[k].astype(BF16), mask(k)) for k in order]


def shards(
    pieces, dest, offsets, kernel_index, weights, basis_col, basis_row, coef_table, det_taps
):
    patches = lax.axis_size("patch")
    strips = lax.axis_size("visit")
    count, height, width = pieces.shape
    basis = basis_col.shape[0]
    halo = det_taps.shape[1] // 2
    strip = PH // strips
    span = -(-(strip + 2 * halo + 1) // 8) * 8
    stride = strip * (strips - 1) + span
    group = width // height
    groups = 12
    parts = patches * strips
    vmem = pl.BlockSpec(memory_space=pltpu.VMEM)
    inputs = (
        basis_col, basis_row, dest.reshape(1, count), offsets.reshape(1, count),
        kernel_index.reshape(1, count), weights.reshape(1, count), coef_table.T, det_taps, pieces,
        dest[:, 0], offsets,
    )
    bits = parts.bit_length() - 1
    halved = bits - 4
    shape = (parts // 2, span, width)
    shapes = [jax.ShapeDtypeStruct(shape, F32), jax.ShapeDtypeStruct(shape, BF16)]
    shapes += [jax.ShapeDtypeStruct((rows, width), BF16) for rows in (width, strip)]
    grant = 24 * 1024 * 1024 + 3 * parts * span * width + 4 * patches * stride * width
    kept, sent, across, along = pl.pallas_call(
        partial(coadd_kernel, (patches, strips, halo, stride, group, groups, halved)),
        out_shape=shapes,
        in_specs=[pl.BlockSpec(memory_space=pltpu.HBM)] * len(inputs),
        out_specs=[vmem] * 4,
        scratch_shapes=[pltpu.VMEM(x.shape, x.dtype) for x in inputs[:-2]]
        + [pltpu.SMEM(x.shape, x.dtype) for x in inputs[-2:]]
        + [
            pltpu.VMEM((basis * width, width), BF16),
            pltpu.VMEM((basis * width, width), BF16),
            pltpu.VMEM((count // (groups * group), groups * group, basis * width), F32),
            pltpu.VMEM((groups * width, basis * width), BF16),
            pltpu.VMEM((groups * width, basis * width), BF16),
            pltpu.VMEM((patches * stride, width), F32),
            pltpu.VMEM((strips, patches, width), F32),
            pltpu.SemaphoreType.DMA((len(inputs),)),
        ],
        compiler_params=pltpu.CompilerParams(vmem_limit_bytes=grant),
        name="coadd_partials",
    )(*[pltpu.with_memory_space_constraint(x, pltpu.HBM) for x in inputs])
    def exchange(x, mask):
        return lax.ppermute(x, ("patch", "visit"), [(d, d ^ mask) for d in range(parts)])

    for stage, mask in enumerate(halving_masks(halved)):
        if stage:
            left = kept.shape[0] // 2
            sent = (kept[left:] + given[left:].astype(F32)).astype(BF16)
            kept = kept[:left] + given[:left].astype(F32)
        given = exchange(sent, mask)
    sums = [kept[4 * k:4 * k + 4] + given[4 * k:4 * k + 4].astype(F32) for k in range(4)]
    terms = exchange_direct(sums, partial(direct_mask, halved, 0), (1, 3, 2))
    total = terms[0]
    for term in terms[1:]:
        total = total + term.astype(F32)
    total = [total[k] for k in range(4)]
    terms = exchange_direct(total, partial(direct_mask, halved, 1), (2, 3, 1))
    shape = jax.ShapeDtypeStruct((strip, width), F32)
    return pl.pallas_call(
        partial(detect_kernel, halo),
        out_shape=(shape, shape),
        in_specs=[vmem] * (len(terms) + 2),
        out_specs=(vmem, vmem),
        compiler_params=pltpu.CompilerParams(vmem_limit_bytes=48 * 1024 * 1024),
        name="detect_strip",
    )(*terms, across, along)


def solution(mesh):
    in_specs = (
        P(("patch", "visit"), None, None),
        P(("patch", "visit"), None),
        P(("patch", "visit")),
        P(("patch", "visit")),
        P(("patch", "visit")),
        P(),
        P(),
        P(),
        P(),
    )
    out_specs = (P(("patch", "visit"), None), P(("patch", "visit"), None))
    return jax.shard_map(shards, mesh=mesh, in_specs=in_specs, out_specs=out_specs, check_vma=False)
```

```python
from functools import partial
import math

import jax
import jax.numpy as jnp
from jax import lax
from jax.experimental import pallas as pl
from jax.experimental.pallas import tpu as pltpu
from jax.sharding import PartitionSpec as P

PH = 256
F32 = jnp.float32
BF16 = jnp.bfloat16


def iota(shape, dim):
    return lax.broadcasted_iota(jnp.int32, shape, dim)


def dot(a, b):
    return jnp.dot(a, b, preferred_element_type=F32)


def dot_nt(a, b):
    return lax.dot_general(a, b, (((1,), (1,)), ((), ())), preferred_element_type=F32)


def dot_tn(a, b):
    return lax.dot_general(a, b, (((0,), (0,)), ((), ())), preferred_element_type=F32)


def toeplitz(taps, rows, lanes, shift):
    first = pltpu.roll(jnp.broadcast_to(taps, (8, lanes)), 0, 1, stride=1, stride_axis=0)
    blocks = [pltpu.roll(first, (i + shift) % lanes, 1) for i in range(0, rows, 8)]
    return jnp.concatenate(blocks, axis=0)


def masked_bands(table, rows, lanes, shift, mask):
    padded = jnp.concatenate(
        [table, jnp.zeros((table.shape[0], lanes - table.shape[1]), F32)], axis=1
    )
    for b in range(table.shape[0]):
        yield b, jnp.where(mask, toeplitz(padded[b:b + 1], rows, lanes, shift), 0.0)


def split(x):
    high = x.astype(BF16)
    return high, (x - high.astype(F32)).astype(BF16)


def coadd_kernel(
    geometry,
    col_h, row_h, dest_h, off_h, kind_h, weight_h, coef_h, taps_h, pieces_h,
    dest_s_h, off_s_h,
    kept, sent, across, along,
    col, row, dest_v, off_v, kind_v, weight_v, coef, det_taps, pieces, dest_s, off_s,
    col_bands, row_bands, factors, even, odd, acc, den, sems,
):
    patches, strips, halo, stride, group, chunks, halved = geometry
    count, height, width = pieces.shape
    basis, taps = col.shape
    half = taps // 2
    strip = PH // strips
    span = kept.shape[1]
    sources = (
        col_h, row_h, dest_h, off_h, kind_h, weight_h, coef_h, taps_h, pieces_h, dest_s_h,
        off_s_h,
    )
    targets = (
        col, row, dest_v, off_v, kind_v, weight_v, coef, det_taps, pieces, dest_s, off_s
    )
    copies = [
        pltpu.make_async_copy(source, target, sems.at[k])
        for k, (source, target) in enumerate(zip(sources, targets))
    ]
    for copy in copies:
        copy.start()
    acc[...] = jnp.zeros_like(acc)
    for copy in copies[:2]:
        copy.wait()
    x, y = iota((width, width), 1), iota((width, width), 0)
    near = jnp.abs(x - y) <= half
    for b, band in masked_bands(col[...].astype(F32), width, width, -half, near):
        col_bands[b * width:(b + 1) * width, :] = band.astype(BF16)
    near = near & (x // height == y // height)
    for b, band in masked_bands(row[...].astype(F32), width, width, -half, near):
        row_bands[b * width:(b + 1) * width, :] = band.astype(BF16)
    for copy in copies[2:]:
        copy.wait()
    table, detect = det_taps[...].astype(F32), det_taps.shape[1]
    ((_, band),) = masked_bands(table[1:2], width, width, -halo, jnp.abs(x - y) <= halo)
    across[...] = band.astype(BF16)
    diff = iota((strip, width), 1) - iota((strip, width), 0)
    ((_, band),) = masked_bands(table[0:1], strip, width, 0, (diff >= 0) & (diff < detect))
    along[...] = band.astype(BF16)
    kinds = coef.shape[1]
    weight = weight_v[...].astype(F32)
    picked = jnp.where(iota((kinds, count), 0) == kind_v[...], weight, 0.0).astype(BF16)
    high, low = split(coef[...])
    high, low = split(dot(high, picked) + dot(low, picked))
    spread = (
        iota((basis, basis * width), 1) // width == iota((basis, basis * width), 0)
    ).astype(BF16)
    factors[...] = dot_tn(high, spread) + dot_tn(low, spread)
    share = jnp.where(iota((patches, count), 0) == dest_v[...], weight, 0.0).astype(BF16)
    for v in range(strips):
        at = iota((width, count), 0) + (v * strip - halo) - off_v[...]
        covered = ((at >= 0) & (at < height)).astype(BF16)
        den[v] = dot_nt(share, covered)

    together = 2

    def row_step(base, groups, scaled):
        images = jnp.concatenate(
            [
                pieces[base + g * group:base + (g + 1) * group].reshape(width, width)
                for g in range(groups)
            ],
            axis=1,
        )
        for start in range(0, basis, together):
            stop = min(start + together, basis)
            rowed = dot(row_bands[start * width:stop * width, :], images)
            for b in range(start, stop):
                at = slice(b * width, (b + 1) * width)
                for g in range(groups):
                    for j in range(group):
                        top = (b - start) * width + j * height
                        part = rowed[top:top + height, g * width:(g + 1) * width]
                        n = base + g * group + j
                        part = part * factors[n:n + 1, at]
                        first = g * width + j * height
                        scaled[first:first + height, at] = part.astype(BF16)

    def column_step(base, groups, scaled):
        matched = dot(scaled[:groups * width, :], col_bands[...])
        for j in range(groups * group):
            place = pl.ds(dest_s[base + j] * stride + halo + off_s[base + j], height)
            acc[place, :] = acc[place, :] + matched[j * height:(j + 1) * height]

    base, before = 0, None
    for k, groups in enumerate(chunks):
        now = (base, groups, (even, odd)[k % 2])
        row_step(*now)
        if before:
            column_step(*before)
        base, before = base + groups * group, now
    column_step(*before)
    own = iota((span, width), 0) < strip + 2 * halo
    me = lax.axis_index("patch") * strips + lax.axis_index("visit")
    parts = patches * strips

    def strip_at(position):
        away = 0
        for stage, mask in enumerate(halving_masks(halved)):
            away = away ^ (((position >> (halved + 3 - stage)) & 1) * mask)
        for k in range(2):
            away = away ^ direct_mask(halved, k, (position >> (2 - 2 * k)) & 3)
        device = away ^ me
        p, v = device // strips, lax.rem(device, strips)
        base = pl.multiple_of(p * stride + v * strip, 8)
        return jnp.where(own, acc[pl.ds(base, span), :], den[v, pl.ds(p, 1), :])

    def finish(i, carry):
        sent[i] = strip_at(i + parts // 2).astype(BF16)
        kept[i] = strip_at(i)
        return carry

    if parts <= 32:
        for i in range(parts // 2):
            finish(i, 0)
    else:
        lax.fori_loop(0, parts // 2, finish, 0, unroll=4)


def detect_kernel(halo, *refs):
    *terms, across, along, coadd, detection = refs
    span, width = terms[0].shape
    strip = coadd.shape[0]
    total = terms[0][...]
    for term in terms[1:]:
        total = total + term[...].astype(F32)
    rows = iota((span, width), 0)
    square = jnp.broadcast_to(total[strip + 2 * halo:strip + 2 * halo + 1], (width, width))
    weight = jnp.transpose(square)[:span]
    value = jnp.where(rows < strip + 2 * halo, total / (1.0 + weight), 0.0)
    coadd[...] = value[halo:halo + strip]
    columns, filt = across[...], along[...]
    high, low = split(value)
    smooth = dot(high, columns) + dot(low, columns)
    smooth = jnp.concatenate([smooth, jnp.zeros((width - span, width), F32)], axis=0)
    high, low = split(smooth)
    detection[...] = dot(filt, high) + dot(filt, low)


def halving_masks(halved):
    return [1 << k | 1 for k in range(halved)]


def direct_mask(halved, k, member):
    return (member << (halved + 2 * k)) | ((member | (member >> 1)) & 1)


def exchange(x, mask):
    parts = lax.axis_size("patch") * lax.axis_size("visit")
    return lax.ppermute(x, ("patch", "visit"), [(d, d ^ mask) for d in range(parts)])


def exchange_direct(sums, mask, order):
    return [sums[0]] + [exchange(sums[k].astype(BF16), mask(k)) for k in order]


def shards(
    pieces, dest, offsets, kernel_index, weights, basis_col, basis_row, coef_table, det_taps
):
    patches = lax.axis_size("patch")
    strips = lax.axis_size("visit")
    count, height, width = pieces.shape
    basis = basis_col.shape[0]
    halo = det_taps.shape[1] // 2
    strip = PH // strips
    span = -(-(strip + 2 * halo + 1) // 8) * 8
    stride = strip * (strips - 1) + span
    group = width // height
    chunks, left = [], count // group
    while left:
        chunks.append(min(left, max(2, (left * 5 + 11) // 12)))
        left = left - chunks[-1]
    parts = patches * strips
    vmem = pl.BlockSpec(memory_space=pltpu.VMEM)
    inputs = (
        basis_col, basis_row, dest.reshape(1, count), offsets.reshape(1, count),
        kernel_index.reshape(1, count), weights.reshape(1, count), coef_table.T, det_taps, pieces,
        dest[:, 0], offsets,
    )
    bits = parts.bit_length() - 1
    halved = bits - 4
    shape = (parts // 2, span, width)
    shapes = [jax.ShapeDtypeStruct(shape, F32), jax.ShapeDtypeStruct(shape, BF16)]
    shapes += [jax.ShapeDtypeStruct((rows, width), BF16) for rows in (width, strip)]
    grant = 24 * 1024 * 1024 + 3 * parts * span * width + 4 * patches * stride * width
    kept, sent, across, along = pl.pallas_call(
        partial(coadd_kernel, (patches, strips, halo, stride, group, chunks, halved)),
        out_shape=shapes,
        in_specs=[pl.BlockSpec(memory_space=pltpu.HBM)] * len(inputs),
        out_specs=[vmem] * 4,
        scratch_shapes=[pltpu.VMEM(x.shape, x.dtype) for x in inputs[:-2]]
        + [pltpu.SMEM(x.shape, x.dtype) for x in inputs[-2:]]
        + [
            pltpu.VMEM((basis * width, width), BF16),
            pltpu.VMEM((basis * width, width), BF16),
            pltpu.VMEM((count, basis * width), F32),
            pltpu.VMEM((max(chunks[0::2]) * width, basis * width), BF16),
            pltpu.VMEM((max(chunks[1::2]) * width, basis * width), BF16),
            pltpu.VMEM((patches * stride, width), F32),
            pltpu.VMEM((strips, patches, width), F32),
            pltpu.SemaphoreType.DMA((len(inputs),)),
        ],
        compiler_params=pltpu.CompilerParams(vmem_limit_bytes=grant),
        name="coadd_partials",
    )(*[pltpu.with_memory_space_constraint(x, pltpu.HBM) for x in inputs])
    def exchange(x, mask):
        return lax.ppermute(x, ("patch", "visit"), [(d, d ^ mask) for d in range(parts)])

    for stage, mask in enumerate(halving_masks(halved)):
        if stage:
            left = kept.shape[0] // 2
            sent = (kept[left:] + given[left:].astype(F32)).astype(BF16)
            kept = kept[:left] + given[:left].astype(F32)
        given = exchange(sent, mask)
    sums = [kept[4 * k:4 * k + 4] + given[4 * k:4 * k + 4].astype(F32) for k in range(4)]
    terms = exchange_direct(sums, partial(direct_mask, halved, 0), (1, 3, 2))
    total = terms[0]
    for term in terms[1:]:
        total = total + term.astype(F32)
    total = [total[k] for k in range(4)]
    terms = exchange_direct(total, partial(direct_mask, halved, 1), (2, 3, 1))
    shape = jax.ShapeDtypeStruct((strip, width), F32)
    return pl.pallas_call(
        partial(detect_kernel, halo),
        out_shape=(shape, shape),
        in_specs=[vmem] * (len(terms) + 2),
        out_specs=(vmem, vmem),
        compiler_params=pltpu.CompilerParams(vmem_limit_bytes=48 * 1024 * 1024),
        name="detect_strip",
    )(*terms, across, along)


def solution(mesh):
    in_specs = (
        P(("patch", "visit"), None, None),
        P(("patch", "visit"), None),
        P(("patch", "visit")),
        P(("patch", "visit")),
        P(("patch", "visit")),
        P(),
        P(),
        P(),
        P(),
    )
    out_specs = (P(("patch", "visit"), None), P(("patch", "visit"), None))
    return jax.shard_map(shards, mesh=mesh, in_specs=in_specs, out_specs=out_specs, check_vma=False)
```

```python
from functools import partial
import math

import jax
import jax.numpy as jnp
from jax import lax
from jax.experimental import pallas as pl
from jax.experimental.pallas import tpu as pltpu
from jax.sharding import PartitionSpec as P

PH = 256
F32 = jnp.float32
BF16 = jnp.bfloat16


def iota(shape, dim):
    return lax.broadcasted_iota(jnp.int32, shape, dim)


def dot(a, b):
    return jnp.dot(a, b, preferred_element_type=F32)


def dot_nt(a, b):
    return lax.dot_general(a, b, (((1,), (1,)), ((), ())), preferred_element_type=F32)


def dot_tn(a, b):
    return lax.dot_general(a, b, (((0,), (0,)), ((), ())), preferred_element_type=F32)


def toeplitz(taps, rows, lanes, shift):
    first = pltpu.roll(jnp.broadcast_to(taps, (8, lanes)), 0, 1, stride=1, stride_axis=0)
    blocks = [pltpu.roll(first, (i + shift) % lanes, 1) for i in range(0, rows, 8)]
    return jnp.concatenate(blocks, axis=0)


def masked_bands(table, rows, lanes, shift, mask):
    padded = jnp.concatenate(
        [table, jnp.zeros((table.shape[0], lanes - table.shape[1]), F32)], axis=1
    )
    for b in range(table.shape[0]):
        yield b, jnp.where(mask, toeplitz(padded[b:b + 1], rows, lanes, shift), 0.0)


def split(x):
    high = x.astype(BF16)
    return high, (x - high.astype(F32)).astype(BF16)


def coadd_kernel(
    geometry,
    col_h, row_h, dest_h, off_h, kind_h, weight_h, coef_h, taps_h, pieces_h,
    dest_s_h, off_s_h,
    kept, sent, across, along,
    col, row, dest_v, off_v, kind_v, weight_v, coef, det_taps, pieces, dest_s, off_s,
    col_bands, row_bands, factors, even, odd, acc, den, sems,
):
    patches, strips, halo, stride, group, chunks, halved = geometry
    count, height, width = pieces.shape
    basis, taps = col.shape
    half = taps // 2
    strip = PH // strips
    span = kept.shape[1]
    sources = (
        col_h, row_h, dest_h, off_h, kind_h, weight_h, coef_h, taps_h, pieces_h, dest_s_h,
        off_s_h,
    )
    targets = (
        col, row, dest_v, off_v, kind_v, weight_v, coef, det_taps, pieces, dest_s, off_s
    )
    copies = [
        pltpu.make_async_copy(source, target, sems.at[k])
        for k, (source, target) in enumerate(zip(sources, targets))
    ]
    for copy in copies:
        copy.start()
    acc[...] = jnp.zeros_like(acc)
    for copy in copies[:2]:
        copy.wait()
    x, y = iota((width, width), 1), iota((width, width), 0)
    near = jnp.abs(x - y) <= half
    for b, band in masked_bands(col[...].astype(F32), width, width, -half, near):
        col_bands[b * width:(b + 1) * width, :] = band.astype(BF16)
    near = near & (x // height == y // height)
    for b, band in masked_bands(row[...].astype(F32), width, width, -half, near):
        row_bands[b * width:(b + 1) * width, :] = band.astype(BF16)
    for copy in copies[2:]:
        copy.wait()
    table, detect = det_taps[...].astype(F32), det_taps.shape[1]
    ((_, band),) = masked_bands(table[1:2], width, width, -halo, jnp.abs(x - y) <= halo)
    across[...] = band.astype(BF16)
    diff = iota((strip, width), 1) - iota((strip, width), 0)
    ((_, band),) = masked_bands(table[0:1], strip, width, 0, (diff >= 0) & (diff < detect))
    along[...] = band.astype(BF16)
    kinds = coef.shape[1]
    weight = weight_v[...].astype(F32)
    picked = jnp.where(iota((kinds, count), 0) == kind_v[...], weight, 0.0).astype(BF16)
    high, low = split(coef[...])
    high, low = split(dot(high, picked) + dot(low, picked))
    spread = (
        iota((basis, basis * width), 1) // width == iota((basis, basis * width), 0)
    ).astype(BF16)
    factors[...] = dot_tn(high, spread) + dot_tn(low, spread)
    share = jnp.where(iota((patches, count), 0) == dest_v[...], weight, 0.0).astype(BF16)
    for v in range(strips):
        at = iota((width, count), 0) + (v * strip - halo) - off_v[...]
        covered = ((at >= 0) & (at < height)).astype(BF16)
        den[v] = dot_nt(share, covered)

    together = 2

    def row_step(base, groups, scaled):
        images = jnp.concatenate(
            [
                pieces[base + g * group:base + (g + 1) * group].reshape(width, width)
                for g in range(groups)
            ],
            axis=1,
        )
        for start in range(0, basis, together):
            stop = min(start + together, basis)
            rowed = dot(row_bands[start * width:stop * width, :], images)
            for b in range(start, stop):
                at = slice(b * width, (b + 1) * width)
                for g in range(groups):
                    for j in range(group):
                        top = (b - start) * width + j * height
                        part = rowed[top:top + height, g * width:(g + 1) * width]
                        n = base + g * group + j
                        part = part * factors[n:n + 1, at]
                        first = g * width + j * height
                        scaled[first:first + height, at] = part.astype(BF16)

    def column_step(base, groups, scaled):
        matched = dot(scaled[:groups * width, :], col_bands[...])
        for j in range(groups * group):
            place = pl.ds(dest_s[base + j] * stride + halo + off_s[base + j], height)
            acc[place, :] = acc[place, :] + matched[j * height:(j + 1) * height]

    base, before = 0, None
    for k, groups in enumerate(chunks):
        now = (base, groups, (even, odd)[k % 2])
        row_step(*now)
        if before:
            column_step(*before)
        base, before = base + groups * group, now
    column_step(*before)
    own = iota((span, width), 0) < strip + 2 * halo
    me = lax.axis_index("patch") * strips + lax.axis_index("visit")
    parts = patches * strips

    def strip_at(position):
        away = 0
        for stage, mask in enumerate(halving_masks(halved)):
            away = away ^ (((position >> (halved + 3 - stage)) & 1) * mask)
        for k in range(2):
            away = away ^ direct_mask(halved, k, (position >> (2 - 2 * k)) & 3)
        device = away ^ me
        p, v = device // strips, lax.rem(device, strips)
        base = pl.multiple_of(p * stride + v * strip, 8)
        return jnp.where(own, acc[pl.ds(base, span), :], den[v, pl.ds(p, 1), :])

    def finish(i, carry):
        sent[i] = strip_at(i + parts // 2).astype(BF16)
        kept[i] = strip_at(i)
        return carry

    if parts <= 32:
        for i in range(parts // 2):
            finish(i, 0)
    else:
        lax.fori_loop(0, parts // 2, finish, 0, unroll=4)


def detect_kernel(halo, *refs):
    *terms, across, along, coadd, detection = refs
    span, width = terms[0].shape
    strip = coadd.shape[0]
    total = terms[0][...]
    for term in terms[1:]:
        total = total + term[...].astype(F32)
    rows = iota((span, width), 0)
    square = jnp.broadcast_to(total[strip + 2 * halo:strip + 2 * halo + 1], (width, width))
    weight = jnp.transpose(square)[:span]
    value = jnp.where(rows < strip + 2 * halo, total / (1.0 + weight), 0.0)
    coadd[...] = value[halo:halo + strip]
    columns, filt = across[...], along[...]
    high, low = split(value)
    smooth = dot(high, columns) + dot(low, columns)
    smooth = jnp.concatenate([smooth, jnp.zeros((width - span, width), F32)], axis=0)
    high, low = split(smooth)
    detection[...] = dot(filt, high) + dot(filt, low)


def halving_masks(halved):
    return [1 << k | 1 for k in range(halved)]


def direct_mask(halved, k, member):
    return (member << (halved + 2 * k)) | ((member | (member >> 1)) & 1)


def exchange(x, mask):
    parts = lax.axis_size("patch") * lax.axis_size("visit")
    return lax.ppermute(x, ("patch", "visit"), [(d, d ^ mask) for d in range(parts)])


def exchange_direct(sums, mask, order):
    return [sums[0]] + [exchange(sums[k].astype(BF16), mask(k)) for k in order]


def shards(
    pieces, dest, offsets, kernel_index, weights, basis_col, basis_row, coef_table, det_taps
):
    patches = lax.axis_size("patch")
    strips = lax.axis_size("visit")
    count, height, width = pieces.shape
    basis = basis_col.shape[0]
    halo = det_taps.shape[1] // 2
    strip = PH // strips
    span = -(-(strip + 2 * halo + 1) // 8) * 8
    stride = strip * (strips - 1) + span
    group = width // height
    chunks, left = [], count // group
    while left:
        chunks.append(min(left, max(2, (left * 5 + 11) // 12)))
        left = left - chunks[-1]
    parts = patches * strips
    vmem = pl.BlockSpec(memory_space=pltpu.VMEM)
    inputs = (
        basis_col, basis_row, dest.reshape(1, count), offsets.reshape(1, count),
        kernel_index.reshape(1, count), weights.reshape(1, count), coef_table.T, det_taps, pieces,
        dest[:, 0], offsets,
    )
    bits = parts.bit_length() - 1
    halved = bits - 4
    shape = (parts // 2, span, width)
    shapes = [jax.ShapeDtypeStruct(shape, F32), jax.ShapeDtypeStruct(shape, BF16)]
    shapes += [jax.ShapeDtypeStruct((rows, width), BF16) for rows in (width, strip)]
    grant = 24 * 1024 * 1024 + 3 * parts * span * width + 4 * patches * stride * width
    kept, sent, across, along = pl.pallas_call(
        partial(coadd_kernel, (patches, strips, halo, stride, group, chunks, halved)),
        out_shape=shapes,
        in_specs=[pl.BlockSpec(memory_space=pltpu.HBM)] * len(inputs),
        out_specs=[vmem] * 4,
        scratch_shapes=[pltpu.VMEM(x.shape, x.dtype) for x in inputs[:-2]]
        + [pltpu.SMEM(x.shape, x.dtype) for x in inputs[-2:]]
        + [
            pltpu.VMEM((basis * width, width), BF16),
            pltpu.VMEM((basis * width, width), BF16),
            pltpu.VMEM((count, basis * width), F32),
            pltpu.VMEM((max(chunks[0::2]) * width, basis * width), BF16),
            pltpu.VMEM((max(chunks[1::2]) * width, basis * width), BF16),
            pltpu.VMEM((patches * stride, width), F32),
            pltpu.VMEM((strips, patches, width), F32),
            pltpu.SemaphoreType.DMA((len(inputs),)),
        ],
        compiler_params=pltpu.CompilerParams(vmem_limit_bytes=grant),
        name="coadd_partials",
    )(*[pltpu.with_memory_space_constraint(x, pltpu.HBM) for x in inputs])
    def exchange(x, mask):
        return lax.ppermute(x, ("patch", "visit"), [(d, d ^ mask) for d in range(parts)])

    for stage, mask in enumerate(halving_masks(halved)):
        if stage:
            left = kept.shape[0] // 2
            sent = (kept[left:] + given[left:].astype(F32)).astype(BF16)
            kept = kept[:left] + given[:left].astype(F32)
        given = exchange(sent, mask)
    sums = [kept[4 * k:4 * k + 4] + given[4 * k:4 * k + 4].astype(F32) for k in range(4)]
    terms = exchange_direct(sums, partial(direct_mask, halved, 0), (3, 1, 2))
    total = terms[0]
    for term in terms[1:]:
        total = total + term.astype(F32)
    total = [total[k] for k in range(4)]
    terms = exchange_direct(total, partial(direct_mask, halved, 1), (3, 2, 1))
    shape = jax.ShapeDtypeStruct((strip, width), F32)
    return pl.pallas_call(
        partial(detect_kernel, halo),
        out_shape=(shape, shape),
        in_specs=[vmem] * (len(terms) + 2),
        out_specs=(vmem, vmem),
        compiler_params=pltpu.CompilerParams(vmem_limit_bytes=48 * 1024 * 1024),
        name="detect_strip",
    )(*terms, across, along)


def solution(mesh):
    in_specs = (
        P(("patch", "visit"), None, None),
        P(("patch", "visit"), None),
        P(("patch", "visit")),
        P(("patch", "visit")),
        P(("patch", "visit")),
        P(),
        P(),
        P(),
        P(),
    )
    out_specs = (P(("patch", "visit"), None), P(("patch", "visit"), None))
    return jax.shard_map(shards, mesh=mesh, in_specs=in_specs, out_specs=out_specs, check_vma=False)
```

```python
from functools import partial
import math

import jax
import jax.numpy as jnp
from jax import lax
from jax.experimental import pallas as pl
from jax.experimental.pallas import tpu as pltpu
from jax.sharding import PartitionSpec as P

PH = 256
F32 = jnp.float32
BF16 = jnp.bfloat16


def iota(shape, dim):
    return lax.broadcasted_iota(jnp.int32, shape, dim)


def dot(a, b):
    return jnp.dot(a, b, preferred_element_type=F32)


def dot_nt(a, b):
    return lax.dot_general(a, b, (((1,), (1,)), ((), ())), preferred_element_type=F32)


def dot_tn(a, b):
    return lax.dot_general(a, b, (((0,), (0,)), ((), ())), preferred_element_type=F32)


def toeplitz(taps, rows, lanes, shift):
    first = pltpu.roll(jnp.broadcast_to(taps, (8, lanes)), 0, 1, stride=1, stride_axis=0)
    blocks = [pltpu.roll(first, (i + shift) % lanes, 1) for i in range(0, rows, 8)]
    return jnp.concatenate(blocks, axis=0)


def masked_bands(table, rows, lanes, shift, mask):
    padded = jnp.concatenate(
        [table, jnp.zeros((table.shape[0], lanes - table.shape[1]), F32)], axis=1
    )
    for b in range(table.shape[0]):
        yield b, jnp.where(mask, toeplitz(padded[b:b + 1], rows, lanes, shift), 0.0)


def split(x):
    high = x.astype(BF16)
    return high, (x - high.astype(F32)).astype(BF16)


def coadd_kernel(
    geometry,
    col_h, row_h, dest_h, off_h, kind_h, weight_h, coef_h, taps_h, pieces_h,
    dest_s_h, off_s_h,
    kept, sent, across, along,
    col, row, dest_v, off_v, kind_v, weight_v, coef, det_taps, pieces, dest_s, off_s,
    col_bands, row_bands, factors, even, odd, acc, den, sems,
):
    patches, strips, halo, stride, group, chunks, halved = geometry
    count, height, width = pieces.shape
    basis, taps = col.shape
    half = taps // 2
    strip = PH // strips
    span = kept.shape[1]
    sources = (
        col_h, row_h, dest_h, off_h, kind_h, weight_h, coef_h, taps_h, pieces_h, dest_s_h,
        off_s_h,
    )
    targets = (
        col, row, dest_v, off_v, kind_v, weight_v, coef, det_taps, pieces, dest_s, off_s
    )
    copies = [
        pltpu.make_async_copy(source, target, sems.at[k])
        for k, (source, target) in enumerate(zip(sources, targets))
    ]
    for copy in copies:
        copy.start()
    acc[...] = jnp.zeros_like(acc)
    for copy in copies[:2]:
        copy.wait()
    x, y = iota((width, width), 1), iota((width, width), 0)
    near = jnp.abs(x - y) <= half
    for b, band in masked_bands(col[...].astype(F32), width, width, -half, near):
        col_bands[b * width:(b + 1) * width, :] = band.astype(BF16)
    near = near & (x // height == y // height)
    for b, band in masked_bands(row[...].astype(F32), width, width, -half, near):
        row_bands[b * width:(b + 1) * width, :] = band.astype(BF16)
    for copy in copies[2:]:
        copy.wait()
    table, detect = det_taps[...].astype(F32), det_taps.shape[1]
    ((_, band),) = masked_bands(table[1:2], width, width, -halo, jnp.abs(x - y) <= halo)
    across[...] = band.astype(BF16)
    diff = iota((strip, width), 1) - iota((strip, width), 0)
    ((_, band),) = masked_bands(table[0:1], strip, width, 0, (diff >= 0) & (diff < detect))
    along[...] = band.astype(BF16)
    kinds = coef.shape[1]
    weight = weight_v[...].astype(F32)
    picked = jnp.where(iota((kinds, count), 0) == kind_v[...], weight, 0.0).astype(BF16)
    high, low = split(coef[...])
    high, low = split(dot(high, picked) + dot(low, picked))
    spread = (
        iota((basis, basis * width), 1) // width == iota((basis, basis * width), 0)
    ).astype(BF16)
    factors[...] = dot_tn(high, spread) + dot_tn(low, spread)
    share = jnp.where(iota((patches, count), 0) == dest_v[...], weight, 0.0).astype(BF16)
    for v in range(strips):
        at = iota((width, count), 0) + (v * strip - halo) - off_v[...]
        covered = ((at >= 0) & (at < height)).astype(BF16)
        den[v] = dot_nt(share, covered)

    together = 2

    def row_step(base, groups, scaled):
        images = jnp.concatenate(
            [
                pieces[base + g * group:base + (g + 1) * group].reshape(width, width)
                for g in range(groups)
            ],
            axis=1,
        )
        for start in range(0, basis, together):
            stop = min(start + together, basis)
            rowed = dot(row_bands[start * width:stop * width, :], images)
            for b in range(start, stop):
                at = slice(b * width, (b + 1) * width)
                for g in range(groups):
                    for j in range(group):
                        top = (b - start) * width + j * height
                        part = rowed[top:top + height, g * width:(g + 1) * width]
                        n = base + g * group + j
                        part = part * factors[n:n + 1, at]
                        first = g * width + j * height
                        scaled[first:first + height, at] = part.astype(BF16)

    def column_step(base, groups, scaled):
        matched = dot(scaled[:groups * width, :], col_bands[...])
        for j in range(groups * group):
            place = pl.ds(dest_s[base + j] * stride + halo + off_s[base + j], height)
            acc[place, :] = acc[place, :] + matched[j * height:(j + 1) * height]

    base, before = 0, None
    for k, groups in enumerate(chunks):
        now = (base, groups, (even, odd)[k % 2])
        row_step(*now)
        if before:
            column_step(*before)
        base, before = base + groups * group, now
    column_step(*before)
    own = iota((span, width), 0) < strip + 2 * halo
    me = lax.axis_index("patch") * strips + lax.axis_index("visit")
    parts = patches * strips

    def strip_at(position):
        away = 0
        for stage, mask in enumerate(halving_masks(halved)):
            away = away ^ (((position >> (halved + 3 - stage)) & 1) * mask)
        for k in range(2):
            away = away ^ direct_mask(halved, k, (position >> (2 - 2 * k)) & 3)
        device = away ^ me
        p, v = device // strips, lax.rem(device, strips)
        base = pl.multiple_of(p * stride + v * strip, 8)
        return jnp.where(own, acc[pl.ds(base, span), :], den[v, pl.ds(p, 1), :])

    def finish(i, carry):
        sent[i] = strip_at(i + parts // 2).astype(BF16)
        kept[i] = strip_at(i)
        return carry

    if parts <= 32:
        for i in range(parts // 2):
            finish(i, 0)
    else:
        lax.fori_loop(0, parts // 2, finish, 0, unroll=4)


def detect_kernel(halo, *refs):
    *terms, across, along, coadd, detection = refs
    span, width = terms[0].shape
    strip = coadd.shape[0]
    total = terms[0][...]
    for term in terms[1:]:
        total = total + term[...].astype(F32)
    rows = iota((span, width), 0)
    square = jnp.broadcast_to(total[strip + 2 * halo:strip + 2 * halo + 1], (width, width))
    weight = jnp.transpose(square)[:span]
    value = jnp.where(rows < strip + 2 * halo, total / (1.0 + weight), 0.0)
    coadd[...] = value[halo:halo + strip]
    columns, filt = across[...], along[...]
    high, low = split(value)
    smooth = dot(high, columns) + dot(low, columns)
    smooth = jnp.concatenate([smooth, jnp.zeros((width - span, width), F32)], axis=0)
    high, low = split(smooth)
    detection[...] = dot(filt, high) + dot(filt, low)


def halving_masks(halved):
    return [1 << k | 1 for k in range(halved)]


def direct_mask(halved, k, member):
    return (member << (halved + 2 * k)) | ((member | (member >> 1)) & 1)


def exchange(x, mask):
    parts = lax.axis_size("patch") * lax.axis_size("visit")
    return lax.ppermute(x, ("patch", "visit"), [(d, d ^ mask) for d in range(parts)])


def exchange_direct(sums, mask, order):
    return [sums[0]] + [exchange(sums[k].astype(BF16), mask(k)) for k in order]


def shards(
    pieces, dest, offsets, kernel_index, weights, basis_col, basis_row, coef_table, det_taps
):
    patches = lax.axis_size("patch")
    strips = lax.axis_size("visit")
    count, height, width = pieces.shape
    basis = basis_col.shape[0]
    halo = det_taps.shape[1] // 2
    strip = PH // strips
    span = -(-(strip + 2 * halo + 1) // 8) * 8
    stride = strip * (strips - 1) + span
    group = width // height
    chunks, left = [], count // group
    while left:
        chunks.append(min(left, max(2, (left * 5 + 11) // 12)))
        left = left - chunks[-1]
    parts = patches * strips
    vmem = pl.BlockSpec(memory_space=pltpu.VMEM)
    inputs = (
        basis_col, basis_row, dest.reshape(1, count), offsets.reshape(1, count),
        kernel_index.reshape(1, count), weights.reshape(1, count), coef_table.T, det_taps, pieces,
        dest[:, 0], offsets,
    )
    bits = parts.bit_length() - 1
    halved = bits - 4
    shape = (parts // 2, span, width)
    shapes = [jax.ShapeDtypeStruct(shape, F32), jax.ShapeDtypeStruct(shape, BF16)]
    shapes += [jax.ShapeDtypeStruct((rows, width), BF16) for rows in (width, strip)]
    grant = 24 * 1024 * 1024 + 3 * parts * span * width + 4 * patches * stride * width
    kept, sent, across, along = pl.pallas_call(
        partial(coadd_kernel, (patches, strips, halo, stride, group, chunks, halved)),
        out_shape=shapes,
        in_specs=[pl.BlockSpec(memory_space=pltpu.HBM)] * len(inputs),
        out_specs=[vmem] * 4,
        scratch_shapes=[pltpu.VMEM(x.shape, x.dtype) for x in inputs[:-2]]
        + [pltpu.SMEM(x.shape, x.dtype) for x in inputs[-2:]]
        + [
            pltpu.VMEM((basis * width, width), BF16),
            pltpu.VMEM((basis * width, width), BF16),
            pltpu.VMEM((count, basis * width), F32),
            pltpu.VMEM((max(chunks[0::2]) * width, basis * width), BF16),
            pltpu.VMEM((max(chunks[1::2]) * width, basis * width), BF16),
            pltpu.VMEM((patches * stride, width), F32),
            pltpu.VMEM((strips, patches, width), F32),
            pltpu.SemaphoreType.DMA((len(inputs),)),
        ],
        compiler_params=pltpu.CompilerParams(vmem_limit_bytes=grant),
        name="coadd_partials",
    )(*[pltpu.with_memory_space_constraint(x, pltpu.HBM) for x in inputs])
    def exchange(x, mask):
        return lax.ppermute(x, ("patch", "visit"), [(d, d ^ mask) for d in range(parts)])

    for stage, mask in enumerate(halving_masks(halved)):
        if stage:
            left = kept.shape[0] // 2
            sent = (kept[left:] + given[left:].astype(F32)).astype(BF16)
            kept = kept[:left] + given[:left].astype(F32)
        given = exchange(sent, mask)
    sums = [kept[4 * k:4 * k + 4] + given[4 * k:4 * k + 4].astype(F32) for k in range(4)]
    terms = exchange_direct(sums, partial(direct_mask, halved, 0), (3, 1, 2))
    total = terms[0]
    for term in terms[1:]:
        total = total + term.astype(F32)
    total = [total[k] for k in range(4)]
    terms = exchange_direct(total, partial(direct_mask, halved, 1), (1, 2, 3))
    shape = jax.ShapeDtypeStruct((strip, width), F32)
    return pl.pallas_call(
        partial(detect_kernel, halo),
        out_shape=(shape, shape),
        in_specs=[vmem] * (len(terms) + 2),
        out_specs=(vmem, vmem),
        compiler_params=pltpu.CompilerParams(vmem_limit_bytes=48 * 1024 * 1024),
        name="detect_strip",
    )(*terms, across, along)


def solution(mesh):
    in_specs = (
        P(("patch", "visit"), None, None),
        P(("patch", "visit"), None),
        P(("patch", "visit")),
        P(("patch", "visit")),
        P(("patch", "visit")),
        P(),
        P(),
        P(),
        P(),
    )
    out_specs = (P(("patch", "visit"), None), P(("patch", "visit"), None))
    return jax.shard_map(shards, mesh=mesh, in_specs=in_specs, out_specs=out_specs, check_vma=False)
```
